512 devices in a mesh: fft: 32 (over x, z), slab: 16 (over y, core).
Axes of the slice: x: 4, y: 8, z: 8, core: 2. Of those that a mesh axis runs over, the one named last changes fastest.
Arguments:
- ml_pos: float32 [3, 16384], replicated, may hold values from 0 to 58
- ml_width: float32 [16384], replicated, may hold values from 0.7 to 1.6
- ml_drive: float32 [16384], P(('fft', 'slab')), may hold values from -8 to 8
- ml_hard: float32 [16384], P(('fft', 'slab')), may hold values from 4 to 12
- mm_charge: float32 [3145728], P(('fft', 'slab')), may hold values from -3 to 3
- mm_frac: float32 [3, 3145728], P(None, ('fft', 'slab')), may hold values from 0 to 1
- mm_cell: int32 [3, 3145728], P(None, ('fft', 'slab')), may hold values from 0 to 383, as said below
- slot_atom: int32 [16384], P(('fft', 'slab')), may hold values from 0 to 16383, each once
- slot_frac: float32 [3, 16384], P(None, ('fft', 'slab')), may hold values from 0 to 1
- slot_cell: int32 [3, 16384], P(None, ('fft', 'slab')), may hold values from 0 to 383, as said below
Outputs:
- ml_charge: float32 [16384], P(('fft', 'slab'))
- struct_re: float32 [384, 192, 384], P('fft', 'slab')
- struct_im: float32 [384, 192, 384], P('fft', 'slab')
The draws below stay inside these ranges and needn't reach their ends.
Inputs may be any that keep to these rules, and one draw needn't show every extreme that they name: `mm_cell`: row 0 is a grid point along the first dimension (0 to 383), row 1 a point of the owner's 24 along the second, row 2 of the owner's 12 along the third. `slot_cell`: as for mm_cell. `slot_atom`: every ML atom is held by exactly one slot.
All inputs are finite; a program needn't handle non-finite values.
Results may differ from the reference program's by a relative error of at most 0.0003.
Values sent between devices are 32-bit elements; how exact they have to be, the bound alone decides.
No kernel may reach another device: no remote copies, remote signals or barrier semaphores. Data moves between devices by JAX's collectives and lax.ppermute only.
A program may use at most 128 MiB of HBM per device.

```python
import math
import jax
import jax.numpy as jnp
from jax import lax

NG = 384
ITERS = 3
ML_ROWS = 512
M_DEV = 6144
ML_ATOMS = 16384
ML_OWN = 32
MM_ATOMS = 3145728
YL = 24
ZL = 12
KH = 192
N_FFT = 32
N_SLAB = 16


def grid_cells(key, count):
    key_x, key_y, key_z = jax.random.split(key, 3)
    first = jax.random.randint(key_x, (count,), 0, NG)
    second = jax.random.randint(key_y, (count,), 0, YL)
    third = jax.random.randint(key_z, (count,), 0, ZL)
    return jnp.stack([first, second, third]).astype(jnp.int32)


def draw_mm_cell(key, part):
    key = jax.random.fold_in(key, 11)
    return grid_cells(key, MM_ATOMS)


def draw_slot_cell(key, part):
    key = jax.random.fold_in(key, 12)
    return grid_cells(key, ML_ATOMS)


def block_scale(own_key, extent, pieces, least, largest):
    def one(position, shards_of):
        draws = jax.random.uniform(jax.random.fold_in(jax.random.fold_in(own_key, 6), position), (shards_of,), jnp.float32, least / len(pieces), largest / len(pieces))
        return jnp.repeat(jnp.exp(draws), extent[position] // shards_of).reshape((-1,) + (1,) * (len(extent) - position - 1))

    level = one(*pieces[0])
    for cut in pieces[1:]:
        level = level * one(*cut)
    return level


def bell_draw(rng, dims, width, bound, cuts=(), kind=jnp.bfloat16):
    drawn = jax.random.normal(rng, dims, jnp.float32) * width
    if len(cuts) > 0:
        drawn = block_scale(rng, dims, cuts, -0.22, 0.18) * drawn
    return jnp.clip(drawn, min=-bound, max=bound).astype(kind)


def setup_inputs(seed: int = 0) -> dict:
    seeds = jax.random.split(jax.random.key(seed), 11)
    ml_pos = jnp.clip(jax.random.uniform(seeds[0], (3, ML_ATOMS), jnp.float32, 0.0, 58.0), 0.0, 58.0)
    ml_width = jnp.clip(jnp.exp(jax.random.uniform(seeds[1], (ML_ATOMS,), jnp.float32, math.log(0.7), math.log(1.6))), 0.7, 1.6)
    ml_drive = bell_draw(seeds[2], (ML_ATOMS,), 2.0, 8.0, ((0, 512),), jnp.float32)
    ml_hard = jnp.clip(jnp.exp(math.log(12.0) - 1.0986123 * jax.random.uniform(seeds[3], (ML_ATOMS,), jnp.float32) ** block_scale(seeds[3], (ML_ATOMS,), ((0, 512),), -0.2, 0.2)), 4.0, 12.0)
    mm_charge = bell_draw(seeds[4], (MM_ATOMS,), 0.6, 3.0, ((0, 512),), jnp.float32)
    mm_frac = jnp.clip(1.0 * jax.random.uniform(seeds[5], (3, MM_ATOMS), jnp.float32) ** block_scale(seeds[5], (3, MM_ATOMS), ((1, 512),), -0.2, 0.2), 0.0, 1.0)
    mm_cell = draw_mm_cell(jax.random.fold_in(seeds[10], 71), 0)
    slot_atom = jax.random.permutation(seeds[7], ML_ATOMS).astype(jnp.int32)
    slot_frac = jnp.clip(1.0 * jax.random.uniform(seeds[8], (3, ML_ATOMS), jnp.float32) ** block_scale(seeds[8], (3, ML_ATOMS), ((1, 512),), -0.2, 0.2), 0.0, 1.0)
    slot_cell = draw_slot_cell(jax.random.fold_in(seeds[10], 71), 0)
    return {"ml_pos": ml_pos, "ml_width": ml_width, "ml_drive": ml_drive, "ml_hard": ml_hard, "mm_charge": mm_charge, "mm_frac": mm_frac, "mm_cell": mm_cell, "slot_atom": slot_atom, "slot_frac": slot_frac, "slot_cell": slot_cell}


KE = 14.4
ALPHA = 0.08
SOFT = 0.01
SQPI = math.sqrt(math.pi)

def couplings(row_pos, row_width, col_pos, col_width, row_first, col_first):
    dist_sq = (row_pos[0][:, None] - col_pos[0][None, :]) ** 2
    dist_sq = dist_sq + (row_pos[1][:, None] - col_pos[1][None, :]) ** 2
    dist_sq = dist_sq + (row_pos[2][:, None] - col_pos[2][None, :]) ** 2
    distance = jnp.sqrt(dist_sq + SOFT)
    pair_len = jnp.sqrt(2.0 * (row_width[:, None] ** 2 + col_width[None, :] ** 2))
    kernel = KE * (lax.erf(distance / pair_len) - lax.erf(ALPHA * distance)) / distance
    row_ids = row_first + jnp.arange(row_pos.shape[1], dtype=jnp.int32)
    col_ids = col_first + jnp.arange(col_pos.shape[1], dtype=jnp.int32)
    return jnp.where(row_ids[:, None] == col_ids[None, :], 0.0, kernel)

def spline(fraction):
    cubed = fraction ** 3
    squared = fraction ** 2
    return jnp.stack([(1.0 - fraction) ** 3 / 6.0, (3.0 * cubed - 6.0 * squared + 4.0) / 6.0, (-3.0 * cubed + 3.0 * squared + 3.0 * fraction + 1.0) / 6.0, cubed / 6.0])

def apply_operator(ml_pos, ml_width, diagonal, vector):
    block_pos = ml_pos.reshape(3, N_FFT, ML_ROWS).transpose(1, 0, 2)
    block_width = ml_width.reshape(N_FFT, ML_ROWS)

    def one_block(inputs):
        block_id, these_pos, these_width = inputs
        coupling = couplings(these_pos, these_width, ml_pos, ml_width, block_id * ML_ROWS, jnp.int32(0))
        return jnp.dot(coupling, vector, preferred_element_type=jnp.float32, precision=lax.Precision.HIGHEST)
    summed = lax.map(one_block, (jnp.arange(N_FFT, dtype=jnp.int32), block_pos, block_width)).reshape(-1)
    return summed + diagonal * vector

def base_points(grid_cell, per_device):
    owner = jnp.arange(grid_cell.shape[1], dtype=jnp.int32) // per_device
    base_y = owner % N_SLAB * YL + grid_cell[1]
    base_z = owner // N_SLAB * ZL + grid_cell[2]
    return (grid_cell[0], base_y, base_z)

def reference(ml_pos, ml_width, ml_drive, ml_hard, mm_charge, mm_frac, mm_cell, slot_atom, slot_frac, slot_cell):
    diagonal = ml_hard + KE * (1.0 / (ml_width * SQPI) - 2.0 * ALPHA / SQPI)
    charge = jnp.zeros_like(ml_drive)
    residue = -ml_drive
    direction = residue
    norm_now = jnp.sum(residue * residue)
    for iteration in range(ITERS):
        applied = apply_operator(ml_pos, ml_width, diagonal, direction)
        step_len = norm_now / jnp.sum(direction * applied)
        charge = charge + step_len * direction
        residue = residue - step_len * applied
        norm_next = jnp.sum(residue * residue)
        direction = residue + norm_next / norm_now * direction
        norm_now = norm_next
    site_charge = jnp.concatenate([mm_charge, charge[slot_atom]])
    mm_x, mm_y, mm_z = base_points(mm_cell, M_DEV)
    sl_x, sl_y, sl_z = base_points(slot_cell, ML_OWN)
    base_x = jnp.concatenate([mm_x, sl_x])
    base_y = jnp.concatenate([mm_y, sl_y])
    base_z = jnp.concatenate([mm_z, sl_z])
    weights = spline(jnp.concatenate([mm_frac, slot_frac], 1))
    charge_grid = jnp.zeros((NG * NG * NG,), jnp.float32)
    for shift_x in range(4):
        for shift_y in range(4):
            for shift_z in range(4):
                grid_index = ((base_x + shift_x) % NG * NG + (base_y + shift_y) % NG) * NG + (base_z + shift_z) % NG
                contrib = site_charge * weights[shift_x, 0] * weights[shift_y, 1] * weights[shift_z, 2]
                charge_grid = charge_grid.at[grid_index].add(contrib)
    spectrum = jnp.fft.fftn(charge_grid.reshape(NG, NG, NG)) * (1.0 / (NG * math.sqrt(NG)))
    spectrum = jnp.transpose(spectrum[:KH], (1, 0, 2))
    return (charge, jnp.real(spectrum).astype(jnp.float32), jnp.imag(spectrum).astype(jnp.float32))
```

```python
import math

import jax
import jax.numpy as jnp
import numpy as np
from jax import lax
from jax.experimental import pallas as pl
from jax.experimental.pallas import tpu as pltpu
from jax.sharding import PartitionSpec as P

NG = 384
N_FFT = 32
N_SLAB = 16
YL = 24
ZL = 12
KX = 12
KY = 12
OWN = 32
ROWS = 512
COLS = 1024
ATOMS = 16384
SITES = 6144
CHUNK = 1024
XE = 392
YE = 32
ZE = 15

KE = 14.4
ALPHA = 0.08
SOFT = 0.01
SQPI = math.sqrt(math.pi)
F32 = jnp.float32
BF16 = jnp.bfloat16
VMEM_LIMIT = 48 * 1024 * 1024


def wave(points, freqs):
    angle = 2.0 * np.pi * ((points[:, None] * freqs[None, :]) % NG) / NG
    return np.cos(angle), np.sin(angle)


def two_parts(table):
    high = np.asarray(table, np.float32).astype(jnp.bfloat16)
    low = (np.asarray(table, np.float64) - high.astype(np.float64)).astype(jnp.bfloat16)
    return high, low


def x_table():
    points = np.arange(XE)
    cos, sin = wave(points, np.arange(NG // 2))
    cos, sin = (t.reshape(XE, N_SLAB, 1, KX) for t in (cos, sin))
    table = np.concatenate([cos, -sin], 2)
    table = table * (points < NG + 3)[:, None, None, None]
    return table.reshape(XE, N_SLAB * 2 * KX)


def y_tables():
    local = np.arange(YE)
    points = (np.arange(N_SLAB)[:, None] * YL + local[None, :]).reshape(-1)
    used = np.tile(local < YL + 3, N_SLAB)[:, None, None, None]
    cos, sin = wave(points, np.arange(NG))
    cos, sin = (t.reshape(-1, N_FFT, 1, KY) for t in (cos, sin))
    from_re = np.concatenate([cos, -sin], 2) * used
    from_im = np.concatenate([sin, cos], 2) * used
    return from_re.reshape(-1, 2 * NG), from_im.reshape(-1, 2 * NG)


def z_tables():
    local = np.arange(16)
    points = (np.arange(N_FFT)[:, None] * ZL + local[None, :]).reshape(-1)
    used = np.tile(local < ZL + 3, N_FFT)[:, None]
    scale = 1.0 / (NG * math.sqrt(NG))
    cos, sin = wave(points, np.arange(NG))
    from_re = np.concatenate([cos, -sin], 1) * used * scale
    from_im = np.concatenate([sin, cos], 1) * used * scale
    return from_re, from_im


def perm_y():
    table = np.zeros((2, KX, 16, 384), np.float32)
    for c in range(2):
        for k in range(KX):
            for z in range(ZE):
                table[c, k, z, z * 24 + c * KX + k] = 1.0
    return table.reshape(384, 384).astype(jnp.bfloat16)


def perm_z():
    table = np.zeros((2, KY, 16, 384), np.float32)
    for c in range(2):
        for k in range(KY):
            for x in range(KX):
                table[c, k, x, x * 24 + c * KY + k] = 1.0
    return table.reshape(384, 384).astype(jnp.bfloat16)


def split(value):
    high = value.astype(BF16)
    return high, (value - high.astype(F32)).astype(BF16)


def dot_nn(a, b):
    return lax.dot_general(a, b, (((1,), (0,)), ((), ())), preferred_element_type=F32)


def dot_nt(a, b):
    return lax.dot_general(a, b, (((1,), (1,)), ((), ())), preferred_element_type=F32)


def three(dot, a, b):
    return dot(a[0], b[0]) + dot(a[0], b[1]) + dot(a[1], b[0])


def spline(u):
    squared = u * u
    cubed = squared * u
    rest = 1.0 - u
    return (
        rest * rest * rest / 6.0,
        (3.0 * cubed - 6.0 * squared + 4.0) / 6.0,
        (-3.0 * cubed + 3.0 * squared + 3.0 * u + 1.0) / 6.0,
        cubed / 6.0,
    )


def placed(rows, cell, weights):
    off = lax.broadcasted_iota(jnp.int32, (rows, cell.shape[1]), 0) - cell
    value = jnp.where(off == 3, weights[3], 0.0)
    value = jnp.where(off == 2, weights[2], value)
    value = jnp.where(off == 1, weights[1], value)
    return jnp.where(off == 0, weights[0], value)


def spread_body(charge, frac, cell, xh, xl, out, acc):
    step = pl.program_id(0)

    @pl.when(step == 0)
    def _():
        acc[...] = jnp.zeros_like(acc)

    along_x = placed(XE, cell[0:1, :], spline(frac[0:1, :]))
    along_y = placed(YE, cell[1:2, :], spline(frac[1:2, :])) * charge[...]
    along_z = placed(16, cell[2:3, :], spline(frac[2:3, :]))
    plane = jnp.concatenate([along_z[z : z + 1, :] * along_y for z in range(ZE)], 0)
    acc[...] += three(dot_nt, split(plane), split(along_x))

    @pl.when(step == pl.num_programs(0) - 1)
    def _():
        freq = three(dot_nn, split(acc[...]), (xh[...], xl[...]))
        for s in range(N_SLAB):
            for z in range(ZE):
                out[s, :, z * 24 : z * 24 + 24] = freq[z * YE : z * YE + YE, s * 24 : s * 24 + 24]
            out[s, :, ZE * 24 : 384] = jnp.zeros((YE, 384 - ZE * 24), F32)


def spread(charge, frac, cell, xh, xl):
    whole = pl.BlockSpec((XE, 384), lambda i: (0, 0))
    return pl.pallas_call(
        spread_body,
        grid=(SITES // CHUNK,),
        in_specs=[
            pl.BlockSpec((1, CHUNK), lambda i: (0, i)),
            pl.BlockSpec((3, CHUNK), lambda i: (0, i)),
            pl.BlockSpec((3, CHUNK), lambda i: (0, i)),
            whole,
            whole,
        ],
        out_specs=pl.BlockSpec((N_SLAB, YE, 384), lambda i: (0, 0, 0)),
        out_shape=jax.ShapeDtypeStruct((N_SLAB, YE, 384), F32),
        scratch_shapes=[pltpu.VMEM((ZE * YE, XE), F32)],
        compiler_params=pltpu.CompilerParams(vmem_limit_bytes=VMEM_LIMIT),
        cost_estimate=pl.CostEstimate(flops=8_000_000_000, bytes_accessed=2_000_000, transcendentals=0),
        name="spread",
    )(charge.reshape(1, SITES), frac, cell, xh, xl)


def y_body(grid, charges, slots, xsh, xsl, perm, arh, arl, aih, ail, out):
    atom = slots[0:1, :].astype(jnp.int32)
    cell = slots[1:4, :].astype(jnp.int32)
    frac = slots[4:7, :]
    lane = lax.broadcasted_iota(jnp.int32, (128, ROWS), 0)
    pick = jnp.where(lane == atom % 128, 1.0, 0.0).astype(BF16)
    q_high, q_low = split(charges[...])
    rows = dot_nn(q_high, pick) + dot_nn(q_low, pick)
    charge = jnp.sum(jnp.where(lane == atom // 128, rows, 0.0), 0, keepdims=True)
    block = lax.broadcasted_iota(jnp.int32, (1, ROWS), 1) // OWN * YE
    along_y = placed(N_SLAB * YE, cell[1:2, :] + block, spline(frac[1:2, :]))
    along_z = placed(16, cell[2:3, :], spline(frac[2:3, :])) * charge
    along_x = placed(XE, cell[0:1, :], spline(frac[0:1, :]))
    wave_x = three(dot_nn, (xsh[...], xsl[...]), split(along_x))
    both = [along_z[z : z + 1, :] * wave_x for z in range(ZE)]
    both = jnp.concatenate(both + [jnp.zeros((24, ROWS), F32)], 0)
    total = grid[...] + three(dot_nt, split(along_y), split(both))
    high, low = split(total)
    high = dot_nt(perm[...], high).astype(BF16)
    low = dot_nt(perm[...], low).astype(BF16)
    freq = three(dot_nn, (high[:192], low[:192]), (arh[...], arl[...]))
    freq = freq + three(dot_nn, (high[192:], low[192:]), (aih[...], ail[...]))
    for f in range(N_FFT):
        for k in range(KX):
            out[f, :, k * 24 : k * 24 + 24] = freq[k * 16 : k * 16 + 16, f * 24 : f * 24 + 24]
        out[f, :, KX * 24 : 384] = jnp.zeros((16, 384 - KX * 24), F32)


def along_y(*operands):
    return pl.pallas_call(
        y_body,
        out_shape=jax.ShapeDtypeStruct((N_FFT, 16, 384), F32),
        compiler_params=pltpu.CompilerParams(vmem_limit_bytes=VMEM_LIMIT),
        cost_estimate=pl.CostEstimate(flops=4_000_000_000, bytes_accessed=5_000_000, transcendentals=0),
        name="along_y",
    )(*operands)


def z_body(grid, perm, brh, brl, bih, bil, out_re, out_im):
    high, low = split(grid[...])
    high = dot_nt(perm[...], high).astype(BF16)
    low = dot_nt(perm[...], low).astype(BF16)
    freq = three(dot_nn, (high[:192], low[:192]), (brh[...], brl[...]))
    freq = freq + three(dot_nn, (high[192:], low[192:]), (bih[...], bil[...]))
    for k in range(KY):
        out_re[k] = freq[k * 16 : k * 16 + KX, :NG]
        out_im[k] = freq[k * 16 : k * 16 + KX, NG:]


def along_z(*operands):
    shape = jax.ShapeDtypeStruct((KY, KX, NG), F32)
    return pl.pallas_call(
        z_body,
        out_shape=(shape, shape),
        compiler_params=pltpu.CompilerParams(vmem_limit_bytes=VMEM_LIMIT),
        cost_estimate=pl.CostEstimate(flops=3_000_000_000, bytes_accessed=5_000_000, transcendentals=0),
        name="along_z",
    )(*operands)


def couplings(row_pos, row_width, col_pos, col_width, row_ids, col_ids, col_diag):
    dist_sq = (row_pos[0][:, None] - col_pos[0][None, :]) ** 2
    dist_sq = dist_sq + (row_pos[1][:, None] - col_pos[1][None, :]) ** 2
    dist_sq = dist_sq + (row_pos[2][:, None] - col_pos[2][None, :]) ** 2
    distance = jnp.sqrt(dist_sq + SOFT)
    pair_len = jnp.sqrt(2.0 * (row_width[:, None] ** 2 + col_width[None, :] ** 2))
    kernel = KE * (lax.erf(distance / pair_len) - lax.erf(ALPHA * distance)) / distance
    return jnp.where(row_ids[:, None] == col_ids[None, :], col_diag[None, :], kernel)


def swap(value, axis):
    return lax.all_to_all(value, axis, 0, 0, tiled=True)


def to_all(value, axis):
    return swap(jnp.broadcast_to(value[None], (lax.axis_size(axis),) + value.shape), axis)


def guarded(value, pivot, scale):
    good = pivot > 1e-6 * scale
    return jnp.where(good, value / jnp.where(good, pivot, 1.0), 0.0)


def galerkin(m):
    l10 = m[2] / m[1]
    l20 = m[3] / m[1]
    d1 = m[3] - l10 * m[2]
    e12 = m[4] - l10 * m[3]
    l21 = guarded(e12, d1, m[3])
    d2 = (m[5] - l20 * m[3]) - l21 * e12
    g1 = m[1] - l10 * m[0]
    g2 = (m[2] - l20 * m[0]) - l21 * g1
    c2 = guarded(g2, d2, m[5])
    c1 = guarded(g1, d1, m[3]) - l21 * c2
    c0 = m[0] / m[1] - l10 * c1 - l20 * c2
    return c0, c1, c2


def on_device(
    ml_pos,
    ml_width,
    ml_drive,
    ml_hard,
    mm_charge,
    mm_frac,
    mm_cell,
    slot_atom,
    slot_frac,
    slot_cell,
):
    f = lax.axis_index("fft")
    s = lax.axis_index("slab")

    def rows_of(value):
        return lax.dynamic_index_in_dim(value.reshape(N_FFT, ROWS), f, 0, False)

    def cols_of(value):
        value = value.reshape(N_FFT, N_SLAB, OWN)
        return lax.dynamic_index_in_dim(value, s, 1, False).reshape(COLS)

    drive = -ml_drive
    slots = jnp.concatenate(
        [
            drive[None],
            slot_atom.astype(F32)[None],
            slot_cell.astype(F32),
            slot_frac,
        ],
        0,
    )
    got = to_all(slots, "slab")
    got = jnp.transpose(got, (1, 0, 2)).reshape(8, ROWS)
    drive_rows = got[0]

    ids = jnp.arange(ATOMS, dtype=jnp.int32)
    own_first = f * ROWS + s * OWN
    own_width = lax.dynamic_slice_in_dim(ml_width, own_first, OWN)
    own_diag = ml_hard + KE * (1.0 / (own_width * SQPI) - 2.0 * ALPHA / SQPI)
    col_diag = lax.dynamic_update_slice_in_dim(jnp.zeros((COLS,), F32), own_diag, f * OWN, 0)
    matrix = couplings(
        [rows_of(ml_pos[i]) for i in range(3)],
        rows_of(ml_width),
        [cols_of(ml_pos[i]) for i in range(3)],
        cols_of(ml_width),
        rows_of(ids),
        cols_of(ids),
        col_diag,
    )
    part = jnp.sum(matrix * drive_rows[:, None], 0)
    got_1 = to_all(jnp.concatenate([part, drive_rows]), "fft")
    first_cols = jnp.sum(got_1[:, :COLS], 0)
    drive_full = got_1[:, COLS:].reshape(ATOMS)

    xh, xl = (jnp.asarray(t) for t in two_parts(x_table()))
    mm = spread(mm_charge, mm_frac, mm_cell, xh, xl)
    part = jnp.sum(matrix * first_cols[None, :], 1)
    tail = jnp.concatenate([part, first_cols]).reshape(1, 4, 384)
    tail = jnp.broadcast_to(tail, (N_SLAB, 4, 384))
    got_2 = swap(jnp.concatenate([mm[:, : YE - 4], tail], 1), "slab")
    tail = got_2[:, YE - 4 :].reshape(N_SLAB, 1536)
    second_rows = jnp.sum(tail[:, :ROWS], 0)
    first_full = jnp.transpose(tail[:, ROWS:].reshape(N_SLAB, N_FFT, OWN), (1, 0, 2)).reshape(ATOMS)

    second_full = to_all(second_rows, "fft").reshape(ATOMS)
    second_cols = cols_of(second_full)
    quad = jnp.sum(second_rows * jnp.sum(matrix * second_cols[None, :], 1))
    quad = jnp.sum(to_all(jnp.full((128,), quad), "slab")[:, 0])
    quad = jnp.sum(to_all(jnp.full((128,), quad), "fft")[:, 0])
    moments = [
        jnp.sum(drive_full * drive_full),
        jnp.sum(drive_full * first_full),
        jnp.sum(first_full * first_full),
        jnp.sum(first_full * second_full),
        jnp.sum(second_full * second_full),
        quad,
    ]
    c0, c1, c2 = galerkin(moments)
    charge = c0 * drive_full + c1 * first_full + c2 * second_full
    charge_piece = lax.dynamic_slice_in_dim(charge, own_first, OWN)

    xs = x_table().T.reshape(N_SLAB, 24, XE)
    xsh, xsl = (lax.dynamic_index_in_dim(jnp.asarray(t), s, 0, False) for t in two_parts(xs))
    arh, arl, aih, ail = (jnp.asarray(t) for part in y_tables() for t in two_parts(part))
    spectrum = along_y(
        got_2.reshape(N_SLAB * YE, 384),
        charge.reshape(128, 128),
        got[1:8],
        xsh,
        xsl,
        jnp.asarray(perm_y()),
        arh,
        arl,
        aih,
        ail,
    )
    spectrum = swap(spectrum, "fft").reshape(N_FFT * 16, 384)
    brh, brl, bih, bil = (jnp.asarray(t) for part in z_tables() for t in two_parts(part))
    struct_re, struct_im = along_z(spectrum, jnp.asarray(perm_z()), brh, brl, bih, bil)
    return (charge_piece, struct_re, struct_im)


def solution(mesh):
    return jax.shard_map(
        on_device,
        mesh=mesh,
        in_specs=(
            P(),
            P(),
            P(("fft", "slab")),
            P(("fft", "slab")),
            P(("fft", "slab")),
            P(None, ("fft", "slab")),
            P(None, ("fft", "slab")),
            P(("fft", "slab")),
            P(None, ("fft", "slab")),
            P(None, ("fft", "slab")),
        ),
        out_specs=(P(("fft", "slab")), P("fft", "slab", None), P("fft", "slab", None)),
        check_vma=False,
    )
```

```python
import math

import jax
import jax.numpy as jnp
import numpy as np
from jax import lax
from jax.experimental import pallas as pl
from jax.experimental.pallas import tpu as pltpu
from jax.sharding import PartitionSpec as P

NG = 384
N_FFT = 32
N_SLAB = 16
YL = 24
ZL = 12
KX = 12
KY = 12
OWN = 32
ROWS = 512
COLS = 1024
ATOMS = 16384
SITES = 6144
CHUNK = 1024
XE = 392
YE = 32
ZE = 15

KE = 14.4
ALPHA = 0.08
SOFT = 0.01
SQPI = math.sqrt(math.pi)
F32 = jnp.float32
BF16 = jnp.bfloat16
VMEM_LIMIT = 48 * 1024 * 1024


def wave(points, freqs):
    angle = 2.0 * np.pi * ((points[:, None] * freqs[None, :]) % NG) / NG
    return np.cos(angle), np.sin(angle)


def two_parts(table):
    high = np.asarray(table, np.float32).astype(jnp.bfloat16)
    low = (np.asarray(table, np.float64) - high.astype(np.float64)).astype(jnp.bfloat16)
    return high, low


def x_table():
    points = np.arange(XE)
    cos, sin = wave(points, np.arange(NG // 2))
    cos, sin = (t.reshape(XE, N_SLAB, 1, KX) for t in (cos, sin))
    table = np.concatenate([cos, -sin], 2)
    table = table * (points < NG + 3)[:, None, None, None]
    return table.reshape(XE, N_SLAB * 2 * KX)


def y_tables():
    local = np.arange(YE)
    points = (np.arange(N_SLAB)[:, None] * YL + local[None, :]).reshape(-1)
    used = np.tile(local < YL + 3, N_SLAB)[:, None, None, None]
    cos, sin = wave(points, np.arange(NG))
    cos, sin = (t.reshape(-1, N_FFT, 1, KY) for t in (cos, sin))
    from_re = np.concatenate([cos, -sin], 2) * used
    from_im = np.concatenate([sin, cos], 2) * used
    return from_re.reshape(-1, 2 * NG), from_im.reshape(-1, 2 * NG)


def z_tables():
    local = np.arange(16)
    points = (np.arange(N_FFT)[:, None] * ZL + local[None, :]).reshape(-1)
    used = np.tile(local < ZL + 3, N_FFT)[:, None]
    scale = 1.0 / (NG * math.sqrt(NG))
    cos, sin = wave(points, np.arange(NG))
    from_re = np.concatenate([cos, -sin], 1) * used * scale
    from_im = np.concatenate([sin, cos], 1) * used * scale
    return from_re, from_im


def perm_y():
    table = np.zeros((2, KX, 16, 384), np.float32)
    for c in range(2):
        for k in range(KX):
            for z in range(ZE):
                table[c, k, z, z * 24 + c * KX + k] = 1.0
    return table.reshape(384, 384).astype(jnp.bfloat16)


def perm_z():
    table = np.zeros((2, KY, 16, 384), np.float32)
    for c in range(2):
        for k in range(KY):
            for x in range(KX):
                table[c, k, x, x * 24 + c * KY + k] = 1.0
    return table.reshape(384, 384).astype(jnp.bfloat16)


def step_table(count):
    freqs = (np.arange(count) * 12)[:, None] + np.arange(16)[None, :]
    angle = 2.0 * np.pi * freqs[:, :, None] * np.arange(4)[None, None, :] / NG
    return np.concatenate([np.cos(angle), -np.sin(angle)], 2).astype(np.float32)


def split(value):
    high = value.astype(BF16)
    return high, (value - high.astype(F32)).astype(BF16)


def dot_nn(a, b):
    return lax.dot_general(a, b, (((1,), (0,)), ((), ())), preferred_element_type=F32)


def dot_nt(a, b):
    return lax.dot_general(a, b, (((1,), (1,)), ((), ())), preferred_element_type=F32)


def three(dot, a, b):
    return dot(a[0], b[0]) + dot(a[0], b[1]) + dot(a[1], b[0])


def spline(u):
    squared = u * u
    cubed = squared * u
    rest = 1.0 - u
    return (
        rest * rest * rest / 6.0,
        (3.0 * cubed - 6.0 * squared + 4.0) / 6.0,
        (-3.0 * cubed + 3.0 * squared + 3.0 * u + 1.0) / 6.0,
        cubed / 6.0,
    )


def placed(rows, cell, weights):
    off = lax.broadcasted_iota(jnp.int32, (rows, cell.shape[1]), 0) - cell
    value = jnp.where(off == 3, weights[3], 0.0)
    value = jnp.where(off == 2, weights[2], value)
    value = jnp.where(off == 1, weights[1], value)
    return jnp.where(off == 0, weights[0], value)


def spread_body(charge, frac, cell, xh, xl, out, acc):
    step = pl.program_id(0)

    @pl.when(step == 0)
    def _():
        acc[...] = jnp.zeros_like(acc)

    along_x = placed(XE, cell[0:1, :], spline(frac[0:1, :]))
    along_y = placed(YE, cell[1:2, :], spline(frac[1:2, :])) * charge[...]
    along_z = placed(16, cell[2:3, :], spline(frac[2:3, :]))
    plane = jnp.concatenate([along_z[z : z + 1, :] * along_y for z in range(ZE)], 0)
    acc[...] += three(dot_nt, split(plane), split(along_x))

    @pl.when(step == pl.num_programs(0) - 1)
    def _():
        freq = three(dot_nn, split(acc[...]), (xh[...], xl[...]))
        for s in range(N_SLAB):
            for z in range(ZE):
                out[s, :, z * 24 : z * 24 + 24] = freq[z * YE : z * YE + YE, s * 24 : s * 24 + 24]
            out[s, :, ZE * 24 : 384] = jnp.zeros((YE, 384 - ZE * 24), F32)


def spread(charge, frac, cell, xh, xl):
    whole = pl.BlockSpec((XE, 384), lambda i: (0, 0))
    return pl.pallas_call(
        spread_body,
        grid=(SITES // CHUNK,),
        in_specs=[
            pl.BlockSpec((1, CHUNK), lambda i: (0, i)),
            pl.BlockSpec((3, CHUNK), lambda i: (0, i)),
            pl.BlockSpec((3, CHUNK), lambda i: (0, i)),
            whole,
            whole,
        ],
        out_specs=pl.BlockSpec((N_SLAB, YE, 384), lambda i: (0, 0, 0)),
        out_shape=jax.ShapeDtypeStruct((N_SLAB, YE, 384), F32),
        scratch_shapes=[pltpu.VMEM((ZE * YE, XE), F32)],
        compiler_params=pltpu.CompilerParams(vmem_limit_bytes=VMEM_LIMIT),
        cost_estimate=pl.CostEstimate(flops=8_000_000_000, bytes_accessed=2_000_000, transcendentals=0),
        name="spread",
    )(charge.reshape(1, SITES), frac, cell, xh, xl)


def y_body(grid, part, rows, perm, arh, arl, aih, ail, out):
    high, low = split(grid[...])
    high = dot_nt(perm[...], high).astype(BF16)
    low = dot_nt(perm[...], low).astype(BF16)
    freq = three(dot_nn, (high[:192], low[:192]), (arh[...], arl[...]))
    freq = freq + three(dot_nn, (high[192:], low[192:]), (aih[...], ail[...]))
    for f in range(N_FFT):
        for k in range(KX):
            out[f, :, k * 24 : k * 24 + 24] = freq[k * 16 : k * 16 + 16, f * 24 : f * 24 + 24]
        out[f, :, 288:352] = part[...]
        out[f, :, 352:384] = rows[...]


def along_y(*operands):
    return pl.pallas_call(
        y_body,
        out_shape=jax.ShapeDtypeStruct((N_FFT, 16, 384), F32),
        compiler_params=pltpu.CompilerParams(vmem_limit_bytes=VMEM_LIMIT),
        cost_estimate=pl.CostEstimate(flops=4_000_000_000, bytes_accessed=5_000_000, transcendentals=0),
        name="along_y",
    )(*operands)


def unit(turns):
    half = (turns - 0.5) * math.pi
    square = half * half
    sine = 0.0
    for power in (11, 9, 7, 5, 3):
        sine = (sine + (-1.0) ** (power // 2) / math.factorial(power)) * square
    sine = half * (1.0 + sine)
    cosine = 0.0
    for power in (12, 10, 8, 6, 4, 2):
        cosine = (cosine + (-1.0) ** (power // 2) / math.factorial(power)) * square
    cosine = 1.0 + cosine
    return 2.0 * sine * sine - 1.0, 2.0 * sine * cosine


def site_wave(first, base, fraction, steps):
    freq = first + lax.broadcasted_iota(jnp.int32, (16, 1), 0).astype(F32)
    phase = freq * base
    phase = phase - NG * jnp.floor(phase * (1.0 / NG))
    re, im = unit(phase * (1.0 / NG))
    weights = spline(fraction)
    w_re = sum(steps[:, i : i + 1] * weights[i] for i in range(4))
    w_im = sum(steps[:, 4 + i : 5 + i] * weights[i] for i in range(1, 4))
    return re * w_re - im * w_im, re * w_im + im * w_re


def table_body(place, slots, steps, out):
    block = (lax.broadcasted_iota(jnp.int32, (1, ROWS), 1) // OWN * YL).astype(F32)
    for g in range(8):
        cell = slots[g, 2:5, :]
        frac = slots[g, 5:8, :]
        x_re, x_im = site_wave(place[0].astype(F32), cell[0:1], frac[0:1], steps[:, 0:8])
        y_re, y_im = site_wave(place[1].astype(F32), cell[1:2] + block, frac[1:2], steps[:, 8:16])
        out[g, 0:16] = x_re
        out[g, 16:32] = x_im
        out[g, 32:48] = y_re
        out[g, 48:64] = y_im


def tables(place, slots, steps):
    return pl.pallas_call(
        table_body,
        grid=(4,),
        in_specs=[
            pl.BlockSpec(memory_space=pltpu.SMEM),
            pl.BlockSpec((8, 8, ROWS), lambda i: (i, 0, 0)),
            pl.BlockSpec((16, 16), lambda i: (0, 0)),
        ],
        out_specs=pl.BlockSpec((8, 64, ROWS), lambda i: (i, 0, 0)),
        out_shape=jax.ShapeDtypeStruct((N_FFT, 64, ROWS), F32),
        compiler_params=pltpu.CompilerParams(vmem_limit_bytes=VMEM_LIMIT),
        cost_estimate=pl.CostEstimate(flops=2_000_000_000, bytes_accessed=5_000_000, transcendentals=0),
        name="tables",
    )(place, slots, steps)


def ml_body(charges, slots, waves, out):
    lane = lax.broadcasted_iota(jnp.int32, (128, ROWS), 0)
    q_high, q_low = split(charges[...])
    for g in range(8):
        atom = slots[g, 1:2, :].astype(jnp.int32)
        cell = slots[g, 4:5, :].astype(jnp.int32)
        pick = jnp.where(lane == (atom & 127), 1.0, 0.0).astype(BF16)
        rows = dot_nn(q_high, pick) + dot_nn(q_low, pick)
        here = lane == (atom >> 7)
        placed_z = placed(16, cell, spline(slots[g, 7:8, :]))
        both = [
            placed_z * jnp.sum(jnp.where(here, rows[v * 128 : v * 128 + 128], 0.0), 0, keepdims=True)
            for v in range(2)
        ]
        x_re, x_im = waves[g, 0:16], waves[g, 16:32]
        parts_re, parts_im = [], []
        for k in range(KY):
            y_re, y_im = waves[g, 32 + k : 33 + k], waves[g, 48 + k : 49 + k]
            parts_re.append(y_re * x_re - y_im * x_im)
            parts_im.append(y_re * x_im + y_im * x_re)
        pairs = jnp.concatenate(parts_re + parts_im, 0)
        total = three(dot_nt, split(pairs), split(jnp.concatenate(both, 0)))
        out[0, :, g * 16 : g * 16 + 16] = total[:, :16]
        out[1, :, g * 16 : g * 16 + 16] = total[:, 16:]


def ml_waves(charges, slots, waves):
    return pl.pallas_call(
        ml_body,
        grid=(4,),
        in_specs=[
            pl.BlockSpec((256, 128), lambda i: (0, 0)),
            pl.BlockSpec((8, 8, ROWS), lambda i: (i, 0, 0)),
            pl.BlockSpec((8, 64, ROWS), lambda i: (i, 0, 0)),
        ],
        out_specs=pl.BlockSpec((2, 384, 128), lambda i: (0, 0, i)),
        out_shape=jax.ShapeDtypeStruct((2, 384, ROWS), F32),
        compiler_params=pltpu.CompilerParams(vmem_limit_bytes=VMEM_LIMIT),
        cost_estimate=pl.CostEstimate(flops=8_000_000_000, bytes_accessed=7_000_000, transcendentals=0),
        name="ml_waves",
    )(charges, slots, waves)


def guarded(value, pivot, scale):
    good = pivot > 1e-6 * scale
    return jnp.where(good, value / jnp.where(good, pivot, 1.0), 0.0)


def moment_body(v0, v1, v2, charges, rest):
    def dot(a, b):
        return jnp.sum(jnp.sum(a * b, 0, keepdims=True), 1, keepdims=True)

    a, b, c = v0[...], v1[...], v2[...]
    m0, m1, m2, m3, m4 = dot(a, a), dot(a, b), dot(b, b), dot(b, c), dot(c, c)
    l10 = m2 / m1
    l20 = m3 / m1
    d1 = m3 - l10 * m2
    e12 = m4 - l10 * m3
    l21 = guarded(e12, d1, m3)
    g1 = m1 - l10 * m0
    g2 = (m2 - l20 * m0) - l21 * g1
    c1 = guarded(g1, d1, m3)
    c0 = m0 / m1 - l10 * c1
    charges[0:128] = c0 * a + c1 * b
    charges[128:256] = c - l21 * b + (l10 * l21 - l20) * a
    rest[0:1] = jnp.broadcast_to(l20 * m3 + l21 * e12, (1, 128))
    rest[1:2] = jnp.broadcast_to(g2, (1, 128))


def moments(*operands):
    return pl.pallas_call(
        moment_body,
        out_shape=(
            jax.ShapeDtypeStruct((256, 128), F32),
            jax.ShapeDtypeStruct((2, 128), F32),
        ),
        name="moments",
    )(*operands)


def z_body(grid, ml, quads, rest, pieces, perm, brh, brl, bih, bil, out_re, out_im, out_q):
    m5 = jnp.sum(quads[...], 0, keepdims=True)
    step = guarded(rest[1:2], m5 - rest[0:1], m5)[:, 0:1]
    high, low = split(grid[...])
    total = dot_nt(perm[...], high) + dot_nt(perm[...], low)
    high, low = split(total + (ml[0] + step * ml[1]))
    freq = three(dot_nn, (high[:192], low[:192]), (brh[...], brl[...]))
    freq = freq + three(dot_nn, (high[192:], low[192:]), (bih[...], bil[...]))
    for k in range(KY):
        out_re[k] = freq[k * 16 : k * 16 + KX, :NG]
        out_im[k] = freq[k * 16 : k * 16 + KX, NG:]
    out_q[...] = pieces[0:1] + step * pieces[1:2]


def along_z(*operands):
    shape = jax.ShapeDtypeStruct((KY, KX, NG), F32)
    return pl.pallas_call(
        z_body,
        out_shape=(shape, shape, jax.ShapeDtypeStruct((1, OWN), F32)),
        compiler_params=pltpu.CompilerParams(vmem_limit_bytes=VMEM_LIMIT),
        cost_estimate=pl.CostEstimate(flops=3_000_000_000, bytes_accessed=5_000_000, transcendentals=0),
        name="along_z",
    )(*operands)


def couplings(row_pos, row_width, col_pos, col_width, row_ids, col_ids, col_diag):
    dist_sq = (row_pos[0][:, None] - col_pos[0][None, :]) ** 2
    dist_sq = dist_sq + (row_pos[1][:, None] - col_pos[1][None, :]) ** 2
    dist_sq = dist_sq + (row_pos[2][:, None] - col_pos[2][None, :]) ** 2
    distance = jnp.sqrt(dist_sq + SOFT)
    pair_len = jnp.sqrt(2.0 * (row_width[:, None] ** 2 + col_width[None, :] ** 2))
    kernel = KE * (lax.erf(distance / pair_len) - lax.erf(ALPHA * distance)) / distance
    return jnp.where(row_ids[:, None] == col_ids[None, :], col_diag[None, :], kernel)


def swap(value, axis):
    return lax.all_to_all(value, axis, 0, 0, tiled=True)


def to_all(value, axis):
    return swap(jnp.broadcast_to(value[None], (lax.axis_size(axis),) + value.shape), axis)


def on_device(
    ml_pos,
    ml_width,
    ml_drive,
    ml_hard,
    mm_charge,
    mm_frac,
    mm_cell,
    slot_atom,
    slot_frac,
    slot_cell,
):
    f = lax.axis_index("fft")
    s = lax.axis_index("slab")

    def rows_of(value):
        return lax.dynamic_index_in_dim(value.reshape(N_FFT, ROWS), f, 0, False)

    def cols_of(value):
        value = value.reshape(N_FFT, N_SLAB, OWN)
        return lax.dynamic_index_in_dim(value, s, 1, False).reshape(COLS)

    drive = -ml_drive
    slots = jnp.concatenate(
        [
            drive[None],
            slot_atom.astype(F32)[None],
            slot_cell.astype(F32),
            slot_frac,
        ],
        0,
    )
    got = to_all(slots, "slab")
    got = jnp.transpose(got, (1, 0, 2)).reshape(8, ROWS)
    drive_rows = got[0]

    ids = jnp.arange(ATOMS, dtype=jnp.int32)
    own_first = f * ROWS + s * OWN
    own_width = lax.dynamic_slice_in_dim(ml_width, own_first, OWN)
    own_diag = ml_hard + KE * (1.0 / (own_width * SQPI) - 2.0 * ALPHA / SQPI)
    col_diag = lax.dynamic_update_slice_in_dim(jnp.zeros((COLS,), F32), own_diag, f * OWN, 0)
    matrix = couplings(
        [rows_of(ml_pos[i]) for i in range(3)],
        rows_of(ml_width),
        [cols_of(ml_pos[i]) for i in range(3)],
        cols_of(ml_width),
        rows_of(ids),
        cols_of(ids),
        col_diag,
    )
    matrix = lax.optimization_barrier(matrix)
    part = jnp.sum(matrix * drive_rows[:, None], 0)
    got_1 = to_all(jnp.concatenate([part, got.reshape(8 * ROWS)]), "fft")
    first_cols = jnp.sum(got_1[:, :COLS], 0)
    slots = got_1[:, COLS:].reshape(N_FFT, 8, ROWS)

    xh, xl = (jnp.asarray(t) for t in two_parts(x_table()))
    mm = spread(mm_charge, mm_frac, mm_cell, xh, xl)
    part = jnp.sum(matrix * first_cols[None, :], 1)
    tail = jnp.concatenate([part, first_cols]).reshape(1, 4, 384)
    tail = jnp.broadcast_to(tail, (N_SLAB, 4, 384))
    got_2 = swap(jnp.concatenate([mm[:, : YE - 4], tail], 1), "slab")
    tail = got_2[:, YE - 4 :].reshape(N_SLAB, 1536)
    second_rows = jnp.sum(tail[:, :ROWS], 0)
    first_full = jnp.transpose(tail[:, ROWS:].reshape(N_SLAB, N_FFT, OWN), (1, 0, 2))
    part = jnp.sum(matrix * second_rows[:, None], 0)

    arh, arl, aih, ail = (jnp.asarray(t) for half in y_tables() for t in two_parts(half))
    spectrum = along_y(
        got_2.reshape(N_SLAB * YE, 384),
        part.reshape(16, 64),
        second_rows.reshape(16, OWN),
        jnp.asarray(perm_y()),
        arh,
        arl,
        aih,
        ail,
    )
    got_3 = swap(spectrum, "fft")
    third_cols = jnp.sum(got_3[:, :, 288:352], 0).reshape(COLS)
    second_full = got_3[:, :, 352:384]
    second_cols = lax.dynamic_index_in_dim(second_full, s, 1, False).reshape(COLS)
    quad = jnp.sum(third_cols * second_cols)
    quads = to_all(jnp.full((128,), quad), "slab")

    steps_x = step_table(N_SLAB)
    steps_y = step_table(N_FFT)
    steps = jnp.concatenate(
        [
            lax.dynamic_index_in_dim(jnp.asarray(steps_x), s, 0, False),
            lax.dynamic_index_in_dim(jnp.asarray(steps_y), f, 0, False),
        ],
        1,
    )
    waves = tables(jnp.stack([s * KX, f * KY]).astype(jnp.int32), slots, steps)
    charges, rest = moments(
        slots[:, 0].reshape(128, 128),
        first_full.reshape(128, 128),
        second_full.reshape(128, 128),
    )
    ml = ml_waves(charges, slots, waves)
    pieces = lax.dynamic_slice_in_dim(charges.reshape(2, ATOMS), own_first, OWN, 1)
    brh, brl, bih, bil = (jnp.asarray(t) for half in z_tables() for t in two_parts(half))
    struct_re, struct_im, charge = along_z(
        got_3.reshape(N_FFT * 16, 384),
        ml,
        quads,
        rest,
        pieces,
        jnp.asarray(perm_z()),
        brh,
        brl,
        bih,
        bil,
    )
    return (charge.reshape(OWN), struct_re, struct_im)


def solution(mesh):
    return jax.shard_map(
        on_device,
        mesh=mesh,
        in_specs=(
            P(),
            P(),
            P(("fft", "slab")),
            P(("fft", "slab")),
            P(("fft", "slab")),
            P(None, ("fft", "slab")),
            P(None, ("fft", "slab")),
            P(("fft", "slab")),
            P(None, ("fft", "slab")),
            P(None, ("fft", "slab")),
        ),
        out_specs=(P(("fft", "slab")), P("fft", "slab", None), P("fft", "slab", None)),
        check_vma=False,
    )
```

```python
import math

import jax
import jax.numpy as jnp
import numpy as np
from jax import lax
from jax.experimental import pallas as pl
from jax.experimental.pallas import tpu as pltpu
from jax.sharding import PartitionSpec as P

NG = 384
N_FFT = 32
N_SLAB = 16
YL = 24
ZL = 12
KX = 12
KY = 12
OWN = 32
ROWS = 512
COLS = 1024
ATOMS = 16384
SITES = 6144
CHUNK = 1024
XE = 392
YE = 32
ZE = 15
PAIRS = 288

KE = 14.4
ALPHA = 0.08
SOFT = 0.01
SQPI = math.sqrt(math.pi)
F32 = jnp.float32
BF16 = jnp.bfloat16
VMEM_LIMIT = 24 * 1024 * 1024


def wave(points, freqs):
    angle = 2.0 * np.pi * ((points[:, None] * freqs[None, :]) % NG) / NG
    return np.cos(angle), np.sin(angle)


def two_parts(table):
    high = np.asarray(table, np.float32).astype(jnp.bfloat16)
    low = (np.asarray(table, np.float64) - high.astype(np.float64)).astype(jnp.bfloat16)
    return high, low


def x_table():
    points = np.arange(XE)
    cos, sin = wave(points, np.arange(NG // 2))
    cos, sin = (t.reshape(XE, N_SLAB, 1, KX) for t in (cos, sin))
    table = np.concatenate([cos, -sin], 2)
    table = table * (points < NG + 3)[:, None, None, None]
    return table.reshape(XE, N_SLAB * 2 * KX)


def y_tables():
    local = np.arange(YE)
    points = (np.arange(N_SLAB)[:, None] * YL + local[None, :]).reshape(-1)
    used = np.tile(local < YL + 3, N_SLAB)[:, None, None, None]
    cos, sin = wave(points, np.arange(NG))
    cos, sin = (t.reshape(-1, N_FFT, 1, KY) for t in (cos, sin))
    from_re = np.concatenate([cos, -sin], 2) * used
    from_im = np.concatenate([sin, cos], 2) * used
    return from_re.reshape(-1, 2 * NG), from_im.reshape(-1, 2 * NG)


def z_tables():
    local = np.arange(16)
    points = (np.arange(N_FFT)[:, None] * ZL + local[None, :]).reshape(-1)
    used = np.tile(local < ZL + 3, N_FFT)[:, None]
    scale = 1.0 / (NG * math.sqrt(NG))
    cos, sin = wave(points, np.arange(NG))
    return cos * used * scale, sin * used * scale


def perm_y():
    table = np.zeros((2, KX, 16, 384), np.float32)
    for c in range(2):
        for k in range(KX):
            for z in range(ZE):
                table[c, k, z, z * 24 + c * KX + k] = 1.0
    return table.reshape(384, 384).astype(jnp.bfloat16)


def perm_z():
    table = np.zeros((384, PAIRS), np.float32)
    for c in range(2):
        for k in range(KY):
            for x in range(KX):
                column = c * 96 + k * 8 + x if x < 8 else 192 + c * 48 + k * 4 + x - 8
                table[x * 24 + c * KY + k, column] = 1.0
    return table.astype(jnp.bfloat16)


def step_table(count):
    local = np.concatenate([np.arange(12), np.arange(8, 12)])
    freqs = (np.arange(count) * 12)[:, None] + local[None, :]
    angle = 2.0 * np.pi * freqs[:, :, None] * np.arange(4)[None, None, :] / NG
    return np.concatenate([np.cos(angle), -np.sin(angle)], 2).astype(np.float32)


def split(value):
    high = value.astype(BF16)
    return high, (value - high.astype(F32)).astype(BF16)


def dot_nn(a, b):
    return lax.dot_general(a, b, (((1,), (0,)), ((), ())), preferred_element_type=F32)


def dot_nt(a, b):
    return lax.dot_general(a, b, (((1,), (1,)), ((), ())), preferred_element_type=F32)


def dot_tn(a, b):
    return lax.dot_general(a, b, (((0,), (0,)), ((), ())), preferred_element_type=F32)


def three(dot, a, b):
    return dot(a[0], b[0]) + dot(a[0], b[1]) + dot(a[1], b[0])


def spline(u):
    squared = u * u
    cubed = squared * u
    rest = 1.0 - u
    return (
        rest * rest * rest / 6.0,
        (3.0 * cubed - 6.0 * squared + 4.0) / 6.0,
        (-3.0 * cubed + 3.0 * squared + 3.0 * u + 1.0) / 6.0,
        cubed / 6.0,
    )


def placed(rows, cell, weights):
    off = lax.broadcasted_iota(jnp.int32, (rows, cell.shape[1]), 0) - cell
    value = jnp.where(off == 3, weights[3], 0.0)
    value = jnp.where(off == 2, weights[2], value)
    value = jnp.where(off == 1, weights[1], value)
    return jnp.where(off == 0, weights[0], value)


def spread_body(charge, frac, cell, xh, xl, out, acc):
    step = pl.program_id(0)

    @pl.when(step == 0)
    def _():
        acc[...] = jnp.zeros_like(acc)

    along_x = placed(XE, cell[0:1, :], spline(frac[0:1, :]))
    along_y = placed(YE, cell[1:2, :], spline(frac[1:2, :])) * charge[...]
    along_z = placed(16, cell[2:3, :], spline(frac[2:3, :]))
    plane = jnp.concatenate([along_z[z : z + 1, :] * along_y for z in range(ZE)], 0)
    acc[...] += three(dot_nt, split(plane), split(along_x))

    @pl.when(step == pl.num_programs(0) - 1)
    def _():
        freq = three(dot_nn, split(acc[...]), (xh[...], xl[...]))
        for s in range(N_SLAB):
            for z in range(ZE):
                out[s, :, z * 24 : z * 24 + 24] = freq[z * YE : z * YE + YE, s * 24 : s * 24 + 24]
            out[s, :, ZE * 24 : 384] = jnp.zeros((YE, 384 - ZE * 24), F32)


def spread(charge, frac, cell, xh, xl):
    whole = pl.BlockSpec((XE, 384), lambda i: (0, 0))
    return pl.pallas_call(
        spread_body,
        grid=(SITES // CHUNK,),
        in_specs=[
            pl.BlockSpec((1, CHUNK), lambda i: (0, i)),
            pl.BlockSpec((3, CHUNK), lambda i: (0, i)),
            pl.BlockSpec((3, CHUNK), lambda i: (0, i)),
            whole,
            whole,
        ],
        out_specs=pl.BlockSpec((N_SLAB, YE, 384), lambda i: (0, 0, 0)),
        out_shape=jax.ShapeDtypeStruct((N_SLAB, YE, 384), F32),
        scratch_shapes=[pltpu.VMEM((ZE * YE, XE), F32)],
        compiler_params=pltpu.CompilerParams(vmem_limit_bytes=VMEM_LIMIT),
        cost_estimate=pl.CostEstimate(flops=8_000_000_000, bytes_accessed=2_000_000, transcendentals=0),
        name="spread",
    )(charge.reshape(1, SITES), frac, cell, xh, xl)


def lanes(tiles):
    return jnp.concatenate([tiles[i : i + 1] for i in range(tiles.shape[0])], 1)


def pack_body(drive, atom, cell, frac, out):
    out[...] = jnp.zeros_like(out)
    for i in range(N_SLAB):
        out[i, 0:1, 0:OWN] = -drive[...]
        out[i, 1:2, 0:OWN] = atom[...].astype(F32)
        out[i, 2:5, 0:OWN] = cell[...].astype(F32)
        out[i, 5:8, 0:OWN] = frac[...]


def pack(drive, atom, cell, frac):
    return pl.pallas_call(
        pack_body,
        out_shape=jax.ShapeDtypeStruct((N_SLAB, 8, 128), F32),
        name="pack",
    )(drive.reshape(1, OWN), atom.reshape(1, OWN), cell, frac)


def erf_ratio(value):
    square = value * value
    p = 0.00022905065861350646
    for c in (0.0034082910107109506, 0.050955695062380861, 0.18520832239976145, 1.128379143519084):
        p = p * square + c
    q = -1.1791602954361697e-7
    for c in (
        0.000023547966471313185,
        0.0010179625278914885,
        0.014070470171167667,
        0.11098505178285362,
        0.49746925110067538,
        1.0,
    ):
        q = q * square + c
    return value * p, q


def couple_body(place, pos, width, hard, out, picked, rows, own):
    f, s = place[0], place[1]
    lane = lax.broadcasted_iota(jnp.int32, (8, 128), 1) >> 5
    for j in range(N_FFT):
        at = pl.multiple_of(j * ROWS + (s >> 2) * 128, 128)
        picked[j, 0:3, :] = pos[:, pl.ds(at, 128)]
        picked[j, 3:4, :] = width[:, pl.ds(at, 128)]
    tiles = []
    for tile in range(COLS // 128):
        value = jnp.zeros((8, 128), F32)
        for j in range(4):
            value = jnp.where(lane == j, pltpu.roll(picked[tile * 4 + j], ((j - (s & 3)) & 3) * OWN, 1), value)
        tiles.append(value)
    cols = jnp.concatenate(tiles, 1)
    at = pl.multiple_of(f * ROWS, 128)
    rows[0:3, :] = pos[:, pl.ds(at, ROWS)]
    rows[3:4, :] = width[:, pl.ds(at, ROWS)]
    side = jnp.transpose(rows[...])
    own[...] = jnp.zeros_like(own)
    own[0:1, 0:OWN] = hard[...]
    own_hard = pltpu.roll(own[...], (f & 3) * OWN, 1)[0:1]
    diag = jnp.concatenate([jnp.where((f >> 2) == t, own_hard, 0.0) for t in range(COLS // 128)], 1)
    diag = diag + KE * (1.0 / (cols[3:4] * SQPI) - 2.0 * ALPHA / SQPI)
    col_id = lax.broadcasted_iota(jnp.int32, (1, COLS), 1) - f * OWN
    col_id = jnp.where((col_id >= 0) & (col_id < OWN), col_id + s * OWN, -1)
    col_sq = 2.0 * cols[3:4] * cols[3:4]
    step = 16
    for first in range(0, ROWS, step):
        here = side[first : first + step]
        square = SOFT
        for i in range(3):
            gap = here[:, i : i + 1] - cols[i : i + 1]
            square = square + gap * gap
        inverse = lax.rsqrt(square)
        distance = square * inverse
        narrow = lax.rsqrt(2.0 * here[:, 3:4] * here[:, 3:4] + col_sq)
        p1, q1 = erf_ratio(jnp.minimum(distance * narrow, 3.832506856900711))
        p2, q2 = erf_ratio(jnp.minimum(distance * ALPHA, 3.832506856900711))
        value = KE * inverse * ((p1 * q2 - p2 * q1) / (q1 * q2))
        row_id = first + lax.broadcasted_iota(jnp.int32, (step, 1), 0)
        out[first : first + step] = jnp.where(row_id == col_id, diag, value)


def couple(place, pos, width, hard):
    return pl.pallas_call(
        couple_body,
        in_specs=[pl.BlockSpec(memory_space=pltpu.SMEM)] + [pl.BlockSpec(memory_space=pltpu.VMEM)] * 3,
        out_shape=jax.ShapeDtypeStruct((ROWS, COLS), F32),
        scratch_shapes=[pltpu.VMEM((N_FFT, 8, 128), F32), pltpu.VMEM((8, ROWS), F32), pltpu.VMEM((8, 128), F32)],
        compiler_params=pltpu.CompilerParams(vmem_limit_bytes=12 * 1024 * 1024),
        cost_estimate=pl.CostEstimate(flops=100_000_000, bytes_accessed=2_000_000, transcendentals=1_000_000),
        name="couple",
    )(place, pos, width.reshape(1, ATOMS), hard.reshape(1, OWN))


def first_body(got, matrix, out, slots):
    for s in range(N_SLAB):
        slots[:, s * OWN : s * OWN + OWN] = got[s, :, 0:OWN]
    every = slots[...]
    part = jnp.sum(matrix[...] * jnp.transpose(every)[:, 0:1], 0, keepdims=True)
    for i in range(8):
        out[0, i : i + 1, :] = part[:, i * 128 : i * 128 + 128]
    for i in range(4):
        out[0, 8 + i * 8 : 16 + i * 8, :] = every[:, i * 128 : i * 128 + 128]
    whole = out[0]
    for f in range(1, N_FFT):
        out[f] = whole


def first_product(got, matrix):
    return pl.pallas_call(
        first_body,
        out_shape=jax.ShapeDtypeStruct((N_FFT, 40, 128), F32),
        scratch_shapes=[pltpu.VMEM((8, ROWS), F32)],
        compiler_params=pltpu.CompilerParams(vmem_limit_bytes=12 * 1024 * 1024),
        name="first_product",
    )(got, matrix)


def y_body(grid, matrix, perm, arh, arl, aih, ail, out, side):
    got = grid[...]
    rows = jnp.sum(got[:, YE - 4 :, 0:128], 0)
    side[0:4, :] = rows
    turned = jnp.transpose(side[...])
    column = jnp.concatenate([turned[:, i : i + 1] for i in range(4)], 0)
    part = jnp.sum(matrix[...] * column, 0, keepdims=True)
    high, low = split(got.reshape(N_SLAB * YE, 384))
    high = dot_nt(perm[...], high).astype(BF16)
    low = dot_nt(perm[...], low).astype(BF16)
    freq = three(dot_nn, (high[:192], low[:192]), (arh[...], arl[...]))
    freq = freq + three(dot_nn, (high[192:], low[192:]), (aih[...], ail[...]))
    for i in range(16):
        out[0, i : i + 1, 288:320] = part[:, i * OWN : i * OWN + OWN]
        out[0, i : i + 1, 320:352] = part[:, ROWS + i * OWN : ROWS + i * OWN + OWN]
        out[0, i : i + 1, 352:384] = rows[i // 4 : i // 4 + 1, i % 4 * OWN : i % 4 * OWN + OWN]
    extra = out[0, :, 256:384]
    for f in range(N_FFT):
        if f > 0:
            out[f, :, 256:384] = extra
        for k in range(KX):
            out[f, :, k * 24 : k * 24 + 24] = freq[k * 16 : k * 16 + 16, f * 24 : f * 24 + 24]


def along_y(*operands):
    return pl.pallas_call(
        y_body,
        out_shape=jax.ShapeDtypeStruct((N_FFT, 16, 384), F32),
        scratch_shapes=[pltpu.VMEM((8, 128), F32)],
        compiler_params=pltpu.CompilerParams(vmem_limit_bytes=24 * 1024 * 1024),
        cost_estimate=pl.CostEstimate(flops=4_000_000_000, bytes_accessed=5_000_000, transcendentals=0),
        name="along_y",
    )(*operands)


def quad_body(place, got, out):
    s = place[1]
    third = jnp.sum(got[:, :, 32:96], 0)
    second = got[:, pl.ds(s, 1), 96:128].reshape(N_FFT, OWN)
    total = jnp.sum(third[:, 0:OWN] * second[0:16] + third[:, OWN:] * second[16:], 0, keepdims=True)
    total = jnp.sum(total, 1, keepdims=True)
    out[...] = jnp.broadcast_to(total[None], out.shape)


def quad_sum(place, got):
    return pl.pallas_call(
        quad_body,
        grid=(1,),
        in_specs=[
            pl.BlockSpec(memory_space=pltpu.SMEM),
            pl.BlockSpec((N_FFT, 16, 128), lambda i: (0, 0, 2)),
        ],
        out_specs=pl.BlockSpec((N_SLAB, 8, 128), lambda i: (0, 0, 0)),
        out_shape=jax.ShapeDtypeStruct((N_SLAB, 8, 128), F32),
        compiler_params=pltpu.CompilerParams(vmem_limit_bytes=8 * 1024 * 1024),
        name="quad_sum",
    )(place, got)


def unit(turns):
    half = (turns - 0.5) * math.pi
    square = half * half
    sine = 0.0
    for power in (11, 9, 7, 5, 3):
        sine = (sine + (-1.0) ** (power // 2) / math.factorial(power)) * square
    sine = half * (1.0 + sine)
    cosine = 0.0
    for power in (12, 10, 8, 6, 4, 2):
        cosine = (cosine + (-1.0) ** (power // 2) / math.factorial(power)) * square
    cosine = 1.0 + cosine
    return 2.0 * sine * sine - 1.0, 2.0 * sine * cosine


def site_wave(first, base, fraction, steps):
    local = lax.broadcasted_iota(jnp.int32, (16, 1), 0)
    freq = first + jnp.where(local < 12, local, local - 4).astype(F32)
    phase = freq * base
    phase = phase - NG * jnp.floor(phase * (1.0 / NG))
    re, im = unit(phase * (1.0 / NG))
    weights = spline(fraction)
    w_re = sum(steps[:, i : i + 1] * weights[i] for i in range(4))
    w_im = sum(steps[:, 4 + i : 5 + i] * weights[i] for i in range(1, 4))
    return re * w_re - im * w_im, re * w_im + im * w_re


def slot_rows(slots, g):
    return jnp.concatenate([slots[g, 8 + i * 8 : 16 + i * 8, :] for i in range(4)], 1)


def table_body(place, slots, steps, out):
    block = (lax.broadcasted_iota(jnp.int32, (1, ROWS), 1) // OWN * YL).astype(F32)
    first_x, first_y = (place[1] * KX).astype(F32), (place[0] * KY).astype(F32)
    for g in range(8):
        rows = slot_rows(slots, g)
        x_re, x_im = site_wave(first_x, rows[2:3], rows[5:6], steps[:, 0:8])
        y_re, y_im = site_wave(first_y, rows[3:4] + block, rows[6:7], steps[:, 8:16])
        out[g, 0:16] = x_re
        out[g, 16:32] = x_im
        out[g, 32:48] = y_re
        out[g, 48:64] = y_im


def tables(place, slots, steps):
    return pl.pallas_call(
        table_body,
        grid=(4,),
        in_specs=[
            pl.BlockSpec(memory_space=pltpu.SMEM),
            pl.BlockSpec((8, 40, 128), lambda i: (i, 0, 0)),
            pl.BlockSpec((16, 16), lambda i: (0, 0)),
        ],
        out_specs=pl.BlockSpec((8, 64, ROWS), lambda i: (i, 0, 0)),
        out_shape=jax.ShapeDtypeStruct((N_FFT, 64, ROWS), F32),
        compiler_params=pltpu.CompilerParams(vmem_limit_bytes=12 * 1024 * 1024),
        cost_estimate=pl.CostEstimate(flops=2_000_000_000, bytes_accessed=5_000_000, transcendentals=0),
        name="tables",
    )(place, slots, steps)


def ml_body(charges, slots, waves, out):
    upper = lax.broadcasted_iota(jnp.int32, (8, 1), 0) < 4
    for g in range(8):
        rows = slot_rows(slots, g)
        placed_z = placed(16, rows[4:5].astype(jnp.int32), spline(rows[7:8]))
        both = [placed_z * lanes(charges[v, g * 4 : g * 4 + 4, :]) for v in range(2)]
        z_high, z_low = split(jnp.concatenate(both, 0))
        x_re, x_im = waves[g, 0:8], waves[g, 16:24]
        parts_re, parts_im = [], []
        for k in range(KY):
            y_re, y_im = waves[g, 32 + k : 33 + k], waves[g, 48 + k : 49 + k]
            parts_re.append(y_re * x_re - y_im * x_im)
            parts_im.append(y_re * x_im + y_im * x_re)
        parts = parts_re + parts_im
        x_re, x_im = waves[g, 8:16], waves[g, 24:32]
        parts_re, parts_im = [], []
        for k in range(0, KY, 2):
            y_re = jnp.where(upper, waves[g, 32 + k : 33 + k], waves[g, 33 + k : 34 + k])
            y_im = jnp.where(upper, waves[g, 48 + k : 49 + k], waves[g, 49 + k : 50 + k])
            parts_re.append(y_re * x_re - y_im * x_im)
            parts_im.append(y_re * x_im + y_im * x_re)
        high, low = split(jnp.concatenate(parts + parts_re + parts_im, 0))
        total = dot_nt(jnp.concatenate([z_high, z_low], 0), high)
        out[g] = total[:32] + total[32:] + dot_nt(z_high, low)


def ml_waves(charges, slots, waves):
    return pl.pallas_call(
        ml_body,
        grid=(4,),
        in_specs=[
            pl.BlockSpec((2, 32, 128), lambda i: (0, i, 0)),
            pl.BlockSpec((8, 40, 128), lambda i: (i, 0, 0)),
            pl.BlockSpec((8, 64, ROWS), lambda i: (i, 0, 0)),
        ],
        out_specs=pl.BlockSpec((8, 32, PAIRS), lambda i: (i, 0, 0)),
        out_shape=jax.ShapeDtypeStruct((N_FFT, 32, PAIRS), F32),
        compiler_params=pltpu.CompilerParams(vmem_limit_bytes=20 * 1024 * 1024),
        cost_estimate=pl.CostEstimate(flops=4_000_000_000, bytes_accessed=7_000_000, transcendentals=0),
        name="ml_waves",
    )(charges, slots, waves)


def guarded(value, pivot, scale):
    good = pivot > 1e-6 * scale
    return jnp.where(good, value / jnp.where(good, pivot, 1.0), 0.0)


def lookup(tables, atom):
    index = lax.broadcasted_iota(jnp.int32, (128, atom.shape[1]), 0)
    pick = jnp.where(index == (atom & 127), 1.0, 0.0).astype(BF16)
    rows = dot_nn(tables, jnp.concatenate([pick, pick], 0))
    here = index == (atom >> 7)
    count = rows.shape[0] // 128
    return [
        jnp.sum(jnp.where(here, rows[v * 128 : v * 128 + 128], 0.0), 0, keepdims=True) for v in range(count)
    ]


def early_body(slots, first, out, v0):
    for i in range(4):
        v0[pl.ds(i, N_FFT, stride=4), :] = slots[:, 8 + i * 8, :]
    both = jnp.concatenate([v0[...], first[...]], 0)
    high, low = split(both)
    both = jnp.concatenate([high, low], 1)
    for g in range(N_FFT):
        found = lookup(both, slot_rows(slots, g)[1:2].astype(jnp.int32))
        for v in range(2):
            for i in range(4):
                out[v, g * 4 + i : g * 4 + i + 1, :] = found[v][:, i * 128 : i * 128 + 128]


def early(slots, first):
    return pl.pallas_call(
        early_body,
        out_shape=jax.ShapeDtypeStruct((2, 128, 128), F32),
        scratch_shapes=[pltpu.VMEM((128, 128), F32)],
        compiler_params=pltpu.CompilerParams(vmem_limit_bytes=12 * 1024 * 1024),
        cost_estimate=pl.CostEstimate(flops=2_000_000_000, bytes_accessed=1_000_000, transcendentals=0),
        name="early",
    )(slots, first)


def moment_body(place, slots, before, first, grid, charges, rest, v2, late):
    f, s = place[0], place[1]
    for i in range(4):
        pieces = [grid[:, i * 4 + j, 96:128] for j in range(4)]
        v2[pl.ds(i, N_FFT, stride=4), :] = jnp.concatenate(pieces, 1)
    high, low = split(v2[...])
    both = jnp.concatenate([high, low], 1)
    for g in range(N_FFT):
        found = lookup(both, slot_rows(slots, g)[1:2].astype(jnp.int32))[0]
        for i in range(4):
            late[g * 4 + i : g * 4 + i + 1, :] = found[:, i * 128 : i * 128 + 128]

    def dot(a, b):
        return jnp.sum(jnp.sum(a * b, 0, keepdims=True), 1, keepdims=True)

    a, b, c = before[0], before[1], late[...]
    m0, m1, m2, m3, m4 = dot(a, a), dot(a, b), dot(b, b), dot(b, c), dot(c, c)
    l10 = m2 / m1
    l20 = m3 / m1
    d1 = m3 - l10 * m2
    e12 = m4 - l10 * m3
    l21 = guarded(e12, d1, m3)
    g1 = m1 - l10 * m0
    g2 = (m2 - l20 * m0) - l21 * g1
    c1 = guarded(g1, d1, m3)
    c0 = m0 / m1 - l10 * c1
    charges[0] = c0 * a + c1 * b
    charges[1] = c - l21 * b + (l10 * l21 - l20) * a
    at = f * 4 + (s >> 2)
    rest[...] = jnp.zeros_like(rest)
    own = [slots[pl.ds(f, 1), 8 + i * 8, :] for i in range(4)]
    a = sum(jnp.where((s >> 2) == i, own[i], 0.0) for i in range(4))
    b, c = first[pl.ds(at, 1), :], v2[pl.ds(at, 1), :]
    rest[0:1] = c0 * a + c1 * b
    rest[1:2] = c - l21 * b + (l10 * l21 - l20) * a
    rest[...] = pltpu.roll(rest[...], ((4 - (s & 3)) & 3) * OWN, 1)
    rest[2:3] = jnp.broadcast_to(l20 * m3 + l21 * e12, (1, 128))
    rest[3:4] = jnp.broadcast_to(g2, (1, 128))


def moments(place, slots, before, first, grid):
    return pl.pallas_call(
        moment_body,
        grid=(1,),
        in_specs=[
            pl.BlockSpec(memory_space=pltpu.SMEM),
            pl.BlockSpec((N_FFT, 40, 128), lambda i: (0, 0, 0)),
            pl.BlockSpec((2, 128, 128), lambda i: (0, 0, 0)),
            pl.BlockSpec((128, 128), lambda i: (0, 0)),
            pl.BlockSpec((N_FFT, 16, 128), lambda i: (0, 0, 2)),
        ],
        out_specs=(
            pl.BlockSpec((2, 128, 128), lambda i: (0, 0, 0)),
            pl.BlockSpec((8, 128), lambda i: (0, 0)),
        ),
        out_shape=(
            jax.ShapeDtypeStruct((2, 128, 128), F32),
            jax.ShapeDtypeStruct((8, 128), F32),
        ),
        scratch_shapes=[pltpu.VMEM((128, 128), F32), pltpu.VMEM((128, 128), F32)],
        compiler_params=pltpu.CompilerParams(vmem_limit_bytes=12 * 1024 * 1024),
        cost_estimate=pl.CostEstimate(flops=1_000_000_000, bytes_accessed=1_000_000, transcendentals=0),
        name="moments",
    )(place, slots, before, first, grid)


def z_body(grid, ml, quads, rest, perm, ch, cl, sh, sl, out_re, out_im, out_q):
    m5 = jnp.sum(quads[:, 0, :], 0, keepdims=True)
    step = guarded(rest[3:4], m5 - rest[2:3], m5)[:, 0:1]
    high, low = split(grid[...].reshape(N_FFT * 16, 384))
    total = dot_nn(high, perm[...]) + dot_nn(low, perm[...])
    extra = ml[:, 0:16] + step[None] * ml[:, 16:32]
    both = split(total + extra.reshape(N_FFT * 16, PAIRS))
    cos = three(dot_tn, both, (ch[...], cl[...]))
    sin = three(dot_tn, both, (sh[...], sl[...]))
    for k in range(KY):
        for first, count, re in ((0, 8, k * 8), (8, 4, 192 + k * 4)):
            im = re + KY * count
            out_re[k, first : first + count] = cos[re : re + count] + sin[im : im + count]
            out_im[k, first : first + count] = cos[im : im + count] - sin[re : re + count]
    out_q[...] = (rest[0:1] + step * rest[1:2])[:, 0:OWN]


def along_z(*operands):
    shape = jax.ShapeDtypeStruct((KY, KX, NG), F32)
    return pl.pallas_call(
        z_body,
        out_shape=(shape, shape, jax.ShapeDtypeStruct((1, OWN), F32)),
        compiler_params=pltpu.CompilerParams(vmem_limit_bytes=20 * 1024 * 1024),
        cost_estimate=pl.CostEstimate(flops=3_000_000_000, bytes_accessed=5_000_000, transcendentals=0),
        name="along_z",
    )(*operands)


def swap(value, axis):
    return lax.all_to_all(value, axis, 0, 0, tiled=True)


def on_device(
    ml_pos,
    ml_width,
    ml_drive,
    ml_hard,
    mm_charge,
    mm_frac,
    mm_cell,
    slot_atom,
    slot_frac,
    slot_cell,
):
    f = lax.axis_index("fft")
    s = lax.axis_index("slab")
    place = jnp.stack([f, s]).astype(jnp.int32)

    got = swap(pack(ml_drive, slot_atom, slot_cell, slot_frac), "slab")
    matrix = couple(place, ml_pos, ml_width, ml_hard)
    got_1 = swap(first_product(got, matrix), "fft")
    xh, xl = (jnp.asarray(t) for t in two_parts(x_table()))
    mm = spread(mm_charge, mm_frac, mm_cell, xh, xl)
    first_cols = jnp.sum(got_1[:, :8], 0)
    part = jnp.sum(matrix * first_cols.reshape(1, COLS), 1)
    tail = jnp.concatenate([part.reshape(4, 128), first_cols[:4], first_cols[4:]], 1)
    tail = jnp.broadcast_to(tail[None], (N_SLAB, 4, 384))
    got_2 = swap(jnp.concatenate([mm[:, : YE - 4], tail], 1), "slab")
    first_full = jnp.concatenate([got_2[:, YE - 4 :, 128:256], got_2[:, YE - 4 :, 256:]], 1)
    first_full = jnp.transpose(first_full.reshape(N_SLAB, N_FFT, OWN), (1, 0, 2)).reshape(128, 128)

    arh, arl, aih, ail = (jnp.asarray(t) for half in y_tables() for t in two_parts(half))
    got_3 = swap(along_y(got_2, matrix, jnp.asarray(perm_y()), arh, arl, aih, ail), "fft")
    quads = swap(quad_sum(place, got_3), "slab")

    steps = jnp.concatenate(
        [
            lax.dynamic_index_in_dim(jnp.asarray(step_table(N_SLAB)), s, 0, False),
            lax.dynamic_index_in_dim(jnp.asarray(step_table(N_FFT)), f, 0, False),
        ],
        1,
    )
    waves = tables(place, got_1, steps)
    charges, rest = moments(place, got_1, early(got_1, first_full), first_full, got_3)
    ml = ml_waves(charges, got_1, waves)
    ch, cl, sh, sl = (jnp.asarray(t) for half in z_tables() for t in two_parts(half))
    struct_re, struct_im, charge = along_z(got_3, ml, quads, rest, jnp.asarray(perm_z()), ch, cl, sh, sl)
    return (charge.reshape(OWN), struct_re, struct_im)


def solution(mesh):
    return jax.shard_map(
        on_device,
        mesh=mesh,
        in_specs=(
            P(),
            P(),
            P(("fft", "slab")),
            P(("fft", "slab")),
            P(("fft", "slab")),
            P(None, ("fft", "slab")),
            P(None, ("fft", "slab")),
            P(("fft", "slab")),
            P(None, ("fft", "slab")),
            P(None, ("fft", "slab")),
        ),
        out_specs=(P(("fft", "slab")), P("fft", "slab", None), P("fft", "slab", None)),
        check_vma=False,
    )
```

```python
import math

import jax
import jax.numpy as jnp
import numpy as np
from jax import lax
from jax.experimental import pallas as pl
from jax.experimental.pallas import tpu as pltpu
from jax.sharding import PartitionSpec as P

NG = 384
N_FFT = 32
N_SLAB = 16
YL = 24
ZL = 12
KX = 12
KY = 12
OWN = 32
ROWS = 512
COLS = 1024
ATOMS = 16384
SITES = 6144
CHUNK = 1024
XE = 392
YE = 32
ZE = 15
PAIRS = 288

KE = 14.4
ALPHA = 0.08
SOFT = 0.01
SQPI = math.sqrt(math.pi)
F32 = jnp.float32
BF16 = jnp.bfloat16
VMEM_LIMIT = 60 * 1024 * 1024


def wave(points, freqs):
    angle = 2.0 * np.pi * ((points[:, None] * freqs[None, :]) % NG) / NG
    return np.cos(angle), np.sin(angle)


def two_parts(table):
    high = np.asarray(table, np.float32).astype(jnp.bfloat16)
    low = (np.asarray(table, np.float64) - high.astype(np.float64)).astype(jnp.bfloat16)
    return high, low


def x_table():
    points = np.arange(XE)
    cos, sin = wave(points, np.arange(NG // 2))
    cos, sin = (t.reshape(XE, N_SLAB, 1, KX) for t in (cos, sin))
    table = np.concatenate([cos, -sin], 2)
    table = table * (points < NG + 3)[:, None, None, None]
    return table.reshape(XE, N_SLAB * 2 * KX)


def y_tables():
    local = np.arange(YE)
    points = (np.arange(N_SLAB)[:, None] * YL + local[None, :]).reshape(-1)
    used = np.tile(local < YL + 3, N_SLAB)[:, None, None, None]
    cos, sin = wave(points, np.arange(NG))
    cos, sin = (t.reshape(-1, N_FFT, 1, KY) for t in (cos, sin))
    from_re = np.concatenate([cos, -sin], 2) * used
    from_im = np.concatenate([sin, cos], 2) * used
    return from_re.reshape(-1, 2 * NG), from_im.reshape(-1, 2 * NG)


def z_tables():
    local = np.arange(16)
    points = (np.arange(N_FFT)[:, None] * ZL + local[None, :]).reshape(-1)
    used = np.tile(local < ZL + 3, N_FFT)[:, None]
    scale = 1.0 / (NG * math.sqrt(NG))
    cos, sin = wave(points, np.arange(NG))
    return cos * used * scale, sin * used * scale


def perm_y():
    table = np.zeros((2, KX, 16, 384), np.float32)
    for c in range(2):
        for k in range(KX):
            for z in range(ZE):
                table[c, k, z, z * 24 + c * KX + k] = 1.0
    return table.reshape(384, 384).astype(jnp.bfloat16)


def perm_z():
    table = np.zeros((384, PAIRS), np.float32)
    for c in range(2):
        for k in range(KY):
            for x in range(KX):
                column = c * 96 + k * 8 + x if x < 8 else 192 + c * 48 + k * 4 + x - 8
                table[x * 24 + c * KY + k, column] = 1.0
    return table.astype(jnp.bfloat16)


def step_table(count):
    local = np.concatenate([np.arange(12), np.arange(8, 12)])
    freqs = (np.arange(count) * 12)[:, None] + local[None, :]
    angle = 2.0 * np.pi * freqs[:, :, None] * np.arange(4)[None, None, :] / NG
    return np.concatenate([np.cos(angle), -np.sin(angle)], 2).astype(np.float32)


def split(value):
    high = value.astype(BF16)
    return high, (value - high.astype(F32)).astype(BF16)


def dot_nn(a, b):
    return lax.dot_general(a, b, (((1,), (0,)), ((), ())), preferred_element_type=F32)


def dot_nt(a, b):
    return lax.dot_general(a, b, (((1,), (1,)), ((), ())), preferred_element_type=F32)


def dot_tn(a, b):
    return lax.dot_general(a, b, (((0,), (0,)), ((), ())), preferred_element_type=F32)


def three(dot, a, b):
    return dot(a[0], b[0]) + dot(a[0], b[1]) + dot(a[1], b[0])


def spline(u):
    squared = u * u
    cubed = squared * u
    rest = 1.0 - u
    return (
        rest * rest * rest / 6.0,
        (3.0 * cubed - 6.0 * squared + 4.0) / 6.0,
        (-3.0 * cubed + 3.0 * squared + 3.0 * u + 1.0) / 6.0,
        cubed / 6.0,
    )


def placed(rows, cell, weights):
    off = lax.broadcasted_iota(jnp.int32, (rows, cell.shape[1]), 0) - cell
    value = jnp.where(off == 3, weights[3], 0.0)
    value = jnp.where(off == 2, weights[2], value)
    value = jnp.where(off == 1, weights[1], value)
    return jnp.where(off == 0, weights[0], value)


def spread_body(charge, frac, cell, waves_from, out, acc, waves, sem):
    step = pl.program_id(0)
    copy = pltpu.make_async_copy(waves_from, waves, sem)

    @pl.when(step == 0)
    def _():
        copy.start()
        acc[...] = jnp.zeros_like(acc)

    along_x = placed(XE, cell[0:1, :], spline(frac[0:1, :]))
    along_y = placed(YE, cell[1:2, :], spline(frac[1:2, :])) * charge[...]
    along_z = placed(16, cell[2:3, :], spline(frac[2:3, :]))
    plane = jnp.concatenate([along_z[z : z + 1, :] * along_y for z in range(ZE)], 0)
    acc[...] += three(dot_nt, split(along_x), split(plane))

    @pl.when(step == pl.num_programs(0) - 1)
    def _():
        copy.wait()
        freq = three(dot_tn, split(acc[...]), (waves[0], waves[1]))
        for s in range(N_SLAB):
            for z in range(ZE):
                out[s, :, z * 24 : z * 24 + 24] = freq[z * YE : z * YE + YE, s * 24 : s * 24 + 24]
            out[s, :, ZE * 24 : 384] = jnp.zeros((YE, 384 - ZE * 24), F32)


def spread(charge, frac, cell, waves):
    return pl.pallas_call(
        spread_body,
        grid=(SITES // CHUNK,),
        in_specs=[
            pl.BlockSpec((1, CHUNK), lambda i: (0, i)),
            pl.BlockSpec((3, CHUNK), lambda i: (0, i)),
            pl.BlockSpec((3, CHUNK), lambda i: (0, i)),
            pl.BlockSpec(memory_space=pltpu.HBM),
        ],
        out_specs=pl.BlockSpec((N_SLAB, YE, 384), lambda i: (0, 0, 0)),
        out_shape=jax.ShapeDtypeStruct((N_SLAB, YE, 384), F32),
        scratch_shapes=[
            pltpu.VMEM((XE, ZE * YE), F32),
            pltpu.VMEM((2, XE, 384), BF16),
            pltpu.SemaphoreType.DMA,
        ],
        compiler_params=pltpu.CompilerParams(vmem_limit_bytes=VMEM_LIMIT),
        cost_estimate=pl.CostEstimate(flops=8_000_000_000, bytes_accessed=2_000_000, transcendentals=0),
        name="spread",
    )(charge.reshape(1, SITES), frac, cell, waves)


def lanes(tiles):
    return jnp.concatenate([tiles[i : i + 1] for i in range(tiles.shape[0])], 1)


def pack_body(drive, atom, cell, frac, out):
    out[...] = jnp.zeros_like(out)
    for i in range(N_SLAB):
        out[i, 0:1, 0:OWN] = -drive[...]
        out[i, 1:2, 0:OWN] = atom[...].astype(F32)
        out[i, 2:5, 0:OWN] = cell[...].astype(F32)
        out[i, 5:8, 0:OWN] = frac[...]


def pack(drive, atom, cell, frac):
    return pl.pallas_call(
        pack_body,
        out_shape=jax.ShapeDtypeStruct((N_SLAB, 8, 128), F32),
        compiler_params=pltpu.CompilerParams(vmem_limit_bytes=VMEM_LIMIT),
        name="pack",
    )(drive.reshape(1, OWN), atom.reshape(1, OWN), cell, frac)


def erf_ratio(value):
    square = value * value
    p = 0.00022905065861350646
    for c in (0.0034082910107109506, 0.050955695062380861, 0.18520832239976145, 1.128379143519084):
        p = p * square + c
    q = -1.1791602954361697e-7
    for c in (
        0.000023547966471313185,
        0.0010179625278914885,
        0.014070470171167667,
        0.11098505178285362,
        0.49746925110067538,
        1.0,
    ):
        q = q * square + c
    return value * p, q


def couple_body(place, pos, width, hard, out, picked, rows, own):
    f, s = place[0], place[1]
    lane = lax.broadcasted_iota(jnp.int32, (8, 128), 1) >> 5
    for j in range(N_FFT):
        at = pl.multiple_of(j * ROWS + (s >> 2) * 128, 128)
        picked[j, 0:3, :] = pos[:, pl.ds(at, 128)]
        picked[j, 3:4, :] = width[:, pl.ds(at, 128)]
    tiles = []
    for tile in range(COLS // 128):
        value = jnp.zeros((8, 128), F32)
        for j in range(4):
            value = jnp.where(lane == j, pltpu.roll(picked[tile * 4 + j], ((j - (s & 3)) & 3) * OWN, 1), value)
        tiles.append(value)
    cols = jnp.concatenate(tiles, 1)
    at = pl.multiple_of(f * ROWS, 128)
    rows[0:3, :] = pos[:, pl.ds(at, ROWS)]
    rows[3:4, :] = width[:, pl.ds(at, ROWS)]
    side = jnp.transpose(rows[...])
    own[...] = jnp.zeros_like(own)
    own[0:1, 0:OWN] = hard[...]
    own_hard = pltpu.roll(own[...], (f & 3) * OWN, 1)[0:1]
    diag = jnp.concatenate([jnp.where((f >> 2) == t, own_hard, 0.0) for t in range(COLS // 128)], 1)
    diag = diag + KE * (1.0 / (cols[3:4] * SQPI) - 2.0 * ALPHA / SQPI)
    col_id = lax.broadcasted_iota(jnp.int32, (1, COLS), 1) - f * OWN
    col_id = jnp.where((col_id >= 0) & (col_id < OWN), col_id + s * OWN, -1)
    col_sq = 2.0 * cols[3:4] * cols[3:4]
    step = 16
    for first in range(0, ROWS, step):
        here = side[first : first + step]
        square = SOFT
        for i in range(3):
            gap = here[:, i : i + 1] - cols[i : i + 1]
            square = square + gap * gap
        inverse = lax.rsqrt(square)
        distance = square * inverse
        narrow = lax.rsqrt(2.0 * here[:, 3:4] * here[:, 3:4] + col_sq)
        p1, q1 = erf_ratio(jnp.minimum(distance * narrow, 3.832506856900711))
        p2, q2 = erf_ratio(jnp.minimum(distance * ALPHA, 3.832506856900711))
        value = KE * inverse * ((p1 * q2 - p2 * q1) / (q1 * q2))
        row_id = first + lax.broadcasted_iota(jnp.int32, (step, 1), 0)
        out[first : first + step] = jnp.where(row_id == col_id, diag, value)


def couple(place, pos, width, hard):
    return pl.pallas_call(
        couple_body,
        in_specs=[pl.BlockSpec(memory_space=pltpu.SMEM)] + [pl.BlockSpec(memory_space=pltpu.VMEM)] * 3,
        out_shape=jax.ShapeDtypeStruct((ROWS, COLS), F32),
        scratch_shapes=[pltpu.VMEM((N_FFT, 8, 128), F32), pltpu.VMEM((8, ROWS), F32), pltpu.VMEM((8, 128), F32)],
        compiler_params=pltpu.CompilerParams(vmem_limit_bytes=VMEM_LIMIT),
        cost_estimate=pl.CostEstimate(flops=100_000_000, bytes_accessed=2_000_000, transcendentals=1_000_000),
        name="couple",
    )(place, pos, width.reshape(1, ATOMS), hard.reshape(1, OWN))


def first_body(got, matrix, out, slots):
    for s in range(N_SLAB):
        slots[:, s * OWN : s * OWN + OWN] = got[s, :, 0:OWN]
    every = slots[...]
    part = jnp.sum(matrix[...] * jnp.transpose(every)[:, 0:1], 0, keepdims=True)
    for i in range(8):
        out[0, i : i + 1, :] = part[:, i * 128 : i * 128 + 128]
    for i in range(4):
        out[0, 8 + i * 8 : 16 + i * 8, :] = every[:, i * 128 : i * 128 + 128]
    whole = out[0]
    for f in range(1, N_FFT):
        out[f] = whole


def first_product(got, matrix):
    return pl.pallas_call(
        first_body,
        out_shape=jax.ShapeDtypeStruct((N_FFT, 40, 128), F32),
        scratch_shapes=[pltpu.VMEM((8, ROWS), F32)],
        compiler_params=pltpu.CompilerParams(vmem_limit_bytes=VMEM_LIMIT),
        name="first_product",
    )(got, matrix)


def y_body(grid, matrix, perm, arh, arl, aih, ail, out, side):
    got = grid[...]
    rows = jnp.sum(got[:, YE - 4 :, 0:128], 0)
    side[0:4, :] = rows
    turned = jnp.transpose(side[...])
    column = jnp.concatenate([turned[:, i : i + 1] for i in range(4)], 0)
    part = jnp.sum(matrix[...] * column, 0, keepdims=True)
    high, low = split(got.reshape(N_SLAB * YE, 384))
    high = dot_nt(perm[...], high).astype(BF16)
    low = dot_nt(perm[...], low).astype(BF16)
    freq = three(dot_nn, (high[:192], low[:192]), (arh[...], arl[...]))
    freq = freq + three(dot_nn, (high[192:], low[192:]), (aih[...], ail[...]))
    for i in range(16):
        out[0, i : i + 1, 288:320] = part[:, i * OWN : i * OWN + OWN]
        out[0, i : i + 1, 320:352] = part[:, ROWS + i * OWN : ROWS + i * OWN + OWN]
        out[0, i : i + 1, 352:384] = rows[i // 4 : i // 4 + 1, i % 4 * OWN : i % 4 * OWN + OWN]
    extra = out[0, :, 256:384]
    for f in range(N_FFT):
        if f > 0:
            out[f, :, 256:384] = extra
        for k in range(KX):
            out[f, :, k * 24 : k * 24 + 24] = freq[k * 16 : k * 16 + 16, f * 24 : f * 24 + 24]


def along_y(*operands):
    return pl.pallas_call(
        y_body,
        out_shape=jax.ShapeDtypeStruct((N_FFT, 16, 384), F32),
        scratch_shapes=[pltpu.VMEM((8, 128), F32)],
        compiler_params=pltpu.CompilerParams(vmem_limit_bytes=VMEM_LIMIT),
        cost_estimate=pl.CostEstimate(flops=4_000_000_000, bytes_accessed=5_000_000, transcendentals=0),
        name="along_y",
    )(*operands)


def quad_body(place, got, out):
    s = place[1]
    third = jnp.sum(got[:, :, 32:96], 0)
    second = got[:, pl.ds(s, 1), 96:128].reshape(N_FFT, OWN)
    total = jnp.sum(third[:, 0:OWN] * second[0:16] + third[:, OWN:] * second[16:], 0, keepdims=True)
    total = jnp.sum(total, 1, keepdims=True)
    out[...] = jnp.broadcast_to(total[None], out.shape)


def quad_sum(place, got):
    return pl.pallas_call(
        quad_body,
        grid=(1,),
        in_specs=[
            pl.BlockSpec(memory_space=pltpu.SMEM),
            pl.BlockSpec((N_FFT, 16, 128), lambda i: (0, 0, 2)),
        ],
        out_specs=pl.BlockSpec((N_SLAB, 8, 128), lambda i: (0, 0, 0)),
        out_shape=jax.ShapeDtypeStruct((N_SLAB, 8, 128), F32),
        compiler_params=pltpu.CompilerParams(vmem_limit_bytes=VMEM_LIMIT),
        name="quad_sum",
    )(place, got)


def unit(turns):
    half = (turns - 0.5) * math.pi
    square = half * half
    sine = 0.0
    for power in (11, 9, 7, 5, 3):
        sine = (sine + (-1.0) ** (power // 2) / math.factorial(power)) * square
    sine = half * (1.0 + sine)
    cosine = 0.0
    for power in (12, 10, 8, 6, 4, 2):
        cosine = (cosine + (-1.0) ** (power // 2) / math.factorial(power)) * square
    cosine = 1.0 + cosine
    return 2.0 * sine * sine - 1.0, 2.0 * sine * cosine


def site_wave(first, base, fraction, steps):
    local = lax.broadcasted_iota(jnp.int32, (16, 1), 0)
    freq = first + jnp.where(local < 12, local, local - 4).astype(F32)
    phase = freq * base
    phase = phase - NG * jnp.floor(phase * (1.0 / NG))
    re, im = unit(phase * (1.0 / NG))
    weights = spline(fraction)
    w_re = sum(steps[:, i : i + 1] * weights[i] for i in range(4))
    w_im = sum(steps[:, 4 + i : 5 + i] * weights[i] for i in range(1, 4))
    return re * w_re - im * w_im, re * w_im + im * w_re


def slot_rows(slots, g):
    return jnp.concatenate([slots[g, 8 + i * 8 : 16 + i * 8, :] for i in range(4)], 1)


def table_body(place, slots, steps, out):
    block = (lax.broadcasted_iota(jnp.int32, (1, ROWS), 1) // OWN * YL).astype(F32)
    first_x, first_y = (place[1] * KX).astype(F32), (place[0] * KY).astype(F32)
    for g in range(8):
        rows = slot_rows(slots, g)
        x_re, x_im = site_wave(first_x, rows[2:3], rows[5:6], steps[:, 0:8])
        y_re, y_im = site_wave(first_y, rows[3:4] + block, rows[6:7], steps[:, 8:16])
        out[g, 0:16] = x_re
        out[g, 16:32] = x_im
        out[g, 32:48] = y_re
        out[g, 48:64] = y_im


def tables(place, slots, steps):
    return pl.pallas_call(
        table_body,
        grid=(4,),
        in_specs=[
            pl.BlockSpec(memory_space=pltpu.SMEM),
            pl.BlockSpec((8, 40, 128), lambda i: (i, 0, 0)),
            pl.BlockSpec((16, 16), lambda i: (0, 0)),
        ],
        out_specs=pl.BlockSpec((8, 64, ROWS), lambda i: (i, 0, 0)),
        out_shape=jax.ShapeDtypeStruct((N_FFT, 64, ROWS), F32),
        compiler_params=pltpu.CompilerParams(vmem_limit_bytes=VMEM_LIMIT),
        cost_estimate=pl.CostEstimate(flops=2_000_000_000, bytes_accessed=5_000_000, transcendentals=0),
        name="tables",
    )(place, slots, steps)


def ml_body(charges, slots, waves, out):
    upper = lax.broadcasted_iota(jnp.int32, (8, 1), 0) < 4
    for g in range(8):
        rows = slot_rows(slots, g)
        placed_z = placed(16, rows[4:5].astype(jnp.int32), spline(rows[7:8]))
        both = [placed_z * lanes(charges[v, g * 4 : g * 4 + 4, :]) for v in range(2)]
        z_high, z_low = split(jnp.concatenate(both, 0))
        x_re, x_im = waves[g, 0:8], waves[g, 16:24]
        parts_re, parts_im = [], []
        for k in range(KY):
            y_re, y_im = waves[g, 32 + k : 33 + k], waves[g, 48 + k : 49 + k]
            parts_re.append(y_re * x_re - y_im * x_im)
            parts_im.append(y_re * x_im + y_im * x_re)
        parts = parts_re + parts_im
        x_re, x_im = waves[g, 8:16], waves[g, 24:32]
        parts_re, parts_im = [], []
        for k in range(0, KY, 2):
            y_re = jnp.where(upper, waves[g, 32 + k : 33 + k], waves[g, 33 + k : 34 + k])
            y_im = jnp.where(upper, waves[g, 48 + k : 49 + k], waves[g, 49 + k : 50 + k])
            parts_re.append(y_re * x_re - y_im * x_im)
            parts_im.append(y_re * x_im + y_im * x_re)
        high, low = split(jnp.concatenate(parts + parts_re + parts_im, 0))
        total = dot_nt(jnp.concatenate([z_high, z_low], 0), high)
        out[g] = total[:32] + total[32:] + dot_nt(z_high, low)


def ml_waves(charges, slots, waves):
    return pl.pallas_call(
        ml_body,
        grid=(4,),
        in_specs=[
            pl.BlockSpec((2, 32, 128), lambda i: (0, i, 0)),
            pl.BlockSpec((8, 40, 128), lambda i: (i, 0, 0)),
            pl.BlockSpec((8, 64, ROWS), lambda i: (i, 0, 0)),
        ],
        out_specs=pl.BlockSpec((8, 32, PAIRS), lambda i: (i, 0, 0)),
        out_shape=jax.ShapeDtypeStruct((N_FFT, 32, PAIRS), F32),
        compiler_params=pltpu.CompilerParams(vmem_limit_bytes=VMEM_LIMIT),
        cost_estimate=pl.CostEstimate(flops=4_000_000_000, bytes_accessed=7_000_000, transcendentals=0),
        name="ml_waves",
    )(charges, slots, waves)


def guarded(value, pivot, scale):
    good = pivot > 1e-6 * scale
    return jnp.where(good, value / jnp.where(good, pivot, 1.0), 0.0)


def lookup(tables, atom):
    index = lax.broadcasted_iota(jnp.int32, (128, atom.shape[1]), 0)
    pick = jnp.where(index == (atom & 127), 1.0, 0.0).astype(BF16)
    rows = dot_nn(tables, jnp.concatenate([pick, pick], 0))
    here = index == (atom >> 7)
    count = rows.shape[0] // 128
    return [
        jnp.sum(jnp.where(here, rows[v * 128 : v * 128 + 128], 0.0), 0, keepdims=True) for v in range(count)
    ]


def early_body(slots, first, out, v0):
    for i in range(4):
        v0[pl.ds(i, N_FFT, stride=4), :] = slots[:, 8 + i * 8, :]
    both = jnp.concatenate([v0[...], first[...]], 0)
    high, low = split(both)
    both = jnp.concatenate([high, low], 1)
    for g in range(N_FFT):
        found = lookup(both, slot_rows(slots, g)[1:2].astype(jnp.int32))
        for v in range(2):
            for i in range(4):
                out[v, g * 4 + i : g * 4 + i + 1, :] = found[v][:, i * 128 : i * 128 + 128]


def early(slots, first):
    return pl.pallas_call(
        early_body,
        out_shape=jax.ShapeDtypeStruct((2, 128, 128), F32),
        scratch_shapes=[pltpu.VMEM((128, 128), F32)],
        compiler_params=pltpu.CompilerParams(vmem_limit_bytes=VMEM_LIMIT),
        cost_estimate=pl.CostEstimate(flops=2_000_000_000, bytes_accessed=1_000_000, transcendentals=0),
        name="early",
    )(slots, first)


def moment_body(place, slots, before, first, grid, charges, rest, v2, late):
    f, s = place[0], place[1]
    for i in range(4):
        pieces = [grid[:, i * 4 + j, 96:128] for j in range(4)]
        v2[pl.ds(i, N_FFT, stride=4), :] = jnp.concatenate(pieces, 1)
    high, low = split(v2[...])
    both = jnp.concatenate([high, low], 1)
    for g in range(N_FFT):
        found = lookup(both, slot_rows(slots, g)[1:2].astype(jnp.int32))[0]
        for i in range(4):
            late[g * 4 + i : g * 4 + i + 1, :] = found[:, i * 128 : i * 128 + 128]

    def dot(a, b):
        return jnp.sum(jnp.sum(a * b, 0, keepdims=True), 1, keepdims=True)

    a, b, c = before[0], before[1], late[...]
    m0, m1, m2, m3, m4 = dot(a, a), dot(a, b), dot(b, b), dot(b, c), dot(c, c)
    l10 = m2 / m1
    l20 = m3 / m1
    d1 = m3 - l10 * m2
    e12 = m4 - l10 * m3
    l21 = guarded(e12, d1, m3)
    g1 = m1 - l10 * m0
    g2 = (m2 - l20 * m0) - l21 * g1
    c1 = guarded(g1, d1, m3)
    c0 = m0 / m1 - l10 * c1
    charges[0] = c0 * a + c1 * b
    charges[1] = c - l21 * b + (l10 * l21 - l20) * a
    at = f * 4 + (s >> 2)
    rest[...] = jnp.zeros_like(rest)
    own = [slots[pl.ds(f, 1), 8 + i * 8, :] for i in range(4)]
    a = sum(jnp.where((s >> 2) == i, own[i], 0.0) for i in range(4))
    b, c = first[pl.ds(at, 1), :], v2[pl.ds(at, 1), :]
    rest[0:1] = c0 * a + c1 * b
    rest[1:2] = c - l21 * b + (l10 * l21 - l20) * a
    rest[...] = pltpu.roll(rest[...], ((4 - (s & 3)) & 3) * OWN, 1)
    rest[2:3] = jnp.broadcast_to(l20 * m3 + l21 * e12, (1, 128))
    rest[3:4] = jnp.broadcast_to(g2, (1, 128))


def moments(place, slots, before, first, grid):
    return pl.pallas_call(
        moment_body,
        grid=(1,),
        in_specs=[
            pl.BlockSpec(memory_space=pltpu.SMEM),
            pl.BlockSpec((N_FFT, 40, 128), lambda i: (0, 0, 0)),
            pl.BlockSpec((2, 128, 128), lambda i: (0, 0, 0)),
            pl.BlockSpec((128, 128), lambda i: (0, 0)),
            pl.BlockSpec((N_FFT, 16, 128), lambda i: (0, 0, 2)),
        ],
        out_specs=(
            pl.BlockSpec((2, 128, 128), lambda i: (0, 0, 0)),
            pl.BlockSpec((8, 128), lambda i: (0, 0)),
        ),
        out_shape=(
            jax.ShapeDtypeStruct((2, 128, 128), F32),
            jax.ShapeDtypeStruct((8, 128), F32),
        ),
        scratch_shapes=[pltpu.VMEM((128, 128), F32), pltpu.VMEM((128, 128), F32)],
        compiler_params=pltpu.CompilerParams(vmem_limit_bytes=VMEM_LIMIT),
        cost_estimate=pl.CostEstimate(flops=1_000_000_000, bytes_accessed=1_000_000, transcendentals=0),
        name="moments",
    )(place, slots, before, first, grid)


def z_body(grid, ml, quads, rest, perm_from, waves_from, out_re, out_im, out_q, perm, waves, sems):
    copies = [
        pltpu.make_async_copy(perm_from, perm, sems.at[0]),
        pltpu.make_async_copy(waves_from, waves, sems.at[1]),
    ]
    for copy in copies:
        copy.start()
    m5 = jnp.sum(quads[:, 0, :], 0, keepdims=True)
    step = guarded(rest[3:4], m5 - rest[2:3], m5)[:, 0:1]
    high, low = split(grid[...].reshape(N_FFT * 16, 384))
    extra = ml[:, 0:16] + step[None] * ml[:, 16:32]
    out_q[...] = (rest[0:1] + step * rest[1:2])[:, 0:OWN]
    copies[0].wait()
    total = dot_nn(high, perm[...]) + dot_nn(low, perm[...])
    both = split(total + extra.reshape(N_FFT * 16, PAIRS))
    copies[1].wait()
    cos = three(dot_tn, both, (waves[0], waves[1]))
    sin = three(dot_tn, both, (waves[2], waves[3]))
    for k in range(KY):
        for first, count, re in ((0, 8, k * 8), (8, 4, 192 + k * 4)):
            im = re + KY * count
            out_re[k, first : first + count] = cos[re : re + count] + sin[im : im + count]
            out_im[k, first : first + count] = cos[im : im + count] - sin[re : re + count]


def along_z(*operands):
    shape = jax.ShapeDtypeStruct((KY, KX, NG), F32)
    return pl.pallas_call(
        z_body,
        in_specs=[pl.BlockSpec(memory_space=pltpu.VMEM)] * 4 + [pl.BlockSpec(memory_space=pltpu.HBM)] * 2,
        out_shape=(shape, shape, jax.ShapeDtypeStruct((1, OWN), F32)),
        scratch_shapes=[
            pltpu.VMEM((384, PAIRS), BF16),
            pltpu.VMEM((4, N_FFT * 16, NG), BF16),
            pltpu.SemaphoreType.DMA((2,)),
        ],
        compiler_params=pltpu.CompilerParams(vmem_limit_bytes=VMEM_LIMIT),
        cost_estimate=pl.CostEstimate(flops=3_000_000_000, bytes_accessed=5_000_000, transcendentals=0),
        name="along_z",
    )(*operands)


def swap(value, axis):
    return lax.all_to_all(value, axis, 0, 0, tiled=True)


def on_device(
    ml_pos,
    ml_width,
    ml_drive,
    ml_hard,
    mm_charge,
    mm_frac,
    mm_cell,
    slot_atom,
    slot_frac,
    slot_cell,
):
    f = lax.axis_index("fft")
    s = lax.axis_index("slab")
    place = jnp.stack([f, s]).astype(jnp.int32)

    got = swap(pack(ml_drive, slot_atom, slot_cell, slot_frac), "slab")
    matrix = couple(place, ml_pos, ml_width, ml_hard)
    got_1 = swap(first_product(got, matrix), "fft")
    mm = spread(mm_charge, mm_frac, mm_cell, jnp.asarray(np.stack(two_parts(x_table()))))
    first_cols = jnp.sum(got_1[:, :8], 0)
    part = jnp.sum(matrix * first_cols.reshape(1, COLS), 1)
    tail = jnp.concatenate([part.reshape(4, 128), first_cols[:4], first_cols[4:]], 1)
    tail = jnp.broadcast_to(tail[None], (N_SLAB, 4, 384))
    got_2 = swap(jnp.concatenate([mm[:, : YE - 4], tail], 1), "slab")
    first_full = jnp.concatenate([got_2[:, YE - 4 :, 128:256], got_2[:, YE - 4 :, 256:]], 1)
    first_full = jnp.transpose(first_full.reshape(N_SLAB, N_FFT, OWN), (1, 0, 2)).reshape(128, 128)

    arh, arl, aih, ail = (jnp.asarray(t) for half in y_tables() for t in two_parts(half))
    got_3 = swap(along_y(got_2, matrix, jnp.asarray(perm_y()), arh, arl, aih, ail), "fft")
    quads = swap(quad_sum(place, got_3), "slab")

    steps = jnp.concatenate(
        [
            lax.dynamic_index_in_dim(jnp.asarray(step_table(N_SLAB)), s, 0, False),
            lax.dynamic_index_in_dim(jnp.asarray(step_table(N_FFT)), f, 0, False),
        ],
        1,
    )
    waves = tables(place, got_1, steps)
    charges, rest = moments(place, got_1, early(got_1, first_full), first_full, got_3)
    ml = ml_waves(charges, got_1, waves)
    z_waves = jnp.asarray(np.stack([t for half in z_tables() for t in two_parts(half)]))
    struct_re, struct_im, charge = along_z(got_3, ml, quads, rest, jnp.asarray(perm_z()), z_waves)
    return (charge.reshape(OWN), struct_re, struct_im)


def solution(mesh):
    return jax.shard_map(
        on_device,
        mesh=mesh,
        in_specs=(
            P(),
            P(),
            P(("fft", "slab")),
            P(("fft", "slab")),
            P(("fft", "slab")),
            P(None, ("fft", "slab")),
            P(None, ("fft", "slab")),
            P(("fft", "slab")),
            P(None, ("fft", "slab")),
            P(None, ("fft", "slab")),
        ),
        out_specs=(P(("fft", "slab")), P("fft", "slab", None), P("fft", "slab", None)),
        check_vma=False,
    )
```

```python
import math

import jax
import jax.numpy as jnp
import numpy as np
from jax import lax
from jax.experimental import pallas as pl
from jax.experimental.pallas import tpu as pltpu
from jax.sharding import PartitionSpec as P

NG = 384
N_FFT = 32
N_SLAB = 16
YL = 24
ZL = 12
KX = 12
KY = 12
OWN = 32
ROWS = 512
COLS = 1024
ATOMS = 16384
SITES = 6144
CHUNK = 1024
XE = 392
YE = 32
ZE = 15
PAIRS = 288

KE = 14.4
ALPHA = 0.08
SOFT = 0.01
SQPI = math.sqrt(math.pi)
F32 = jnp.float32
BF16 = jnp.bfloat16
MOST = 60 * 1024 * 1024
SOME = 12 * 1024 * 1024


def wave(points, freqs):
    angle = 2.0 * np.pi * ((points[:, None] * freqs[None, :]) % NG) / NG
    return np.cos(angle), np.sin(angle)


def two_parts(table):
    high = np.asarray(table, np.float32).astype(jnp.bfloat16)
    low = (np.asarray(table, np.float64) - high.astype(np.float64)).astype(jnp.bfloat16)
    return high, low


def x_table():
    points = np.arange(XE)
    cos, sin = wave(points, np.arange(NG // 2))
    cos, sin = (t.reshape(XE, N_SLAB, 1, KX) for t in (cos, sin))
    table = np.concatenate([cos, -sin], 2)
    table = table * (points < NG + 3)[:, None, None, None]
    return table.reshape(XE, N_SLAB * 2 * KX)


def y_tables():
    local = np.arange(YE)
    points = (np.arange(N_SLAB)[:, None] * YL + local[None, :]).reshape(-1)
    used = np.tile(local < YL + 3, N_SLAB)[:, None, None, None]
    cos, sin = wave(points, np.arange(NG))
    cos, sin = (t.reshape(-1, N_FFT, 1, KY) for t in (cos, sin))
    from_re = np.concatenate([cos, -sin], 2) * used
    from_im = np.concatenate([sin, cos], 2) * used
    return from_re.reshape(-1, 2 * NG), from_im.reshape(-1, 2 * NG)


def z_tables():
    local = np.arange(16)
    points = (np.arange(N_FFT)[:, None] * ZL + local[None, :]).reshape(-1)
    used = np.tile(local < ZL + 3, N_FFT)[:, None]
    scale = 1.0 / (NG * math.sqrt(NG))
    cos, sin = wave(points, np.arange(NG))
    return cos * used * scale, sin * used * scale


def perm_y():
    table = np.zeros((2, KX, 16, 384), np.float32)
    for c in range(2):
        for k in range(KX):
            for z in range(ZE):
                table[c, k, z, z * 24 + c * KX + k] = 1.0
    return table.reshape(384, 384).astype(jnp.bfloat16)


def perm_z():
    table = np.zeros((384, PAIRS), np.float32)
    for c in range(2):
        for k in range(KY):
            for x in range(KX):
                column = c * 96 + k * 8 + x if x < 8 else 192 + c * 48 + k * 4 + x - 8
                table[x * 24 + c * KY + k, column] = 1.0
    return table.astype(jnp.bfloat16)


def step_table(count):
    local = np.concatenate([np.arange(12), np.arange(8, 12)])
    freqs = (np.arange(count) * 12)[:, None] + local[None, :]
    angle = 2.0 * np.pi * freqs[:, :, None] * np.arange(4)[None, None, :] / NG
    return np.concatenate([np.cos(angle), -np.sin(angle)], 2).astype(np.float32)


def split(value):
    high = value.astype(BF16)
    return high, (value - high.astype(F32)).astype(BF16)


def dot_nn(a, b):
    return lax.dot_general(a, b, (((1,), (0,)), ((), ())), preferred_element_type=F32)


def dot_nt(a, b):
    return lax.dot_general(a, b, (((1,), (1,)), ((), ())), preferred_element_type=F32)


def dot_tn(a, b):
    return lax.dot_general(a, b, (((0,), (0,)), ((), ())), preferred_element_type=F32)


def three(dot, a, b):
    return dot(a[0], b[0]) + dot(a[0], b[1]) + dot(a[1], b[0])


def spline(u):
    squared = u * u
    cubed = squared * u
    rest = 1.0 - u
    return (
        rest * rest * rest / 6.0,
        (3.0 * cubed - 6.0 * squared + 4.0) / 6.0,
        (-3.0 * cubed + 3.0 * squared + 3.0 * u + 1.0) / 6.0,
        cubed / 6.0,
    )


def placed(rows, cell, weights):
    off = lax.broadcasted_iota(jnp.int32, (rows, cell.shape[1]), 0) - cell
    value = jnp.where(off == 3, weights[3], 0.0)
    value = jnp.where(off == 2, weights[2], value)
    value = jnp.where(off == 1, weights[1], value)
    return jnp.where(off == 0, weights[0], value)


def spread_body(charge, frac, cell, waves_from, out, acc, waves, sem):
    step = pl.program_id(0)
    copy = pltpu.make_async_copy(waves_from, waves, sem)

    @pl.when(step == 0)
    def _():
        copy.start()
        acc[...] = jnp.zeros_like(acc)

    along_x = placed(XE, cell[0:1, :], spline(frac[0:1, :]))
    along_y = placed(YE, cell[1:2, :], spline(frac[1:2, :])) * charge[...]
    along_z = placed(16, cell[2:3, :], spline(frac[2:3, :]))
    plane = jnp.concatenate([along_z[z : z + 1, :] * along_y for z in range(ZE)], 0)
    acc[...] += three(dot_nt, split(along_x), split(plane))

    @pl.when(step == pl.num_programs(0) - 1)
    def _():
        copy.wait()
        freq = three(dot_tn, split(acc[...]), (waves[0], waves[1]))
        for s in range(N_SLAB):
            for z in range(ZE):
                out[s, :, z * 24 : z * 24 + 24] = freq[z * YE : z * YE + YE, s * 24 : s * 24 + 24]
            out[s, :, ZE * 24 : 384] = jnp.zeros((YE, 384 - ZE * 24), F32)


def spread(charge, frac, cell, waves):
    return pl.pallas_call(
        spread_body,
        grid=(SITES // CHUNK,),
        in_specs=[
            pl.BlockSpec((1, CHUNK), lambda i: (0, i)),
            pl.BlockSpec((3, CHUNK), lambda i: (0, i)),
            pl.BlockSpec((3, CHUNK), lambda i: (0, i)),
            pl.BlockSpec(memory_space=pltpu.HBM),
        ],
        out_specs=pl.BlockSpec((N_SLAB, YE, 384), lambda i: (0, 0, 0)),
        out_shape=jax.ShapeDtypeStruct((N_SLAB, YE, 384), F32),
        scratch_shapes=[
            pltpu.VMEM((XE, ZE * YE), F32),
            pltpu.VMEM((2, XE, 384), BF16),
            pltpu.SemaphoreType.DMA,
        ],
        compiler_params=pltpu.CompilerParams(vmem_limit_bytes=MOST),
        cost_estimate=pl.CostEstimate(flops=8_000_000_000, bytes_accessed=2_000_000, transcendentals=0),
        name="spread",
    )(charge.reshape(1, SITES), frac, cell, waves)


def lanes(tiles):
    return jnp.concatenate([tiles[i : i + 1] for i in range(tiles.shape[0])], 1)


def pack_body(place, drive, atom, cell, frac, hard, pos, width, out, cols, rows, picked):
    f, s = place[0], place[1]
    out[...] = jnp.zeros_like(out)
    for i in range(N_SLAB):
        out[i, 0:1, 0:OWN] = -drive[...]
        out[i, 1:2, 0:OWN] = atom[...].astype(F32)
        out[i, 2:5, 0:OWN] = cell[...].astype(F32)
        out[i, 5:8, 0:OWN] = frac[...]
    for j in range(N_FFT):
        at = pl.multiple_of(j * ROWS + (s >> 2) * 128, 128)
        picked[j, 0:3, :] = pos[:, pl.ds(at, 128)]
        picked[j, 3:4, :] = width[:, pl.ds(at, 128)]
    lane = lax.broadcasted_iota(jnp.int32, (8, 128), 1) >> 5
    for tile in range(COLS // 128):
        value = jnp.zeros((8, 128), F32)
        for j in range(4):
            value = jnp.where(lane == j, pltpu.roll(picked[tile * 4 + j], ((j - (s & 3)) & 3) * OWN, 1), value)
        cols[:, tile * 128 : tile * 128 + 128] = value
    at = pl.multiple_of(f * ROWS, 128)
    rows[...] = jnp.zeros_like(rows)
    rows[0:3, :] = pos[:, pl.ds(at, ROWS)]
    rows[3:4, :] = width[:, pl.ds(at, ROWS)]
    rows[4:5, 0:OWN] = hard[...]


def pack(place, drive, atom, cell, frac, hard, pos, width):
    return pl.pallas_call(
        pack_body,
        in_specs=[pl.BlockSpec(memory_space=pltpu.SMEM)] + [pl.BlockSpec(memory_space=pltpu.VMEM)] * 7,
        out_shape=(
            jax.ShapeDtypeStruct((N_SLAB, 8, 128), F32),
            jax.ShapeDtypeStruct((8, COLS), F32),
            jax.ShapeDtypeStruct((8, ROWS), F32),
        ),
        scratch_shapes=[pltpu.VMEM((N_FFT, 8, 128), F32)],
        compiler_params=pltpu.CompilerParams(vmem_limit_bytes=MOST),
        name="pack",
    )(
        place,
        drive.reshape(1, OWN),
        atom.reshape(1, OWN),
        cell,
        frac,
        hard.reshape(1, OWN),
        pos,
        width.reshape(1, ATOMS),
    )


def erf_ratio(value):
    square = value * value
    p = 0.00022905065861350646
    for c in (0.0034082910107109506, 0.050955695062380861, 0.18520832239976145, 1.128379143519084):
        p = p * square + c
    q = -1.1791602954361697e-7
    for c in (
        0.000023547966471313185,
        0.0010179625278914885,
        0.014070470171167667,
        0.11098505178285362,
        0.49746925110067538,
        1.0,
    ):
        q = q * square + c
    return value * p, q


def couple_body(place, cols_ref, rows, out, own):
    f, s = place[0], place[1]
    cols = cols_ref[...]
    side = jnp.transpose(rows[...])
    own[...] = jnp.zeros_like(own)
    own[0:1, 0:OWN] = rows[4:5, 0:OWN]
    own_hard = pltpu.roll(own[...], (f & 3) * OWN, 1)[0:1]
    diag = jnp.concatenate([jnp.where((f >> 2) == t, own_hard, 0.0) for t in range(COLS // 128)], 1)
    diag = diag + KE * (1.0 / (cols[3:4] * SQPI) - 2.0 * ALPHA / SQPI)
    col_id = lax.broadcasted_iota(jnp.int32, (1, COLS), 1) - f * OWN
    col_id = jnp.where((col_id >= 0) & (col_id < OWN), col_id + s * OWN, -1)
    col_sq = 2.0 * cols[3:4] * cols[3:4]
    step = 16
    for first in range(0, ROWS, step):
        here = side[first : first + step]
        square = SOFT
        for i in range(3):
            gap = here[:, i : i + 1] - cols[i : i + 1]
            square = square + gap * gap
        inverse = lax.rsqrt(square)
        distance = square * inverse
        narrow = lax.rsqrt(2.0 * here[:, 3:4] * here[:, 3:4] + col_sq)
        p1, q1 = erf_ratio(jnp.minimum(distance * narrow, 3.832506856900711))
        p2, q2 = erf_ratio(jnp.minimum(distance * ALPHA, 3.832506856900711))
        value = KE * inverse * ((p1 * q2 - p2 * q1) / (q1 * q2))
        row_id = first + lax.broadcasted_iota(jnp.int32, (step, 1), 0)
        out[first : first + step] = jnp.where(row_id == col_id, diag, value)


def couple(place, cols, rows):
    return pl.pallas_call(
        couple_body,
        in_specs=[pl.BlockSpec(memory_space=pltpu.SMEM)] + [pl.BlockSpec(memory_space=pltpu.VMEM)] * 2,
        out_shape=jax.ShapeDtypeStruct((ROWS, COLS), F32),
        scratch_shapes=[pltpu.VMEM((8, 128), F32)],
        compiler_params=pltpu.CompilerParams(vmem_limit_bytes=SOME),
        cost_estimate=pl.CostEstimate(flops=100_000_000, bytes_accessed=2_000_000, transcendentals=1_000_000),
        name="couple",
    )(place, cols, rows)


def first_body(got, matrix, out, slots):
    for s in range(N_SLAB):
        slots[:, s * OWN : s * OWN + OWN] = got[s, :, 0:OWN]
    every = slots[...]
    part = jnp.sum(matrix[...] * jnp.transpose(every)[:, 0:1], 0, keepdims=True)
    for i in range(8):
        out[0, i : i + 1, :] = part[:, i * 128 : i * 128 + 128]
    for i in range(4):
        out[0, 8 + i * 8 : 16 + i * 8, :] = every[:, i * 128 : i * 128 + 128]
    whole = out[0]
    for f in range(1, N_FFT):
        out[f] = whole


def first_product(got, matrix):
    return pl.pallas_call(
        first_body,
        out_shape=jax.ShapeDtypeStruct((N_FFT, 40, 128), F32),
        scratch_shapes=[pltpu.VMEM((8, ROWS), F32)],
        compiler_params=pltpu.CompilerParams(vmem_limit_bytes=SOME),
        name="first_product",
    )(got, matrix)


def y_body(grid, matrix, perm, arh, arl, aih, ail, out, side):
    got = grid[...]
    rows = jnp.sum(got[:, YE - 4 :, 0:128], 0)
    side[0:4, :] = rows
    turned = jnp.transpose(side[...])
    column = jnp.concatenate([turned[:, i : i + 1] for i in range(4)], 0)
    part = jnp.sum(matrix[...] * column, 0, keepdims=True)
    high, low = split(got.reshape(N_SLAB * YE, 384))
    high = dot_nt(perm[...], high).astype(BF16)
    low = dot_nt(perm[...], low).astype(BF16)
    freq = three(dot_nn, (high[:192], low[:192]), (arh[...], arl[...]))
    freq = freq + three(dot_nn, (high[192:], low[192:]), (aih[...], ail[...]))
    for i in range(16):
        out[0, i : i + 1, 288:320] = part[:, i * OWN : i * OWN + OWN]
        out[0, i : i + 1, 320:352] = part[:, ROWS + i * OWN : ROWS + i * OWN + OWN]
        out[0, i : i + 1, 352:384] = rows[i // 4 : i // 4 + 1, i % 4 * OWN : i % 4 * OWN + OWN]
    extra = out[0, :, 256:384]
    for f in range(N_FFT):
        if f > 0:
            out[f, :, 256:384] = extra
        for k in range(KX):
            out[f, :, k * 24 : k * 24 + 24] = freq[k * 16 : k * 16 + 16, f * 24 : f * 24 + 24]


def along_y(*operands):
    return pl.pallas_call(
        y_body,
        out_shape=jax.ShapeDtypeStruct((N_FFT, 16, 384), F32),
        scratch_shapes=[pltpu.VMEM((8, 128), F32)],
        compiler_params=pltpu.CompilerParams(vmem_limit_bytes=2 * SOME),
        cost_estimate=pl.CostEstimate(flops=4_000_000_000, bytes_accessed=5_000_000, transcendentals=0),
        name="along_y",
    )(*operands)


def quad_body(place, got, out):
    s = place[1]
    third = jnp.sum(got[:, :, 32:96], 0)
    second = got[:, pl.ds(s, 1), 96:128].reshape(N_FFT, OWN)
    total = jnp.sum(third[:, 0:OWN] * second[0:16] + third[:, OWN:] * second[16:], 0, keepdims=True)
    total = jnp.sum(total, 1, keepdims=True)
    out[...] = jnp.broadcast_to(total[None], out.shape)


def quad_sum(place, got):
    return pl.pallas_call(
        quad_body,
        grid=(1,),
        in_specs=[
            pl.BlockSpec(memory_space=pltpu.SMEM),
            pl.BlockSpec((N_FFT, 16, 128), lambda i: (0, 0, 2)),
        ],
        out_specs=pl.BlockSpec((N_SLAB, 8, 128), lambda i: (0, 0, 0)),
        out_shape=jax.ShapeDtypeStruct((N_SLAB, 8, 128), F32),
        compiler_params=pltpu.CompilerParams(vmem_limit_bytes=SOME),
        name="quad_sum",
    )(place, got)


def unit(turns):
    half = (turns - 0.5) * math.pi
    square = half * half
    sine = 0.0
    for power in (11, 9, 7, 5, 3):
        sine = (sine + (-1.0) ** (power // 2) / math.factorial(power)) * square
    sine = half * (1.0 + sine)
    cosine = 0.0
    for power in (12, 10, 8, 6, 4, 2):
        cosine = (cosine + (-1.0) ** (power // 2) / math.factorial(power)) * square
    cosine = 1.0 + cosine
    return 2.0 * sine * sine - 1.0, 2.0 * sine * cosine


def site_wave(first, base, fraction, steps):
    local = lax.broadcasted_iota(jnp.int32, (16, 1), 0)
    freq = first + jnp.where(local < 12, local, local - 4).astype(F32)
    phase = freq * base
    phase = phase - NG * jnp.floor(phase * (1.0 / NG))
    re, im = unit(phase * (1.0 / NG))
    weights = spline(fraction)
    w_re = sum(steps[:, i : i + 1] * weights[i] for i in range(4))
    w_im = sum(steps[:, 4 + i : 5 + i] * weights[i] for i in range(1, 4))
    return re * w_re - im * w_im, re * w_im + im * w_re


def slot_rows(slots, g):
    return jnp.concatenate([slots[g, 8 + i * 8 : 16 + i * 8, :] for i in range(4)], 1)


def table_body(place, slots, steps, out):
    block = (lax.broadcasted_iota(jnp.int32, (1, ROWS), 1) // OWN * YL).astype(F32)
    first_x, first_y = (place[1] * KX).astype(F32), (place[0] * KY).astype(F32)
    for g in range(8):
        rows = slot_rows(slots, g)
        x_re, x_im = site_wave(first_x, rows[2:3], rows[5:6], steps[:, 0:8])
        y_re, y_im = site_wave(first_y, rows[3:4] + block, rows[6:7], steps[:, 8:16])
        out[g, 0:16] = x_re
        out[g, 16:32] = x_im
        out[g, 32:48] = y_re
        out[g, 48:64] = y_im


def tables(place, slots, steps):
    return pl.pallas_call(
        table_body,
        grid=(4,),
        in_specs=[
            pl.BlockSpec(memory_space=pltpu.SMEM),
            pl.BlockSpec((8, 40, 128), lambda i: (i, 0, 0)),
            pl.BlockSpec((16, 16), lambda i: (0, 0)),
        ],
        out_specs=pl.BlockSpec((8, 64, ROWS), lambda i: (i, 0, 0)),
        out_shape=jax.ShapeDtypeStruct((N_FFT, 64, ROWS), F32),
        compiler_params=pltpu.CompilerParams(vmem_limit_bytes=SOME),
        cost_estimate=pl.CostEstimate(flops=2_000_000_000, bytes_accessed=5_000_000, transcendentals=0),
        name="tables",
    )(place, slots, steps)


def guarded(value, pivot, scale):
    good = pivot > 1e-6 * scale
    return jnp.where(good, value / jnp.where(good, pivot, 1.0), 0.0)


def lookup(tables, atom):
    index = lax.broadcasted_iota(jnp.int32, (128, atom.shape[1]), 0)
    pick = jnp.where(index == (atom & 127), 1.0, 0.0).astype(BF16)
    rows = dot_nn(tables, jnp.concatenate([pick, pick], 0))
    here = index == (atom >> 7)
    count = rows.shape[0] // 128
    return [
        jnp.sum(jnp.where(here, rows[v * 128 : v * 128 + 128], 0.0), 0, keepdims=True) for v in range(count)
    ]


def early_body(slots, first, out, v0):
    for i in range(4):
        v0[pl.ds(i, N_FFT, stride=4), :] = slots[:, 8 + i * 8, :]
    both = jnp.concatenate([v0[...], first[...]], 0)
    high, low = split(both)
    both = jnp.concatenate([high, low], 1)
    for g in range(N_FFT):
        found = lookup(both, slot_rows(slots, g)[1:2].astype(jnp.int32))
        for v in range(2):
            for i in range(4):
                out[v, g * 4 + i : g * 4 + i + 1, :] = found[v][:, i * 128 : i * 128 + 128]


def early(slots, first):
    return pl.pallas_call(
        early_body,
        out_shape=jax.ShapeDtypeStruct((2, 128, 128), F32),
        scratch_shapes=[pltpu.VMEM((128, 128), F32)],
        compiler_params=pltpu.CompilerParams(vmem_limit_bytes=SOME),
        cost_estimate=pl.CostEstimate(flops=2_000_000_000, bytes_accessed=1_000_000, transcendentals=0),
        name="early",
    )(slots, first)


def late_body(place, slots, before, first, grid, perm, waves_from, out, rest, v2, late, charges, waves, sems):
    copies = [
        pltpu.make_async_copy(waves_from.at[pl.ds(i * 8, 8)], waves.at[pl.ds(i * 8, 8)], sems.at[i])
        for i in range(4)
    ]
    for copy in copies:
        copy.start()
    f, s = place[0], place[1]
    for i in range(4):
        pieces = [grid[:, i * 4 + j, 352:384] for j in range(4)]
        v2[pl.ds(i, N_FFT, stride=4), :] = jnp.concatenate(pieces, 1)
    high, low = split(v2[...])
    both = jnp.concatenate([high, low], 1)
    for g in range(N_FFT):
        found = lookup(both, slot_rows(slots, g)[1:2].astype(jnp.int32))[0]
        for i in range(4):
            late[g * 4 + i : g * 4 + i + 1, :] = found[:, i * 128 : i * 128 + 128]

    def dot(a, b):
        return jnp.sum(jnp.sum(a * b, 0, keepdims=True), 1, keepdims=True)

    a, b, c = before[0], before[1], late[...]
    m0, m1, m2, m3, m4 = dot(a, a), dot(a, b), dot(b, b), dot(b, c), dot(c, c)
    l10 = m2 / m1
    l20 = m3 / m1
    d1 = m3 - l10 * m2
    e12 = m4 - l10 * m3
    l21 = guarded(e12, d1, m3)
    g1 = m1 - l10 * m0
    g2 = (m2 - l20 * m0) - l21 * g1
    c1 = guarded(g1, d1, m3)
    c0 = m0 / m1 - l10 * c1
    charges[0] = c0 * a + c1 * b
    charges[1] = c - l21 * b + (l10 * l21 - l20) * a
    at = f * 4 + (s >> 2)
    rest[...] = jnp.zeros_like(rest)
    own = [slots[pl.ds(f, 1), 8 + i * 8, :] for i in range(4)]
    a = sum(jnp.where((s >> 2) == i, own[i], 0.0) for i in range(4))
    b, c = first[pl.ds(at, 1), :], v2[pl.ds(at, 1), :]
    rest[0:1] = c0 * a + c1 * b
    rest[1:2] = c - l21 * b + (l10 * l21 - l20) * a
    rest[...] = pltpu.roll(rest[...], ((4 - (s & 3)) & 3) * OWN, 1)
    rest[2:3] = jnp.broadcast_to(l20 * m3 + l21 * e12, (1, 128))
    rest[3:4] = jnp.broadcast_to(g2, (1, 128))

    upper = lax.broadcasted_iota(jnp.int32, (8, 1), 0) < 4

    def group(i, carry):
        at = pl.multiple_of(i * 16, 16)
        charge = [charges[v, pl.ds(at, 16), :] for v in range(2)]
        high, low = split(grid[pl.ds(i * 4, 4)].reshape(64, 384))
        base = (dot_nn(high, perm[...]) + dot_nn(low, perm[...])).reshape(4, 16, PAIRS)
        for j in range(4):
            g = i * 4 + j
            rows = slot_rows(slots, g)
            placed_z = placed(16, rows[4:5].astype(jnp.int32), spline(rows[7:8]))
            both = [placed_z * lanes(charge[v][j * 4 : j * 4 + 4]) for v in range(2)]
            z_high, z_low = split(jnp.concatenate(both, 0))
            x_re, x_im = waves[g, 0:8], waves[g, 16:24]
            parts_re, parts_im = [], []
            for k in range(KY):
                y_re, y_im = waves[g, 32 + k : 33 + k], waves[g, 48 + k : 49 + k]
                parts_re.append(y_re * x_re - y_im * x_im)
                parts_im.append(y_re * x_im + y_im * x_re)
            parts = parts_re + parts_im
            x_re, x_im = waves[g, 8:16], waves[g, 24:32]
            parts_re, parts_im = [], []
            for k in range(0, KY, 2):
                y_re = jnp.where(upper, waves[g, 32 + k : 33 + k], waves[g, 33 + k : 34 + k])
                y_im = jnp.where(upper, waves[g, 48 + k : 49 + k], waves[g, 49 + k : 50 + k])
                parts_re.append(y_re * x_re - y_im * x_im)
                parts_im.append(y_re * x_im + y_im * x_re)
            high, low = split(jnp.concatenate(parts + parts_re + parts_im, 0))
            total = dot_nt(jnp.concatenate([z_high, z_low], 0), high)
            total = total[:32] + total[32:] + dot_nt(z_high, low)
            out[g, 0:16] = total[:16] + base[j]
            out[g, 16:32] = total[16:]
        return carry

    for i in range(4):
        copies[i].wait()
        lax.fori_loop(i * 2, i * 2 + 2, group, 0)


def late_waves(*operands):
    return pl.pallas_call(
        late_body,
        in_specs=[pl.BlockSpec(memory_space=pltpu.SMEM)]
        + [pl.BlockSpec(memory_space=pltpu.VMEM)] * 5
        + [pl.BlockSpec(memory_space=pl.ANY)],
        out_shape=(
            jax.ShapeDtypeStruct((N_FFT, 32, PAIRS), F32),
            jax.ShapeDtypeStruct((8, 128), F32),
        ),
        scratch_shapes=[
            pltpu.VMEM((128, 128), F32),
            pltpu.VMEM((128, 128), F32),
            pltpu.VMEM((2, 128, 128), F32),
            pltpu.VMEM((N_FFT, 64, ROWS), F32),
            pltpu.SemaphoreType.DMA((4,)),
        ],
        compiler_params=pltpu.CompilerParams(vmem_limit_bytes=MOST),
        cost_estimate=pl.CostEstimate(flops=5_000_000_000, bytes_accessed=7_000_000, transcendentals=0),
        name="late_waves",
    )(*operands)


def z_body(ml, quads, rest, waves, out_re, out_im, out_q):
    m5 = jnp.sum(quads[:, 0, :], 0, keepdims=True)
    step = guarded(rest[3:4], m5 - rest[2:3], m5)[:, 0:1]
    total = ml[:, 0:16] + step[None] * ml[:, 16:32]
    both = split(total.reshape(N_FFT * 16, PAIRS))
    cos = three(dot_tn, both, (waves[0], waves[1]))
    sin = three(dot_tn, both, (waves[2], waves[3]))
    for k in range(KY):
        for first, count, re in ((0, 8, k * 8), (8, 4, 192 + k * 4)):
            im = re + KY * count
            out_re[k, first : first + count] = cos[re : re + count] + sin[im : im + count]
            out_im[k, first : first + count] = cos[im : im + count] - sin[re : re + count]
    out_q[...] = (rest[0:1] + step * rest[1:2])[:, 0:OWN]


def along_z(*operands):
    shape = jax.ShapeDtypeStruct((KY, KX, NG), F32)
    return pl.pallas_call(
        z_body,
        out_shape=(shape, shape, jax.ShapeDtypeStruct((1, OWN), F32)),
        compiler_params=pltpu.CompilerParams(vmem_limit_bytes=2 * SOME),
        cost_estimate=pl.CostEstimate(flops=3_000_000_000, bytes_accessed=5_000_000, transcendentals=0),
        name="along_z",
    )(*operands)


def swap(value, axis):
    return lax.all_to_all(value, axis, 0, 0, tiled=True)


def on_device(
    ml_pos,
    ml_width,
    ml_drive,
    ml_hard,
    mm_charge,
    mm_frac,
    mm_cell,
    slot_atom,
    slot_frac,
    slot_cell,
):
    f = lax.axis_index("fft")
    s = lax.axis_index("slab")
    place = jnp.stack([f, s]).astype(jnp.int32)

    sent, cols, rows = pack(place, ml_drive, slot_atom, slot_cell, slot_frac, ml_hard, ml_pos, ml_width)
    got = swap(sent, "slab")
    matrix = couple(place, cols, rows)
    got_1 = swap(first_product(got, matrix), "fft")
    mm = spread(mm_charge, mm_frac, mm_cell, jnp.asarray(np.stack(two_parts(x_table()))))
    first_cols = jnp.sum(got_1[:, :8], 0)
    part = jnp.sum(matrix * first_cols.reshape(1, COLS), 1)
    tail = jnp.concatenate([part.reshape(4, 128), first_cols[:4], first_cols[4:]], 1)
    tail = jnp.broadcast_to(tail[None], (N_SLAB, 4, 384))
    got_2 = swap(jnp.concatenate([mm[:, : YE - 4], tail], 1), "slab")
    first_full = jnp.concatenate([got_2[:, YE - 4 :, 128:256], got_2[:, YE - 4 :, 256:]], 1)
    first_full = jnp.transpose(first_full.reshape(N_SLAB, N_FFT, OWN), (1, 0, 2)).reshape(128, 128)

    arh, arl, aih, ail = (jnp.asarray(t) for half in y_tables() for t in two_parts(half))
    got_3 = swap(along_y(got_2, matrix, jnp.asarray(perm_y()), arh, arl, aih, ail), "fft")
    quads = swap(quad_sum(place, got_3), "slab")

    steps = jnp.concatenate(
        [
            lax.dynamic_index_in_dim(jnp.asarray(step_table(N_SLAB)), s, 0, False),
            lax.dynamic_index_in_dim(jnp.asarray(step_table(N_FFT)), f, 0, False),
        ],
        1,
    )
    waves = tables(place, got_1, steps)
    before = early(got_1, first_full)
    ml, rest = late_waves(place, got_1, before, first_full, got_3, jnp.asarray(perm_z()), waves)
    z_waves = jnp.asarray(np.stack([t for half in z_tables() for t in two_parts(half)]))
    struct_re, struct_im, charge = along_z(ml, quads, rest, z_waves)
    return (charge.reshape(OWN), struct_re, struct_im)


def solution(mesh):
    return jax.shard_map(
        on_device,
        mesh=mesh,
        in_specs=(
            P(),
            P(),
            P(("fft", "slab")),
            P(("fft", "slab")),
            P(("fft", "slab")),
            P(None, ("fft", "slab")),
            P(None, ("fft", "slab")),
            P(("fft", "slab")),
            P(None, ("fft", "slab")),
            P(None, ("fft", "slab")),
        ),
        out_specs=(P(("fft", "slab")), P("fft", "slab", None), P("fft", "slab", None)),
        check_vma=False,
    )
```

```python
import math

import jax
import jax.numpy as jnp
import numpy as np
from jax import lax
from jax.experimental import pallas as pl
from jax.experimental.pallas import tpu as pltpu
from jax.sharding import PartitionSpec as P

NG = 384
N_FFT = 32
N_SLAB = 16
YL = 24
ZL = 12
KX = 12
KY = 12
OWN = 32
ROWS = 512
COLS = 1024
ATOMS = 16384
SITES = 6144
CHUNK = 1024
XE = 392
YE = 32
ZE = 15
PAIRS = 288

KE = 14.4
ALPHA = 0.08
SOFT = 0.01
SQPI = math.sqrt(math.pi)
F32 = jnp.float32
BF16 = jnp.bfloat16
MOST = 60 * 1024 * 1024
SOME = 12 * 1024 * 1024
LATE = 61000000


def wave(points, freqs):
    angle = 2.0 * np.pi * ((points[:, None] * freqs[None, :]) % NG) / NG
    return np.cos(angle), np.sin(angle)


def two_parts(table):
    high = np.asarray(table, np.float32).astype(jnp.bfloat16)
    low = (np.asarray(table, np.float64) - high.astype(np.float64)).astype(jnp.bfloat16)
    return high, low


def x_table():
    points = np.arange(XE)
    cos, sin = wave(points, np.arange(NG // 2))
    cos, sin = (t.reshape(XE, N_SLAB, 1, KX) for t in (cos, sin))
    table = np.concatenate([cos, -sin], 2)
    table = table * (points < NG + 3)[:, None, None, None]
    return table.reshape(XE, N_SLAB * 2 * KX)


def y_tables():
    local = np.arange(YE)
    points = (np.arange(N_SLAB)[:, None] * YL + local[None, :]).reshape(-1)
    used = np.tile(local < YL + 3, N_SLAB)[:, None, None, None]
    cos, sin = wave(points, np.arange(NG))
    cos, sin = (t.reshape(-1, N_FFT, 1, KY) for t in (cos, sin))
    from_re = np.concatenate([cos, -sin], 2) * used
    from_im = np.concatenate([sin, cos], 2) * used
    return from_re.reshape(-1, 2 * NG), from_im.reshape(-1, 2 * NG)


def z_tables():
    local = np.arange(16)
    points = (np.arange(N_FFT)[:, None] * ZL + local[None, :]).reshape(-1)
    used = np.tile(local < ZL + 3, N_FFT)[:, None]
    scale = 1.0 / (NG * math.sqrt(NG))
    cos, sin = wave(points, np.arange(NG))
    return cos * used * scale, sin * used * scale


def perm_y():
    table = np.zeros((2, KX, 16, 384), np.float32)
    for c in range(2):
        for k in range(KX):
            for z in range(ZE):
                table[c, k, z, z * 24 + c * KX + k] = 1.0
    return table.reshape(384, 384).astype(jnp.bfloat16)


def perm_z():
    table = np.zeros((384, PAIRS), np.float32)
    for c in range(2):
        for k in range(KY):
            for x in range(KX):
                column = c * 96 + k * 8 + x if x < 8 else 192 + c * 48 + k * 4 + x - 8
                table[x * 24 + c * KY + k, column] = 1.0
    return table.astype(jnp.bfloat16)


def step_table(count):
    local = np.concatenate([np.arange(12), np.arange(8, 12)])
    freqs = (np.arange(count) * 12)[:, None] + local[None, :]
    angle = 2.0 * np.pi * freqs[:, :, None] * np.arange(4)[None, None, :] / NG
    return np.concatenate([np.cos(angle), -np.sin(angle)], 2).astype(np.float32)


def my_place():
    return lax.axis_index("fft"), lax.axis_index("slab")


def split(value):
    high = value.astype(BF16)
    return high, (value - high.astype(F32)).astype(BF16)


def dot_nn(a, b):
    return lax.dot_general(a, b, (((1,), (0,)), ((), ())), preferred_element_type=F32)


def dot_nt(a, b):
    return lax.dot_general(a, b, (((1,), (1,)), ((), ())), preferred_element_type=F32)


def dot_tn(a, b):
    return lax.dot_general(a, b, (((0,), (0,)), ((), ())), preferred_element_type=F32)


def three(dot, a, b):
    return dot(a[0], b[0]) + dot(a[0], b[1]) + dot(a[1], b[0])


def spline(u):
    squared = u * u
    cubed = squared * u
    rest = 1.0 - u
    return (
        rest * rest * rest / 6.0,
        (3.0 * cubed - 6.0 * squared + 4.0) / 6.0,
        (-3.0 * cubed + 3.0 * squared + 3.0 * u + 1.0) / 6.0,
        cubed / 6.0,
    )


def placed(rows, cell, weights):
    off = lax.broadcasted_iota(jnp.int32, (rows, cell.shape[1]), 0) - cell
    value = jnp.where(off == 3, weights[3], 0.0)
    value = jnp.where(off == 2, weights[2], value)
    value = jnp.where(off == 1, weights[1], value)
    return jnp.where(off == 0, weights[0], value)


def spread_body(charge, frac, cell, waves_from, out, acc, waves, sem):
    step = pl.program_id(0)
    copy = pltpu.make_async_copy(waves_from, waves, sem)

    @pl.when(step == 0)
    def _():
        copy.start()
        acc[...] = jnp.zeros_like(acc)

    along_x = placed(XE, cell[0:1, :], spline(frac[0:1, :]))
    along_y = placed(YE, cell[1:2, :], spline(frac[1:2, :])) * charge[...]
    along_z = placed(16, cell[2:3, :], spline(frac[2:3, :]))
    plane = jnp.concatenate([along_z[z : z + 1, :] * along_y for z in range(ZE)], 0)
    acc[...] += three(dot_nt, split(along_x), split(plane))

    @pl.when(step == pl.num_programs(0) - 1)
    def _():
        copy.wait()
        freq = three(dot_tn, split(acc[...]), (waves[0], waves[1]))
        for s in range(N_SLAB):
            for z in range(ZE):
                out[s, :, z * 24 : z * 24 + 24] = freq[z * YE : z * YE + YE, s * 24 : s * 24 + 24]
            out[s, :, ZE * 24 : 384] = jnp.zeros((YE, 384 - ZE * 24), F32)


def spread(charge, frac, cell, waves):
    return pl.pallas_call(
        spread_body,
        grid=(SITES // CHUNK,),
        in_specs=[
            pl.BlockSpec((1, CHUNK), lambda i: (0, i)),
            pl.BlockSpec((3, CHUNK), lambda i: (0, i)),
            pl.BlockSpec((3, CHUNK), lambda i: (0, i)),
            pl.BlockSpec(memory_space=pltpu.HBM),
        ],
        out_specs=pl.BlockSpec((N_SLAB, YE, 384), lambda i: (0, 0, 0)),
        out_shape=jax.ShapeDtypeStruct((N_SLAB, YE, 384), F32),
        scratch_shapes=[
            pltpu.VMEM((XE, ZE * YE), F32),
            pltpu.VMEM((2, XE, 384), BF16),
            pltpu.SemaphoreType.DMA,
        ],
        compiler_params=pltpu.CompilerParams(vmem_limit_bytes=MOST),
        cost_estimate=pl.CostEstimate(flops=8_000_000_000, bytes_accessed=2_000_000, transcendentals=0),
        name="spread",
    )(charge.reshape(1, SITES), frac, cell, waves)


def lanes(tiles):
    return jnp.concatenate([tiles[i : i + 1] for i in range(tiles.shape[0])], 1)


def pack_body(drive, atom, cell, frac, hard, pos, width, out, near, picked):
    f, s = my_place()
    out[...] = jnp.zeros_like(out)
    for i in range(N_SLAB):
        out[i, 0:1, 0:OWN] = -drive[...]
        out[i, 1:2, 0:OWN] = atom[...].astype(F32)
        out[i, 2:5, 0:OWN] = cell[...].astype(F32)
        out[i, 5:8, 0:OWN] = frac[...]
    for j in range(N_FFT):
        at = pl.multiple_of(j * ROWS + (s >> 2) * 128, 128)
        picked[j, 0:3, :] = pos[:, pl.ds(at, 128)]
        picked[j, 3:4, :] = width[:, pl.ds(at, 128)]
    lane = lax.broadcasted_iota(jnp.int32, (8, 128), 1) >> 5
    for tile in range(COLS // 128):
        value = jnp.zeros((8, 128), F32)
        for j in range(4):
            value = jnp.where(lane == j, pltpu.roll(picked[tile * 4 + j], ((j - (s & 3)) & 3) * OWN, 1), value)
        near[:, tile * 128 : tile * 128 + 128] = value
    at = pl.multiple_of(f * ROWS, 128)
    near[:, COLS:] = jnp.zeros((8, ROWS), F32)
    near[0:3, COLS:] = pos[:, pl.ds(at, ROWS)]
    near[3:4, COLS:] = width[:, pl.ds(at, ROWS)]
    near[4:5, COLS : COLS + OWN] = hard[...]


def pack(drive, atom, cell, frac, hard, pos, width):
    return pl.pallas_call(
        pack_body,
        out_shape=(
            jax.ShapeDtypeStruct((N_SLAB, 8, 128), F32),
            jax.ShapeDtypeStruct((8, COLS + ROWS), F32),
        ),
        scratch_shapes=[pltpu.VMEM((N_FFT, 8, 128), F32)],
        compiler_params=pltpu.CompilerParams(vmem_limit_bytes=MOST),
        name="pack",
    )(
        drive.reshape(1, OWN),
        atom.reshape(1, OWN),
        cell,
        frac,
        hard.reshape(1, OWN),
        pos,
        width.reshape(1, ATOMS),
    )


def erf_ratio(value):
    square = value * value
    p = 0.00022905065861350646
    for c in (0.0034082910107109506, 0.050955695062380861, 0.18520832239976145, 1.128379143519084):
        p = p * square + c
    q = -1.1791602954361697e-7
    for c in (
        0.000023547966471313185,
        0.0010179625278914885,
        0.014070470171167667,
        0.11098505178285362,
        0.49746925110067538,
        1.0,
    ):
        q = q * square + c
    return value * p, q


def couple_body(near, out, own):
    f, s = my_place()
    cols = near[:, :COLS]
    side = jnp.transpose(near[:, COLS:])
    own[...] = jnp.zeros_like(own)
    own[0:1, 0:OWN] = near[4:5, COLS : COLS + OWN]
    own_hard = pltpu.roll(own[...], (f & 3) * OWN, 1)[0:1]
    diag = jnp.concatenate([jnp.where((f >> 2) == t, own_hard, 0.0) for t in range(COLS // 128)], 1)
    diag = diag + KE * (1.0 / (cols[3:4] * SQPI) - 2.0 * ALPHA / SQPI)
    col_id = lax.broadcasted_iota(jnp.int32, (1, COLS), 1) - f * OWN
    col_id = jnp.where((col_id >= 0) & (col_id < OWN), col_id + s * OWN, -1)
    col_sq = 2.0 * cols[3:4] * cols[3:4]
    step = 16
    for first in range(0, ROWS, step):
        here = side[first : first + step]
        square = SOFT
        for i in range(3):
            gap = here[:, i : i + 1] - cols[i : i + 1]
            square = square + gap * gap
        inverse = lax.rsqrt(square)
        distance = square * inverse
        narrow = lax.rsqrt(2.0 * here[:, 3:4] * here[:, 3:4] + col_sq)
        p1, q1 = erf_ratio(jnp.minimum(distance * narrow, 3.832506856900711))
        p2, q2 = erf_ratio(jnp.minimum(distance * ALPHA, 3.832506856900711))
        value = KE * inverse * ((p1 * q2 - p2 * q1) / (q1 * q2))
        row_id = first + lax.broadcasted_iota(jnp.int32, (step, 1), 0)
        out[first : first + step] = jnp.where(row_id == col_id, diag, value)


def couple(near):
    return pl.pallas_call(
        couple_body,
        out_shape=jax.ShapeDtypeStruct((ROWS, COLS), F32),
        scratch_shapes=[pltpu.VMEM((8, 128), F32)],
        compiler_params=pltpu.CompilerParams(vmem_limit_bytes=SOME),
        cost_estimate=pl.CostEstimate(flops=100_000_000, bytes_accessed=2_000_000, transcendentals=1_000_000),
        name="couple",
    )(near)


def first_body(got, matrix, out, slots):
    for s in range(N_SLAB):
        slots[:, s * OWN : s * OWN + OWN] = got[s, :, 0:OWN]
    every = slots[...]
    part = jnp.sum(matrix[...] * jnp.transpose(every)[:, 0:1], 0, keepdims=True)
    for i in range(8):
        out[0, i : i + 1, :] = part[:, i * 128 : i * 128 + 128]
    for i in range(4):
        out[0, 8 + i * 8 : 16 + i * 8, :] = every[:, i * 128 : i * 128 + 128]
    whole = out[0]
    for f in range(1, N_FFT):
        out[f] = whole


def first_product(got, matrix):
    return pl.pallas_call(
        first_body,
        out_shape=jax.ShapeDtypeStruct((N_FFT, 40, 128), F32),
        scratch_shapes=[pltpu.VMEM((8, ROWS), F32)],
        compiler_params=pltpu.CompilerParams(vmem_limit_bytes=SOME),
        name="first_product",
    )(got, matrix)


def y_body(grid, matrix, perm, arh, arl, aih, ail, out, side):
    got = grid[...]
    rows = jnp.sum(got[:, YE - 4 :, 0:128], 0)
    side[0:4, :] = rows
    turned = jnp.transpose(side[...])
    column = jnp.concatenate([turned[:, i : i + 1] for i in range(4)], 0)
    part = jnp.sum(matrix[...] * column, 0, keepdims=True)
    high, low = split(got.reshape(N_SLAB * YE, 384))
    high = dot_nt(perm[...], high).astype(BF16)
    low = dot_nt(perm[...], low).astype(BF16)
    freq = three(dot_nn, (high[:192], low[:192]), (arh[...], arl[...]))
    freq = freq + three(dot_nn, (high[192:], low[192:]), (aih[...], ail[...]))
    for i in range(16):
        out[0, i : i + 1, 288:320] = part[:, i * OWN : i * OWN + OWN]
        out[0, i : i + 1, 320:352] = part[:, ROWS + i * OWN : ROWS + i * OWN + OWN]
        out[0, i : i + 1, 352:384] = rows[i // 4 : i // 4 + 1, i % 4 * OWN : i % 4 * OWN + OWN]
    extra = out[0, :, 256:384]
    for f in range(N_FFT):
        if f > 0:
            out[f, :, 256:384] = extra
        for k in range(KX):
            out[f, :, k * 24 : k * 24 + 24] = freq[k * 16 : k * 16 + 16, f * 24 : f * 24 + 24]


def along_y(*operands):
    return pl.pallas_call(
        y_body,
        out_shape=jax.ShapeDtypeStruct((N_FFT, 16, 384), F32),
        scratch_shapes=[pltpu.VMEM((8, 128), F32)],
        compiler_params=pltpu.CompilerParams(vmem_limit_bytes=2 * SOME),
        cost_estimate=pl.CostEstimate(flops=4_000_000_000, bytes_accessed=5_000_000, transcendentals=0),
        name="along_y",
    )(*operands)


def quad_body(got, out):
    s = my_place()[1]
    third = jnp.sum(got[:, :, 32:96], 0)
    second = got[:, pl.ds(s, 1), 96:128].reshape(N_FFT, OWN)
    total = jnp.sum(third[:, 0:OWN] * second[0:16] + third[:, OWN:] * second[16:], 0, keepdims=True)
    total = jnp.sum(total, 1, keepdims=True)
    out[...] = jnp.broadcast_to(total[None], out.shape)


def quad_sum(got):
    return pl.pallas_call(
        quad_body,
        grid=(1,),
        in_specs=[
            pl.BlockSpec((N_FFT, 16, 128), lambda i: (0, 0, 2)),
        ],
        out_specs=pl.BlockSpec((N_SLAB, 8, 128), lambda i: (0, 0, 0)),
        out_shape=jax.ShapeDtypeStruct((N_SLAB, 8, 128), F32),
        compiler_params=pltpu.CompilerParams(vmem_limit_bytes=SOME),
        name="quad_sum",
    )(got)


def unit(turns):
    half = (turns - 0.5) * math.pi
    square = half * half
    sine = 0.0
    for power in (11, 9, 7, 5, 3):
        sine = (sine + (-1.0) ** (power // 2) / math.factorial(power)) * square
    sine = half * (1.0 + sine)
    cosine = 0.0
    for power in (12, 10, 8, 6, 4, 2):
        cosine = (cosine + (-1.0) ** (power // 2) / math.factorial(power)) * square
    cosine = 1.0 + cosine
    return 2.0 * sine * sine - 1.0, 2.0 * sine * cosine


def site_wave(first, base, fraction, steps):
    local = lax.broadcasted_iota(jnp.int32, (16, 1), 0)
    freq = first + jnp.where(local < 12, local, local - 4).astype(F32)
    phase = freq * base
    phase = phase - NG * jnp.floor(phase * (1.0 / NG))
    re, im = unit(phase * (1.0 / NG))
    weights = spline(fraction)
    w_re = sum(steps[:, i : i + 1] * weights[i] for i in range(4))
    w_im = sum(steps[:, 4 + i : 5 + i] * weights[i] for i in range(1, 4))
    return re * w_re - im * w_im, re * w_im + im * w_re


def slot_rows(slots, g):
    return jnp.concatenate([slots[g, 8 + i * 8 : 16 + i * 8, :] for i in range(4)], 1)


def table_body(slots, steps, out):
    f, s = my_place()
    block = (lax.broadcasted_iota(jnp.int32, (1, ROWS), 1) // OWN * YL).astype(F32)
    first_x, first_y = (s * KX).astype(F32), (f * KY).astype(F32)
    for g in range(8):
        rows = slot_rows(slots, g)
        x_re, x_im = site_wave(first_x, rows[2:3], rows[5:6], steps[:, 0:8])
        y_re, y_im = site_wave(first_y, rows[3:4] + block, rows[6:7], steps[:, 8:16])
        out[g, 0:16] = x_re
        out[g, 16:32] = x_im
        out[g, 32:48] = y_re
        out[g, 48:64] = y_im
        out[g, 64:96] = jnp.zeros((32, ROWS), F32)


def tables(slots, steps):
    return pl.pallas_call(
        table_body,
        grid=(4,),
        in_specs=[
            pl.BlockSpec((8, 40, 128), lambda i: (i, 0, 0)),
            pl.BlockSpec((16, 16), lambda i: (0, 0)),
        ],
        out_specs=pl.BlockSpec((8, 96, ROWS), lambda i: (i, 0, 0)),
        out_shape=jax.ShapeDtypeStruct((N_FFT, 96, ROWS), F32),
        compiler_params=pltpu.CompilerParams(vmem_limit_bytes=MOST),
        cost_estimate=pl.CostEstimate(flops=2_000_000_000, bytes_accessed=5_000_000, transcendentals=0),
        name="tables",
    )(slots, steps)


def guarded(value, pivot, scale):
    good = pivot > 1e-6 * scale
    return jnp.where(good, value / jnp.where(good, pivot, 1.0), 0.0)


def lookup(tables, atom):
    index = lax.broadcasted_iota(jnp.int32, (128, atom.shape[1]), 0)
    pick = jnp.where(index == (atom & 127), 1.0, 0.0).astype(BF16)
    rows = dot_nn(tables, jnp.concatenate([pick, pick], 0))
    here = index == (atom >> 7)
    count = rows.shape[0] // 128
    return [
        jnp.sum(jnp.where(here, rows[v * 128 : v * 128 + 128], 0.0), 0, keepdims=True) for v in range(count)
    ]


def early_body(slots, first, out, v0):
    for i in range(4):
        v0[pl.ds(i, N_FFT, stride=4), :] = slots[:, 8 + i * 8, :]
    both = jnp.concatenate([v0[...], first[...]], 0)
    high, low = split(both)
    both = jnp.concatenate([high, low], 1)
    for g in range(N_FFT):
        found = lookup(both, slot_rows(slots, g)[1:2].astype(jnp.int32))
        for v in range(2):
            for i in range(4):
                out[v, g * 4 + i : g * 4 + i + 1, :] = found[v][:, i * 128 : i * 128 + 128]


def early(slots, first):
    return pl.pallas_call(
        early_body,
        out_shape=jax.ShapeDtypeStruct((2, 128, 128), F32),
        scratch_shapes=[pltpu.VMEM((128, 128), F32)],
        compiler_params=pltpu.CompilerParams(vmem_limit_bytes=SOME),
        cost_estimate=pl.CostEstimate(flops=2_000_000_000, bytes_accessed=1_000_000, transcendentals=0),
        name="early",
    )(slots, first)


def late_body(slots, before, first, grid, perm, waves_from, out, rest, v2, late, charges, waves, sems):
    copies = [
        pltpu.make_async_copy(
            waves_from.at[pl.ds(i * 8, 8), pl.ds(0, 64)], waves.at[pl.ds(i * 8, 8)], sems.at[i]
        )
        for i in range(4)
    ]
    for copy in copies:
        copy.start()
    f, s = my_place()
    for i in range(4):
        pieces = [grid[:, i * 4 + j, 352:384] for j in range(4)]
        v2[pl.ds(i, N_FFT, stride=4), :] = jnp.concatenate(pieces, 1)
    high, low = split(v2[...])
    both = jnp.concatenate([high, low], 1)
    for g in range(N_FFT):
        found = lookup(both, slot_rows(slots, g)[1:2].astype(jnp.int32))[0]
        for i in range(4):
            late[g * 4 + i : g * 4 + i + 1, :] = found[:, i * 128 : i * 128 + 128]

    def dot(a, b):
        return jnp.sum(jnp.sum(a * b, 0, keepdims=True), 1, keepdims=True)

    a, b, c = before[0], before[1], late[...]
    m0, m1, m2, m3, m4 = dot(a, a), dot(a, b), dot(b, b), dot(b, c), dot(c, c)
    l10 = m2 / m1
    l20 = m3 / m1
    d1 = m3 - l10 * m2
    e12 = m4 - l10 * m3
    l21 = guarded(e12, d1, m3)
    g1 = m1 - l10 * m0
    g2 = (m2 - l20 * m0) - l21 * g1
    c1 = guarded(g1, d1, m3)
    c0 = m0 / m1 - l10 * c1
    charges[0] = c0 * a + c1 * b
    charges[1] = c - l21 * b + (l10 * l21 - l20) * a
    at = f * 4 + (s >> 2)
    rest[...] = jnp.zeros_like(rest)
    own = [slots[pl.ds(f, 1), 8 + i * 8, :] for i in range(4)]
    a = sum(jnp.where((s >> 2) == i, own[i], 0.0) for i in range(4))
    b, c = first[pl.ds(at, 1), :], v2[pl.ds(at, 1), :]
    rest[0:1] = c0 * a + c1 * b
    rest[1:2] = c - l21 * b + (l10 * l21 - l20) * a
    rest[...] = pltpu.roll(rest[...], ((4 - (s & 3)) & 3) * OWN, 1)
    rest[2:3] = jnp.broadcast_to(l20 * m3 + l21 * e12, (1, 128))
    rest[3:4] = jnp.broadcast_to(g2, (1, 128))

    upper = lax.broadcasted_iota(jnp.int32, (8, 1), 0) < 4

    def group(i, carry):
        at = pl.multiple_of(i * 32, 32)
        charge = [charges[v, pl.ds(at, 32), :] for v in range(2)]
        high, low = split(grid[pl.ds(i * 8, 8)].reshape(128, 384))
        base = (dot_nn(high, perm[...]) + dot_nn(low, perm[...])).reshape(8, 16, PAIRS)
        for j in range(8):
            g = i * 8 + j
            rows = slot_rows(slots, g)
            placed_z = placed(16, rows[4:5].astype(jnp.int32), spline(rows[7:8]))
            both = [placed_z * lanes(charge[v][j * 4 : j * 4 + 4]) for v in range(2)]
            z_high, z_low = split(jnp.concatenate(both, 0))
            x_re, x_im = waves[g, 0:8], waves[g, 16:24]
            parts_re, parts_im = [], []
            for k in range(KY):
                y_re, y_im = waves[g, 32 + k : 33 + k], waves[g, 48 + k : 49 + k]
                parts_re.append(y_re * x_re - y_im * x_im)
                parts_im.append(y_re * x_im + y_im * x_re)
            parts = parts_re + parts_im
            x_re, x_im = waves[g, 8:16], waves[g, 24:32]
            parts_re, parts_im = [], []
            for k in range(0, KY, 2):
                y_re = jnp.where(upper, waves[g, 32 + k : 33 + k], waves[g, 33 + k : 34 + k])
                y_im = jnp.where(upper, waves[g, 48 + k : 49 + k], waves[g, 49 + k : 50 + k])
                parts_re.append(y_re * x_re - y_im * x_im)
                parts_im.append(y_re * x_im + y_im * x_re)
            high, low = split(jnp.concatenate(parts + parts_re + parts_im, 0))
            total = dot_nt(jnp.concatenate([z_high, z_low], 0), high)
            total = total[:32] + total[32:] + dot_nt(z_high, low)
            out[g, 0:16] = total[:16] + base[j]
            out[g, 16:32] = total[16:]
        return carry

    for copy in copies:
        copy.wait()
    lax.fori_loop(0, 4, group, 0)


def late_waves(*operands):
    return pl.pallas_call(
        late_body,
        in_specs=[pl.BlockSpec(memory_space=pltpu.VMEM)] * 5 + [pl.BlockSpec(memory_space=pl.ANY)],
        out_shape=(
            jax.ShapeDtypeStruct((N_FFT, 32, PAIRS), F32),
            jax.ShapeDtypeStruct((8, 128), F32),
        ),
        scratch_shapes=[
            pltpu.VMEM((128, 128), F32),
            pltpu.VMEM((128, 128), F32),
            pltpu.VMEM((2, 128, 128), F32),
            pltpu.VMEM((N_FFT, 64, ROWS), F32),
            pltpu.SemaphoreType.DMA((4,)),
        ],
        compiler_params=pltpu.CompilerParams(vmem_limit_bytes=LATE),
        cost_estimate=pl.CostEstimate(flops=5_000_000_000, bytes_accessed=7_000_000, transcendentals=0),
        name="late_waves",
    )(*operands)


def z_body(ml, quads, rest, waves, out_re, out_im, out_q):
    m5 = jnp.sum(quads[:, 0, :], 0, keepdims=True)
    step = guarded(rest[3:4], m5 - rest[2:3], m5)[:, 0:1]
    total = ml[:, 0:16] + step[None] * ml[:, 16:32]
    both = split(total.reshape(N_FFT * 16, PAIRS))
    cos = three(dot_tn, both, (waves[0], waves[1]))
    sin = three(dot_tn, both, (waves[2], waves[3]))
    for k in range(KY):
        for first, count, re in ((0, 8, k * 8), (8, 4, 192 + k * 4)):
            im = re + KY * count
            out_re[k, first : first + count] = cos[re : re + count] + sin[im : im + count]
            out_im[k, first : first + count] = cos[im : im + count] - sin[re : re + count]
    out_q[...] = (rest[0:1] + step * rest[1:2])[:, 0:OWN]


def along_z(*operands):
    shape = jax.ShapeDtypeStruct((KY, KX, NG), F32)
    return pl.pallas_call(
        z_body,
        out_shape=(shape, shape, jax.ShapeDtypeStruct((1, OWN), F32)),
        compiler_params=pltpu.CompilerParams(vmem_limit_bytes=2 * SOME),
        cost_estimate=pl.CostEstimate(flops=3_000_000_000, bytes_accessed=5_000_000, transcendentals=0),
        name="along_z",
    )(*operands)


def swap(value, axis):
    return lax.all_to_all(value, axis, 0, 0, tiled=True)


def on_device(
    ml_pos,
    ml_width,
    ml_drive,
    ml_hard,
    mm_charge,
    mm_frac,
    mm_cell,
    slot_atom,
    slot_frac,
    slot_cell,
):
    f = lax.axis_index("fft")
    s = lax.axis_index("slab")

    sent, near = pack(ml_drive, slot_atom, slot_cell, slot_frac, ml_hard, ml_pos, ml_width)
    got = swap(sent, "slab")
    matrix = couple(near)
    got_1 = swap(first_product(got, matrix), "fft")
    mm = spread(mm_charge, mm_frac, mm_cell, jnp.asarray(np.stack(two_parts(x_table()))))
    first_cols = jnp.sum(got_1[:, :8], 0)
    part = jnp.sum(matrix * first_cols.reshape(1, COLS), 1)
    tail = jnp.concatenate([part.reshape(4, 128), first_cols[:4], first_cols[4:]], 1)
    tail = jnp.broadcast_to(tail[None], (N_SLAB, 4, 384))
    got_2 = swap(jnp.concatenate([mm[:, : YE - 4], tail], 1), "slab")
    first_full = jnp.concatenate([got_2[:, YE - 4 :, 128:256], got_2[:, YE - 4 :, 256:]], 1)
    first_full = jnp.transpose(first_full.reshape(N_SLAB, N_FFT, OWN), (1, 0, 2)).reshape(128, 128)

    arh, arl, aih, ail = (jnp.asarray(t) for half in y_tables() for t in two_parts(half))
    got_3 = swap(along_y(got_2, matrix, jnp.asarray(perm_y()), arh, arl, aih, ail), "fft")
    quads = swap(quad_sum(got_3), "slab")

    steps = jnp.concatenate(
        [
            lax.dynamic_index_in_dim(jnp.asarray(step_table(N_SLAB)), s, 0, False),
            lax.dynamic_index_in_dim(jnp.asarray(step_table(N_FFT)), f, 0, False),
        ],
        1,
    )
    waves = tables(got_1, steps)
    before = early(got_1, first_full)
    ml, rest = late_waves(got_1, before, first_full, got_3, jnp.asarray(perm_z()), waves)
    z_waves = jnp.asarray(np.stack([t for half in z_tables() for t in two_parts(half)]))
    struct_re, struct_im, charge = along_z(ml, quads, rest, z_waves)
    return (charge.reshape(OWN), struct_re, struct_im)


def solution(mesh):
    return jax.shard_map(
        on_device,
        mesh=mesh,
        in_specs=(
            P(),
            P(),
            P(("fft", "slab")),
            P(("fft", "slab")),
            P(("fft", "slab")),
            P(None, ("fft", "slab")),
            P(None, ("fft", "slab")),
            P(("fft", "slab")),
            P(None, ("fft", "slab")),
            P(None, ("fft", "slab")),
        ),
        out_specs=(P(("fft", "slab")), P("fft", "slab", None), P("fft", "slab", None)),
        check_vma=False,
    )
```

```python
import math

import jax
import jax.numpy as jnp
import numpy as np
from jax import lax
from jax.experimental import pallas as pl
from jax.experimental.pallas import tpu as pltpu
from jax.sharding import PartitionSpec as P

NG = 384
N_FFT = 32
N_SLAB = 16
YL = 24
ZL = 12
KX = 12
KY = 12
OWN = 32
ROWS = 512
COLS = 1024
ATOMS = 16384
SITES = 6144
CHUNK = 1024
XE = 392
YE = 32
ZE = 15
PAIRS = 288

KE = 14.4
ALPHA = 0.08
SOFT = 0.01
SQPI = math.sqrt(math.pi)
F32 = jnp.float32
BF16 = jnp.bfloat16
MOST = 60 * 1024 * 1024
SOME = 12 * 1024 * 1024


def wave(points, freqs):
    angle = 2.0 * np.pi * ((points[:, None] * freqs[None, :]) % NG) / NG
    return np.cos(angle), np.sin(angle)


def two_parts(table):
    high = np.asarray(table, np.float32).astype(jnp.bfloat16)
    low = (np.asarray(table, np.float64) - high.astype(np.float64)).astype(jnp.bfloat16)
    return high, low


def x_table():
    points = np.arange(XE)
    cos, sin = wave(points, np.arange(NG // 2))
    cos, sin = (t.reshape(XE, N_SLAB, 1, KX) for t in (cos, sin))
    table = np.concatenate([cos, -sin], 2)
    table = table * (points < NG + 3)[:, None, None, None]
    return table.reshape(XE, N_SLAB * 2 * KX)


def y_tables():
    local = np.arange(YE)
    points = (np.arange(N_SLAB)[:, None] * YL + local[None, :]).reshape(-1)
    used = np.tile(local < YL + 3, N_SLAB)[:, None, None, None]
    cos, sin = wave(points, np.arange(NG))
    cos, sin = (t.reshape(-1, N_FFT, 1, KY) for t in (cos, sin))
    from_re = np.concatenate([cos, -sin], 2) * used
    from_im = np.concatenate([sin, cos], 2) * used
    return from_re.reshape(-1, 2 * NG), from_im.reshape(-1, 2 * NG)


def z_tables():
    local = np.arange(16)
    points = (np.arange(N_FFT)[:, None] * ZL + local[None, :]).reshape(-1)
    used = np.tile(local < ZL + 3, N_FFT)[:, None]
    scale = 1.0 / (NG * math.sqrt(NG))
    cos, sin = wave(points, np.arange(NG))
    return cos * used * scale, sin * used * scale


def perm_y():
    table = np.zeros((2, KX, 16, 384), np.float32)
    for c in range(2):
        for k in range(KX):
            for z in range(ZE):
                table[c, k, z, z * 24 + c * KX + k] = 1.0
    return table.reshape(384, 384).astype(jnp.bfloat16)


def perm_z():
    table = np.zeros((384, PAIRS), np.float32)
    for c in range(2):
        for k in range(KY):
            for x in range(KX):
                column = c * 96 + k * 8 + x if x < 8 else 192 + c * 48 + k * 4 + x - 8
                table[x * 24 + c * KY + k, column] = 1.0
    return table.astype(jnp.bfloat16)


def step_table(count):
    freqs = (np.arange(count) * 12)[:, None] + np.arange(12)[None, :]
    angle = 2.0 * np.pi * freqs[:, :, None] * np.arange(4)[None, None, :] / NG
    return np.concatenate([np.cos(angle), -np.sin(angle)], 2).astype(np.float32)


def my_place():
    return lax.axis_index("fft"), lax.axis_index("slab")


def split(value):
    high = value.astype(BF16)
    return high, (value - high.astype(F32)).astype(BF16)


def dot_nn(a, b):
    return lax.dot_general(a, b, (((1,), (0,)), ((), ())), preferred_element_type=F32)


def dot_nt(a, b):
    return lax.dot_general(a, b, (((1,), (1,)), ((), ())), preferred_element_type=F32)


def dot_tn(a, b):
    return lax.dot_general(a, b, (((0,), (0,)), ((), ())), preferred_element_type=F32)


def three(dot, a, b):
    return dot(a[0], b[0]) + dot(a[0], b[1]) + dot(a[1], b[0])


def spline(u):
    squared = u * u
    cubed = squared * u
    rest = 1.0 - u
    return (
        rest * rest * rest / 6.0,
        (3.0 * cubed - 6.0 * squared + 4.0) / 6.0,
        (-3.0 * cubed + 3.0 * squared + 3.0 * u + 1.0) / 6.0,
        cubed / 6.0,
    )


def placed(rows, cell, weights):
    off = lax.broadcasted_iota(jnp.int32, (rows, cell.shape[1]), 0) - cell
    value = jnp.where(off == 3, weights[3], 0.0)
    value = jnp.where(off == 2, weights[2], value)
    value = jnp.where(off == 1, weights[1], value)
    return jnp.where(off == 0, weights[0], value)


def spread_body(charge, frac, cell, waves_from, out, acc, waves, sem):
    step = pl.program_id(0)
    copy = pltpu.make_async_copy(waves_from, waves, sem)

    @pl.when(step == 0)
    def _():
        copy.start()
        acc[...] = jnp.zeros_like(acc)

    along_x = placed(XE, cell[0:1, :], spline(frac[0:1, :]))
    along_y = placed(YE, cell[1:2, :], spline(frac[1:2, :])) * charge[...]
    along_z = placed(16, cell[2:3, :], spline(frac[2:3, :]))
    plane = jnp.concatenate([along_z[z : z + 1, :] * along_y for z in range(ZE)], 0)
    acc[...] += three(dot_nt, split(along_x), split(plane))

    @pl.when(step == pl.num_programs(0) - 1)
    def _():
        copy.wait()
        freq = three(dot_tn, split(acc[...]), (waves[0], waves[1]))
        for s in range(N_SLAB):
            for z in range(ZE):
                out[s, :, z * 24 : z * 24 + 24] = freq[z * YE : z * YE + YE, s * 24 : s * 24 + 24]
            out[s, :, ZE * 24 : 384] = jnp.zeros((YE, 384 - ZE * 24), F32)


def spread(charge, frac, cell, waves):
    return pl.pallas_call(
        spread_body,
        grid=(SITES // CHUNK,),
        in_specs=[
            pl.BlockSpec((1, CHUNK), lambda i: (0, i)),
            pl.BlockSpec((3, CHUNK), lambda i: (0, i)),
            pl.BlockSpec((3, CHUNK), lambda i: (0, i)),
            pl.BlockSpec(memory_space=pltpu.HBM),
        ],
        out_specs=pl.BlockSpec((N_SLAB, YE, 384), lambda i: (0, 0, 0)),
        out_shape=jax.ShapeDtypeStruct((N_SLAB, YE, 384), F32),
        scratch_shapes=[
            pltpu.VMEM((XE, ZE * YE), F32),
            pltpu.VMEM((2, XE, 384), BF16),
            pltpu.SemaphoreType.DMA,
        ],
        compiler_params=pltpu.CompilerParams(vmem_limit_bytes=MOST),
        cost_estimate=pl.CostEstimate(flops=8_000_000_000, bytes_accessed=2_000_000, transcendentals=0),
        name="spread",
    )(charge.reshape(1, SITES), frac, cell, waves)


def lanes(tiles):
    return jnp.concatenate([tiles[i : i + 1] for i in range(tiles.shape[0])], 1)


def pack_body(drive, atom, cell, frac, hard, pos, width, out, near, picked):
    f, s = my_place()
    out[...] = jnp.zeros_like(out)
    for i in range(N_SLAB):
        out[i, 0:1, 0:OWN] = -drive[...]
        out[i, 1:2, 0:OWN] = atom[...].astype(F32)
        out[i, 2:5, 0:OWN] = cell[...].astype(F32)
        out[i, 5:8, 0:OWN] = frac[...]
    for j in range(N_FFT):
        at = pl.multiple_of(j * ROWS + (s >> 2) * 128, 128)
        picked[j, 0:3, :] = pos[:, pl.ds(at, 128)]
        picked[j, 3:4, :] = width[:, pl.ds(at, 128)]
    lane = lax.broadcasted_iota(jnp.int32, (8, 128), 1) >> 5
    for tile in range(COLS // 128):
        value = jnp.zeros((8, 128), F32)
        for j in range(4):
            value = jnp.where(lane == j, pltpu.roll(picked[tile * 4 + j], ((j - (s & 3)) & 3) * OWN, 1), value)
        near[:, tile * 128 : tile * 128 + 128] = value
    at = pl.multiple_of(f * ROWS, 128)
    near[:, COLS:] = jnp.zeros((8, ROWS), F32)
    near[0:3, COLS:] = pos[:, pl.ds(at, ROWS)]
    near[3:4, COLS:] = width[:, pl.ds(at, ROWS)]
    near[4:5, COLS : COLS + OWN] = hard[...]


def pack(drive, atom, cell, frac, hard, pos, width):
    return pl.pallas_call(
        pack_body,
        out_shape=(
            jax.ShapeDtypeStruct((N_SLAB, 8, 128), F32),
            jax.ShapeDtypeStruct((8, COLS + ROWS), F32),
        ),
        scratch_shapes=[pltpu.VMEM((N_FFT, 8, 128), F32)],
        compiler_params=pltpu.CompilerParams(vmem_limit_bytes=MOST),
        name="pack",
    )(
        drive.reshape(1, OWN),
        atom.reshape(1, OWN),
        cell,
        frac,
        hard.reshape(1, OWN),
        pos,
        width.reshape(1, ATOMS),
    )


def erf_ratio(value):
    square = value * value
    p = 0.00022905065861350646
    for c in (0.0034082910107109506, 0.050955695062380861, 0.18520832239976145, 1.128379143519084):
        p = p * square + c
    q = -1.1791602954361697e-7
    for c in (
        0.000023547966471313185,
        0.0010179625278914885,
        0.014070470171167667,
        0.11098505178285362,
        0.49746925110067538,
        1.0,
    ):
        q = q * square + c
    return value * p, q


def couple_body(near, out, own):
    f, s = my_place()
    cols = near[:, :COLS]
    side = jnp.transpose(near[:, COLS:])
    own[...] = jnp.zeros_like(own)
    own[0:1, 0:OWN] = near[4:5, COLS : COLS + OWN]
    own_hard = pltpu.roll(own[...], (f & 3) * OWN, 1)[0:1]
    diag = jnp.concatenate([jnp.where((f >> 2) == t, own_hard, 0.0) for t in range(COLS // 128)], 1)
    diag = diag + KE * (1.0 / (cols[3:4] * SQPI) - 2.0 * ALPHA / SQPI)
    col_id = lax.broadcasted_iota(jnp.int32, (1, COLS), 1) - f * OWN
    col_id = jnp.where((col_id >= 0) & (col_id < OWN), col_id + s * OWN, -1)
    col_sq = 2.0 * cols[3:4] * cols[3:4]
    step = 16
    for first in range(0, ROWS, step):
        here = side[first : first + step]
        square = SOFT
        for i in range(3):
            gap = here[:, i : i + 1] - cols[i : i + 1]
            square = square + gap * gap
        inverse = lax.rsqrt(square)
        distance = square * inverse
        narrow = lax.rsqrt(2.0 * here[:, 3:4] * here[:, 3:4] + col_sq)
        p1, q1 = erf_ratio(jnp.minimum(distance * narrow, 3.832506856900711))
        p2, q2 = erf_ratio(jnp.minimum(distance * ALPHA, 3.832506856900711))
        value = KE * inverse * ((p1 * q2 - p2 * q1) / (q1 * q2))
        row_id = first + lax.broadcasted_iota(jnp.int32, (step, 1), 0)
        out[first : first + step] = jnp.where(row_id == col_id, diag, value)


def couple(near):
    return pl.pallas_call(
        couple_body,
        out_shape=jax.ShapeDtypeStruct((ROWS, COLS), F32),
        scratch_shapes=[pltpu.VMEM((8, 128), F32)],
        compiler_params=pltpu.CompilerParams(vmem_limit_bytes=SOME),
        cost_estimate=pl.CostEstimate(flops=100_000_000, bytes_accessed=2_000_000, transcendentals=1_000_000),
        name="couple",
    )(near)


def first_body(got, matrix, out, slots):
    for s in range(N_SLAB):
        slots[:, s * OWN : s * OWN + OWN] = got[s, :, 0:OWN]
    every = slots[...]
    part = jnp.sum(matrix[...] * jnp.transpose(every)[:, 0:1], 0, keepdims=True)
    for i in range(8):
        out[0, i : i + 1, :] = part[:, i * 128 : i * 128 + 128]
    for i in range(4):
        out[0, 8 + i * 8 : 16 + i * 8, :] = every[:, i * 128 : i * 128 + 128]
    whole = out[0]
    for f in range(1, N_FFT):
        out[f] = whole


def first_product(got, matrix):
    return pl.pallas_call(
        first_body,
        out_shape=jax.ShapeDtypeStruct((N_FFT, 40, 128), F32),
        scratch_shapes=[pltpu.VMEM((8, ROWS), F32)],
        compiler_params=pltpu.CompilerParams(vmem_limit_bytes=SOME),
        name="first_product",
    )(got, matrix)


def y_body(grid, matrix, perm, arh, arl, aih, ail, out, side):
    got = grid[...]
    rows = jnp.sum(got[:, YE - 4 :, 0:128], 0)
    side[0:4, :] = rows
    turned = jnp.transpose(side[...])
    column = jnp.concatenate([turned[:, i : i + 1] for i in range(4)], 0)
    part = jnp.sum(matrix[...] * column, 0, keepdims=True)
    high, low = split(got.reshape(N_SLAB * YE, 384))
    high = dot_nt(perm[...], high).astype(BF16)
    low = dot_nt(perm[...], low).astype(BF16)
    freq = three(dot_nn, (high[:192], low[:192]), (arh[...], arl[...]))
    freq = freq + three(dot_nn, (high[192:], low[192:]), (aih[...], ail[...]))
    for i in range(16):
        out[0, i : i + 1, 288:320] = part[:, i * OWN : i * OWN + OWN]
        out[0, i : i + 1, 320:352] = part[:, ROWS + i * OWN : ROWS + i * OWN + OWN]
        out[0, i : i + 1, 352:384] = rows[i // 4 : i // 4 + 1, i % 4 * OWN : i % 4 * OWN + OWN]
    extra = out[0, :, 256:384]
    for f in range(N_FFT):
        if f > 0:
            out[f, :, 256:384] = extra
        for k in range(KX):
            out[f, :, k * 24 : k * 24 + 24] = freq[k * 16 : k * 16 + 16, f * 24 : f * 24 + 24]


def along_y(*operands):
    return pl.pallas_call(
        y_body,
        out_shape=jax.ShapeDtypeStruct((N_FFT, 16, 384), F32),
        scratch_shapes=[pltpu.VMEM((8, 128), F32)],
        compiler_params=pltpu.CompilerParams(vmem_limit_bytes=2 * SOME),
        cost_estimate=pl.CostEstimate(flops=4_000_000_000, bytes_accessed=5_000_000, transcendentals=0),
        name="along_y",
    )(*operands)


def quad_body(got, out):
    s = my_place()[1]
    third = jnp.sum(got[:, :, 32:96], 0)
    second = got[:, pl.ds(s, 1), 96:128].reshape(N_FFT, OWN)
    total = jnp.sum(third[:, 0:OWN] * second[0:16] + third[:, OWN:] * second[16:], 0, keepdims=True)
    total = jnp.sum(total, 1, keepdims=True)
    out[...] = jnp.broadcast_to(total[None], out.shape)


def quad_sum(got):
    return pl.pallas_call(
        quad_body,
        grid=(1,),
        in_specs=[
            pl.BlockSpec((N_FFT, 16, 128), lambda i: (0, 0, 2)),
        ],
        out_specs=pl.BlockSpec((N_SLAB, 8, 128), lambda i: (0, 0, 0)),
        out_shape=jax.ShapeDtypeStruct((N_SLAB, 8, 128), F32),
        compiler_params=pltpu.CompilerParams(vmem_limit_bytes=SOME),
        name="quad_sum",
    )(got)


def unit(turns):
    half = (turns - 0.5) * math.pi
    square = half * half
    sine = 0.0
    for power in (11, 9, 7, 5, 3):
        sine = (sine + (-1.0) ** (power // 2) / math.factorial(power)) * square
    sine = half * (1.0 + sine)
    cosine = 0.0
    for power in (12, 10, 8, 6, 4, 2):
        cosine = (cosine + (-1.0) ** (power // 2) / math.factorial(power)) * square
    cosine = 1.0 + cosine
    return 2.0 * sine * sine - 1.0, 2.0 * sine * cosine


def site_waves(freq, base, fraction, steps):
    upper = lax.broadcasted_iota(jnp.int32, (8, 1), 0) < 4

    def in_rows(x, y):
        wide = [jnp.broadcast_to(v, (8, ROWS)) for v in (x, y)]
        return jnp.concatenate(wide + [jnp.where(upper, x, y)], 0)

    phase = freq * in_rows(*base)
    phase = phase - NG * jnp.floor(phase * (1.0 / NG))
    re, im = unit(phase * (1.0 / NG))
    weights = [in_rows(x, y) for x, y in zip(spline(fraction[0]), spline(fraction[1]), strict=True)]
    w_re = sum(steps[:, i : i + 1] * weights[i] for i in range(4))
    w_im = sum(steps[:, 4 + i : 5 + i] * weights[i] for i in range(1, 4))
    return re * w_re - im * w_im, re * w_im + im * w_re


def slot_rows(slots, g):
    return jnp.concatenate([slots[g, 8 + i * 8 : 16 + i * 8, :] for i in range(4)], 1)


def guarded(value, pivot, scale):
    good = pivot > 1e-6 * scale
    return jnp.where(good, value / jnp.where(good, pivot, 1.0), 0.0)


def lookup(tables, atom):
    index = lax.broadcasted_iota(jnp.int32, (128, atom.shape[1]), 0)
    pick = jnp.where(index == (atom & 127), 1.0, 0.0).astype(BF16)
    rows = dot_nn(tables, jnp.concatenate([pick, pick], 0))
    here = index == (atom >> 7)
    count = rows.shape[0] // 128
    return [
        jnp.sum(jnp.where(here, rows[v * 128 : v * 128 + 128], 0.0), 0, keepdims=True) for v in range(count)
    ]


def early_body(slots, first, out, v0):
    for i in range(4):
        v0[pl.ds(i, N_FFT, stride=4), :] = slots[:, 8 + i * 8, :]
    both = jnp.concatenate([v0[...], first[...]], 0)
    high, low = split(both)
    both = jnp.concatenate([high, low], 1)
    for g in range(N_FFT):
        found = lookup(both, slot_rows(slots, g)[1:2].astype(jnp.int32))
        for v in range(2):
            for i in range(4):
                out[v, g * 4 + i : g * 4 + i + 1, :] = found[v][:, i * 128 : i * 128 + 128]


def early(slots, first):
    return pl.pallas_call(
        early_body,
        out_shape=jax.ShapeDtypeStruct((2, 128, 128), F32),
        scratch_shapes=[pltpu.VMEM((128, 128), F32)],
        compiler_params=pltpu.CompilerParams(vmem_limit_bytes=SOME),
        cost_estimate=pl.CostEstimate(flops=2_000_000_000, bytes_accessed=1_000_000, transcendentals=0),
        name="early",
    )(slots, first)


def late_body(slots, before, first, grid, perm, steps, out, rest, v2, late, charges):
    f, s = my_place()
    for i in range(4):
        pieces = [grid[:, i * 4 + j, 352:384] for j in range(4)]
        v2[pl.ds(i, N_FFT, stride=4), :] = jnp.concatenate(pieces, 1)
    high, low = split(v2[...])
    both = jnp.concatenate([high, low], 1)
    for g in range(N_FFT):
        found = lookup(both, slot_rows(slots, g)[1:2].astype(jnp.int32))[0]
        for i in range(4):
            late[g * 4 + i : g * 4 + i + 1, :] = found[:, i * 128 : i * 128 + 128]

    def dot(a, b):
        return jnp.sum(jnp.sum(a * b, 0, keepdims=True), 1, keepdims=True)

    a, b, c = before[0], before[1], late[...]
    m0, m1, m2, m3, m4 = dot(a, a), dot(a, b), dot(b, b), dot(b, c), dot(c, c)
    l10 = m2 / m1
    l20 = m3 / m1
    d1 = m3 - l10 * m2
    e12 = m4 - l10 * m3
    l21 = guarded(e12, d1, m3)
    g1 = m1 - l10 * m0
    g2 = (m2 - l20 * m0) - l21 * g1
    c1 = guarded(g1, d1, m3)
    c0 = m0 / m1 - l10 * c1
    charges[0] = c0 * a + c1 * b
    charges[1] = c - l21 * b + (l10 * l21 - l20) * a
    at = f * 4 + (s >> 2)
    rest[...] = jnp.zeros_like(rest)
    own = [slots[pl.ds(f, 1), 8 + i * 8, :] for i in range(4)]
    a = sum(jnp.where((s >> 2) == i, own[i], 0.0) for i in range(4))
    b, c = first[pl.ds(at, 1), :], v2[pl.ds(at, 1), :]
    rest[0:1] = c0 * a + c1 * b
    rest[1:2] = c - l21 * b + (l10 * l21 - l20) * a
    rest[...] = pltpu.roll(rest[...], ((4 - (s & 3)) & 3) * OWN, 1)
    rest[2:3] = jnp.broadcast_to(l20 * m3 + l21 * e12, (1, 128))
    rest[3:4] = jnp.broadcast_to(g2, (1, 128))

    upper = lax.broadcasted_iota(jnp.int32, (8, 1), 0) < 4
    block = (lax.broadcasted_iota(jnp.int32, (1, ROWS), 1) // OWN * YL).astype(F32)
    local = lax.broadcasted_iota(jnp.int32, (24, 1), 0)
    freq = jnp.where(local < 8, s * KX + local, f * KY + local - 8)
    freq = jnp.where(local < 16, freq, jnp.where(local < 20, s * KX + local - 8, f * KY + local - 12)).astype(F32)

    def group(i, carry):
        at = pl.multiple_of(i * 32, 32)
        charge = [charges[v, pl.ds(at, 32), :] for v in range(2)]
        high, low = split(grid[pl.ds(i * 8, 8)].reshape(128, 384))
        base = (dot_nn(high, perm[...]) + dot_nn(low, perm[...])).reshape(8, 16, PAIRS)
        for j in range(8):
            g = i * 8 + j
            rows = slot_rows(slots, g)
            placed_z = placed(16, rows[4:5].astype(jnp.int32), spline(rows[7:8]))
            both = [placed_z * lanes(charge[v][j * 4 : j * 4 + 4]) for v in range(2)]
            z_high, z_low = split(jnp.concatenate(both, 0))
            re, im = site_waves(freq, (rows[2:3], rows[3:4] + block), (rows[5:6], rows[6:7]), steps[...])
            x_re, x_im = re[0:8], im[0:8]
            y_re = [re[8 + k : 9 + k] for k in range(8)] + [re[20 + k : 21 + k] for k in range(4)]
            y_im = [im[8 + k : 9 + k] for k in range(8)] + [im[20 + k : 21 + k] for k in range(4)]
            parts_re, parts_im = [], []
            for k in range(KY):
                a, b = y_re[k], y_im[k]
                parts_re.append(a * x_re - b * x_im)
                parts_im.append(a * x_im + b * x_re)
            parts = parts_re + parts_im
            x_re, x_im = (jnp.where(upper, v[16:24], pltpu.roll(v[16:24], 4, 0)) for v in (re, im))
            parts_re, parts_im = [], []
            for k in range(0, KY, 2):
                a = jnp.where(upper, y_re[k], y_re[k + 1])
                b = jnp.where(upper, y_im[k], y_im[k + 1])
                parts_re.append(a * x_re - b * x_im)
                parts_im.append(a * x_im + b * x_re)
            high, low = split(jnp.concatenate(parts + parts_re + parts_im, 0))
            total = dot_nt(jnp.concatenate([z_high, z_low], 0), high)
            total = total[:32] + total[32:] + dot_nt(z_high, low)
            out[g, 0:16] = total[:16] + base[j]
            out[g, 16:32] = total[16:]
        return carry

    lax.fori_loop(0, 4, group, 0)


def late_waves(*operands):
    return pl.pallas_call(
        late_body,
        out_shape=(
            jax.ShapeDtypeStruct((N_FFT, 32, PAIRS), F32),
            jax.ShapeDtypeStruct((8, 128), F32),
        ),
        scratch_shapes=[
            pltpu.VMEM((128, 128), F32),
            pltpu.VMEM((128, 128), F32),
            pltpu.VMEM((2, 128, 128), F32),
        ],
        compiler_params=pltpu.CompilerParams(vmem_limit_bytes=SOME),
        cost_estimate=pl.CostEstimate(flops=5_000_000_000, bytes_accessed=7_000_000, transcendentals=0),
        name="late_waves",
    )(*operands)


def z_body(ml, quads, rest, waves, out_re, out_im, out_q):
    m5 = jnp.sum(quads[:, 0, :], 0, keepdims=True)
    step = guarded(rest[3:4], m5 - rest[2:3], m5)[:, 0:1]
    total = ml[:, 0:16] + step[None] * ml[:, 16:32]
    both = split(total.reshape(N_FFT * 16, PAIRS))
    cos = three(dot_tn, both, (waves[0], waves[1]))
    sin = three(dot_tn, both, (waves[2], waves[3]))
    for k in range(KY):
        for first, count, re in ((0, 8, k * 8), (8, 4, 192 + k * 4)):
            im = re + KY * count
            out_re[k, first : first + count] = cos[re : re + count] + sin[im : im + count]
            out_im[k, first : first + count] = cos[im : im + count] - sin[re : re + count]
    out_q[...] = (rest[0:1] + step * rest[1:2])[:, 0:OWN]


def along_z(*operands):
    shape = jax.ShapeDtypeStruct((KY, KX, NG), F32)
    return pl.pallas_call(
        z_body,
        out_shape=(shape, shape, jax.ShapeDtypeStruct((1, OWN), F32)),
        compiler_params=pltpu.CompilerParams(vmem_limit_bytes=SOME),
        cost_estimate=pl.CostEstimate(flops=3_000_000_000, bytes_accessed=5_000_000, transcendentals=0),
        name="along_z",
    )(*operands)


def swap(value, axis):
    return lax.all_to_all(value, axis, 0, 0, tiled=True)


def on_device(
    ml_pos,
    ml_width,
    ml_drive,
    ml_hard,
    mm_charge,
    mm_frac,
    mm_cell,
    slot_atom,
    slot_frac,
    slot_cell,
):
    f = lax.axis_index("fft")
    s = lax.axis_index("slab")

    sent, near = pack(ml_drive, slot_atom, slot_cell, slot_frac, ml_hard, ml_pos, ml_width)
    got = swap(sent, "slab")
    matrix = couple(near)
    got_1 = swap(first_product(got, matrix), "fft")
    mm = spread(mm_charge, mm_frac, mm_cell, jnp.asarray(np.stack(two_parts(x_table()))))
    first_cols = jnp.sum(got_1[:, :8], 0)
    part = jnp.sum(matrix * first_cols.reshape(1, COLS), 1)
    tail = jnp.concatenate([part.reshape(4, 128), first_cols[:4], first_cols[4:]], 1)
    tail = jnp.broadcast_to(tail[None], (N_SLAB, 4, 384))
    got_2 = swap(jnp.concatenate([mm[:, : YE - 4], tail], 1), "slab")
    first_full = jnp.concatenate([got_2[:, YE - 4 :, 128:256], got_2[:, YE - 4 :, 256:]], 1)
    first_full = jnp.transpose(first_full.reshape(N_SLAB, N_FFT, OWN), (1, 0, 2)).reshape(128, 128)

    arh, arl, aih, ail = (jnp.asarray(t) for half in y_tables() for t in two_parts(half))
    got_3 = swap(along_y(got_2, matrix, jnp.asarray(perm_y()), arh, arl, aih, ail), "fft")
    quads = swap(quad_sum(got_3), "slab")

    steps_x = lax.dynamic_index_in_dim(jnp.asarray(step_table(N_SLAB)), s, 0, False)
    steps_y = lax.dynamic_index_in_dim(jnp.asarray(step_table(N_FFT)), f, 0, False)
    steps = jnp.concatenate([steps_x[:8], steps_y[:8], steps_x[8:], steps_y[8:]], 0)
    before = early(got_1, first_full)
    ml, rest = late_waves(got_1, before, first_full, got_3, jnp.asarray(perm_z()), steps)
    z_waves = jnp.asarray(np.stack([t for half in z_tables() for t in two_parts(half)]))
    struct_re, struct_im, charge = along_z(ml, quads, rest, z_waves)
    return (charge.reshape(OWN), struct_re, struct_im)


def solution(mesh):
    return jax.shard_map(
        on_device,
        mesh=mesh,
        in_specs=(
            P(),
            P(),
            P(("fft", "slab")),
            P(("fft", "slab")),
            P(("fft", "slab")),
            P(None, ("fft", "slab")),
            P(None, ("fft", "slab")),
            P(("fft", "slab")),
            P(None, ("fft", "slab")),
            P(None, ("fft", "slab")),
        ),
        out_specs=(P(("fft", "slab")), P("fft", "slab", None), P("fft", "slab", None)),
        check_vma=False,
    )
```

```python
import math

import jax
import jax.numpy as jnp
import numpy as np
from jax import lax
from jax.experimental import pallas as pl
from jax.experimental.pallas import tpu as pltpu
from jax.sharding import PartitionSpec as P

NG = 384
N_FFT = 32
N_SLAB = 16
YL = 24
ZL = 12
KX = 12
KY = 12
OWN = 32
ROWS = 512
COLS = 1024
ATOMS = 16384
SITES = 6144
CHUNK = 1024
XE = 392
YE = 32
ZE = 15
PAIRS = 288

KE = 14.4
ALPHA = 0.08
SOFT = 0.01
SQPI = math.sqrt(math.pi)
F32 = jnp.float32
BF16 = jnp.bfloat16
MOST = 60 * 1024 * 1024
SOME = 12 * 1024 * 1024


def wave(points, freqs):
    angle = 2.0 * np.pi * ((points[:, None] * freqs[None, :]) % NG) / NG
    return np.cos(angle), np.sin(angle)


def two_parts(table):
    high = np.asarray(table, np.float32).astype(jnp.bfloat16)
    low = (np.asarray(table, np.float64) - high.astype(np.float64)).astype(jnp.bfloat16)
    return high, low


def x_table():
    points = np.arange(XE)
    cos, sin = wave(points, np.arange(NG // 2))
    cos, sin = (t.reshape(XE, N_SLAB, 1, KX) for t in (cos, sin))
    table = np.concatenate([cos, -sin], 2)
    table = table * (points < NG + 3)[:, None, None, None]
    return table.reshape(XE, N_SLAB * 2 * KX)


def y_tables():
    local = np.arange(YE)
    points = (np.arange(N_SLAB)[:, None] * YL + local[None, :]).reshape(-1)
    used = np.tile(local < YL + 3, N_SLAB)[:, None, None, None]
    cos, sin = wave(points, np.arange(NG))
    cos, sin = (t.reshape(-1, N_FFT, 1, KY) for t in (cos, sin))
    from_re = np.concatenate([cos, -sin], 2) * used
    from_im = np.concatenate([sin, cos], 2) * used
    return from_re.reshape(-1, 2 * NG), from_im.reshape(-1, 2 * NG)


def z_tables():
    local = np.arange(16)
    points = (np.arange(N_FFT)[:, None] * ZL + local[None, :]).reshape(-1)
    used = np.tile(local < ZL + 3, N_FFT)[:, None]
    scale = 1.0 / (NG * math.sqrt(NG))
    cos, sin = wave(points, np.arange(NG))
    return cos * used * scale, sin * used * scale


def perm_y():
    table = np.zeros((2, KX, 16, 384), np.float32)
    for c in range(2):
        for k in range(KX):
            for z in range(ZE):
                table[c, k, z, z * 24 + c * KX + k] = 1.0
    return table.reshape(384, 384).astype(jnp.bfloat16)


def perm_z():
    table = np.zeros((384, PAIRS), np.float32)
    for c in range(2):
        for k in range(KY):
            for x in range(KX):
                column = c * 96 + k * 8 + x if x < 8 else 192 + c * 48 + k * 4 + x - 8
                table[x * 24 + c * KY + k, column] = 1.0
    return table.astype(jnp.bfloat16)


def step_table(count):
    freqs = (np.arange(count) * 12)[:, None] + np.arange(12)[None, :]
    angle = 2.0 * np.pi * freqs[:, :, None] * np.arange(4)[None, None, :] / NG
    return np.concatenate([np.cos(angle), -np.sin(angle)], 2).astype(np.float32)


def my_place():
    return lax.axis_index("fft"), lax.axis_index("slab")


def split(value):
    high = value.astype(BF16)
    return high, (value - high.astype(F32)).astype(BF16)


def dot_nn(a, b):
    return lax.dot_general(a, b, (((1,), (0,)), ((), ())), preferred_element_type=F32)


def dot_nt(a, b):
    return lax.dot_general(a, b, (((1,), (1,)), ((), ())), preferred_element_type=F32)


def dot_tn(a, b):
    return lax.dot_general(a, b, (((0,), (0,)), ((), ())), preferred_element_type=F32)


def three(dot, a, b):
    return dot(a[0], b[0]) + dot(a[0], b[1]) + dot(a[1], b[0])


def spline(u):
    squared = u * u
    cubed = squared * u
    rest = 1.0 - u
    return (
        rest * rest * rest / 6.0,
        (3.0 * cubed - 6.0 * squared + 4.0) / 6.0,
        (-3.0 * cubed + 3.0 * squared + 3.0 * u + 1.0) / 6.0,
        cubed / 6.0,
    )


def placed(rows, cell, weights):
    off = lax.broadcasted_iota(jnp.int32, (rows, cell.shape[1]), 0) - cell
    value = jnp.where(off == 3, weights[3], 0.0)
    value = jnp.where(off == 2, weights[2], value)
    value = jnp.where(off == 1, weights[1], value)
    return jnp.where(off == 0, weights[0], value)


def spread_body(charge, frac, cell, waves_from, out, acc, waves, sem):
    step = pl.program_id(0)
    copy = pltpu.make_async_copy(waves_from, waves, sem)

    @pl.when(step == 0)
    def _():
        copy.start()
        acc[...] = jnp.zeros_like(acc)

    along_x = placed(XE, cell[0:1, :], spline(frac[0:1, :]))
    along_y = placed(YE, cell[1:2, :], spline(frac[1:2, :])) * charge[...]
    along_z = placed(16, cell[2:3, :], spline(frac[2:3, :]))
    plane = jnp.concatenate([along_z[z : z + 1, :] * along_y for z in range(ZE)], 0)
    acc[...] += three(dot_nt, split(along_x), split(plane))

    @pl.when(step == pl.num_programs(0) - 1)
    def _():
        copy.wait()
        freq = three(dot_tn, split(acc[...]), (waves[0], waves[1]))
        for s in range(N_SLAB):
            for z in range(ZE):
                out[s, :, z * 24 : z * 24 + 24] = freq[z * YE : z * YE + YE, s * 24 : s * 24 + 24]
            out[s, :, ZE * 24 : 384] = jnp.zeros((YE, 384 - ZE * 24), F32)


def spread(charge, frac, cell, waves):
    return pl.pallas_call(
        spread_body,
        grid=(SITES // CHUNK,),
        in_specs=[
            pl.BlockSpec((1, CHUNK), lambda i: (0, i)),
            pl.BlockSpec((3, CHUNK), lambda i: (0, i)),
            pl.BlockSpec((3, CHUNK), lambda i: (0, i)),
            pl.BlockSpec(memory_space=pltpu.HBM),
        ],
        out_specs=pl.BlockSpec((N_SLAB, YE, 384), lambda i: (0, 0, 0)),
        out_shape=jax.ShapeDtypeStruct((N_SLAB, YE, 384), F32),
        scratch_shapes=[
            pltpu.VMEM((XE, ZE * YE), F32),
            pltpu.VMEM((2, XE, 384), BF16),
            pltpu.SemaphoreType.DMA,
        ],
        compiler_params=pltpu.CompilerParams(vmem_limit_bytes=MOST),
        cost_estimate=pl.CostEstimate(flops=8_000_000_000, bytes_accessed=2_000_000, transcendentals=0),
        name="spread",
    )(charge.reshape(1, SITES), frac, cell, waves)


def lanes(tiles):
    return jnp.concatenate([tiles[i : i + 1] for i in range(tiles.shape[0])], 1)


def pack_body(drive, atom, cell, frac, hard, pos, width, out, near, picked):
    f, s = my_place()
    out[...] = jnp.zeros_like(out)
    for i in range(N_SLAB):
        out[i, 0:1, 0:OWN] = -drive[...]
        out[i, 1:2, 0:OWN] = atom[...].astype(F32)
        out[i, 2:5, 0:OWN] = cell[...].astype(F32)
        out[i, 5:8, 0:OWN] = frac[...]
    for j in range(N_FFT):
        at = pl.multiple_of(j * ROWS + (s >> 2) * 128, 128)
        picked[j, 0:3, :] = pos[:, pl.ds(at, 128)]
        picked[j, 3:4, :] = width[:, pl.ds(at, 128)]
    lane = lax.broadcasted_iota(jnp.int32, (8, 128), 1) >> 5
    for tile in range(COLS // 128):
        value = jnp.zeros((8, 128), F32)
        for j in range(4):
            value = jnp.where(lane == j, pltpu.roll(picked[tile * 4 + j], ((j - (s & 3)) & 3) * OWN, 1), value)
        near[:, tile * 128 : tile * 128 + 128] = value
    at = pl.multiple_of(f * ROWS, 128)
    near[:, COLS:] = jnp.zeros((8, ROWS), F32)
    near[0:3, COLS:] = pos[:, pl.ds(at, ROWS)]
    near[3:4, COLS:] = width[:, pl.ds(at, ROWS)]
    near[4:5, COLS : COLS + OWN] = hard[...]


def pack(drive, atom, cell, frac, hard, pos, width):
    return pl.pallas_call(
        pack_body,
        out_shape=(
            jax.ShapeDtypeStruct((N_SLAB, 8, 128), F32),
            jax.ShapeDtypeStruct((8, COLS + ROWS), F32),
        ),
        scratch_shapes=[pltpu.VMEM((N_FFT, 8, 128), F32)],
        compiler_params=pltpu.CompilerParams(vmem_limit_bytes=MOST),
        name="pack",
    )(
        drive.reshape(1, OWN),
        atom.reshape(1, OWN),
        cell,
        frac,
        hard.reshape(1, OWN),
        pos,
        width.reshape(1, ATOMS),
    )


def erf_ratio(value):
    square = value * value
    p = 0.00022905065861350646
    for c in (0.0034082910107109506, 0.050955695062380861, 0.18520832239976145, 1.128379143519084):
        p = p * square + c
    q = -1.1791602954361697e-7
    for c in (
        0.000023547966471313185,
        0.0010179625278914885,
        0.014070470171167667,
        0.11098505178285362,
        0.49746925110067538,
        1.0,
    ):
        q = q * square + c
    return value * p, q


def couple_body(near, out, own):
    f, s = my_place()
    cols = near[:, :COLS]
    side = jnp.transpose(near[:, COLS:])
    own[...] = jnp.zeros_like(own)
    own[0:1, 0:OWN] = near[4:5, COLS : COLS + OWN]
    own_hard = pltpu.roll(own[...], (f & 3) * OWN, 1)[0:1]
    diag = jnp.concatenate([jnp.where((f >> 2) == t, own_hard, 0.0) for t in range(COLS // 128)], 1)
    diag = diag + KE * (1.0 / (cols[3:4] * SQPI) - 2.0 * ALPHA / SQPI)
    col_id = lax.broadcasted_iota(jnp.int32, (1, COLS), 1) - f * OWN
    col_id = jnp.where((col_id >= 0) & (col_id < OWN), col_id + s * OWN, -1)
    col_sq = 2.0 * cols[3:4] * cols[3:4]
    step = 16
    for first in range(0, ROWS, step):
        here = side[first : first + step]
        square = SOFT
        for i in range(3):
            gap = here[:, i : i + 1] - cols[i : i + 1]
            square = square + gap * gap
        inverse = lax.rsqrt(square)
        distance = square * inverse
        narrow = lax.rsqrt(2.0 * here[:, 3:4] * here[:, 3:4] + col_sq)
        p1, q1 = erf_ratio(jnp.minimum(distance * narrow, 3.832506856900711))
        p2, q2 = erf_ratio(jnp.minimum(distance * ALPHA, 3.832506856900711))
        value = KE * inverse * ((p1 * q2 - p2 * q1) / (q1 * q2))
        row_id = first + lax.broadcasted_iota(jnp.int32, (step, 1), 0)
        out[first : first + step] = jnp.where(row_id == col_id, diag, value)


def couple(near):
    return pl.pallas_call(
        couple_body,
        out_shape=jax.ShapeDtypeStruct((ROWS, COLS), F32),
        scratch_shapes=[pltpu.VMEM((8, 128), F32)],
        compiler_params=pltpu.CompilerParams(vmem_limit_bytes=SOME),
        cost_estimate=pl.CostEstimate(flops=100_000_000, bytes_accessed=2_000_000, transcendentals=1_000_000),
        name="couple",
    )(near)


def first_body(got, matrix, out, slots):
    for s in range(N_SLAB):
        slots[:, s * OWN : s * OWN + OWN] = got[s, :, 0:OWN]
    every = slots[...]
    part = jnp.sum(matrix[...] * jnp.transpose(every)[:, 0:1], 0, keepdims=True)
    for i in range(8):
        out[0, i : i + 1, :] = part[:, i * 128 : i * 128 + 128]
    for i in range(4):
        out[0, 8 + i * 8 : 16 + i * 8, :] = every[:, i * 128 : i * 128 + 128]
    whole = out[0]
    for f in range(1, N_FFT):
        out[f] = whole


def first_product(got, matrix):
    return pl.pallas_call(
        first_body,
        out_shape=jax.ShapeDtypeStruct((N_FFT, 40, 128), F32),
        scratch_shapes=[pltpu.VMEM((8, ROWS), F32)],
        compiler_params=pltpu.CompilerParams(vmem_limit_bytes=SOME),
        name="first_product",
    )(got, matrix)


def y_body(grid, matrix, perm, arh, arl, aih, ail, out, side):
    got = grid[...]
    rows = jnp.sum(got[:, YE - 4 :, 0:128], 0)
    side[0:4, :] = rows
    turned = jnp.transpose(side[...])
    column = jnp.concatenate([turned[:, i : i + 1] for i in range(4)], 0)
    part = jnp.sum(matrix[...] * column, 0, keepdims=True)
    high, low = split(got.reshape(N_SLAB * YE, 384))
    high = dot_nt(perm[...], high).astype(BF16)
    low = dot_nt(perm[...], low).astype(BF16)
    freq = three(dot_nn, (high[:192], low[:192]), (arh[...], arl[...]))
    freq = freq + three(dot_nn, (high[192:], low[192:]), (aih[...], ail[...]))
    for i in range(16):
        out[0, i : i + 1, 288:320] = part[:, i * OWN : i * OWN + OWN]
        out[0, i : i + 1, 320:352] = part[:, ROWS + i * OWN : ROWS + i * OWN + OWN]
        out[0, i : i + 1, 352:384] = rows[i // 4 : i // 4 + 1, i % 4 * OWN : i % 4 * OWN + OWN]
    extra = out[0, :, 256:384]
    for f in range(N_FFT):
        if f > 0:
            out[f, :, 256:384] = extra
        for k in range(KX):
            out[f, :, k * 24 : k * 24 + 24] = freq[k * 16 : k * 16 + 16, f * 24 : f * 24 + 24]


def along_y(*operands):
    return pl.pallas_call(
        y_body,
        out_shape=jax.ShapeDtypeStruct((N_FFT, 16, 384), F32),
        scratch_shapes=[pltpu.VMEM((8, 128), F32)],
        compiler_params=pltpu.CompilerParams(vmem_limit_bytes=2 * SOME),
        cost_estimate=pl.CostEstimate(flops=4_000_000_000, bytes_accessed=5_000_000, transcendentals=0),
        name="along_y",
    )(*operands)


def quad_body(got, out):
    s = my_place()[1]
    third = jnp.sum(got[:, :, 32:96], 0)
    second = got[:, pl.ds(s, 1), 96:128].reshape(N_FFT, OWN)
    total = jnp.sum(third[:, 0:OWN] * second[0:16] + third[:, OWN:] * second[16:], 0, keepdims=True)
    total = jnp.sum(total, 1, keepdims=True)
    out[...] = jnp.broadcast_to(total[None], out.shape)


def quad_sum(got):
    return pl.pallas_call(
        quad_body,
        grid=(1,),
        in_specs=[
            pl.BlockSpec((N_FFT, 16, 128), lambda i: (0, 0, 2)),
        ],
        out_specs=pl.BlockSpec((N_SLAB, 8, 128), lambda i: (0, 0, 0)),
        out_shape=jax.ShapeDtypeStruct((N_SLAB, 8, 128), F32),
        compiler_params=pltpu.CompilerParams(vmem_limit_bytes=SOME),
        name="quad_sum",
    )(got)


def unit(turns):
    half = (turns - 0.5) * math.pi
    square = half * half
    sine = 0.0
    for power in (11, 9, 7, 5, 3):
        sine = (sine + (-1.0) ** (power // 2) / math.factorial(power)) * square
    sine = half * (1.0 + sine)
    cosine = 0.0
    for power in (12, 10, 8, 6, 4, 2):
        cosine = (cosine + (-1.0) ** (power // 2) / math.factorial(power)) * square
    cosine = 1.0 + cosine
    return 2.0 * sine * sine - 1.0, 2.0 * sine * cosine


def site_waves(freq, base, fraction, steps):
    upper = lax.broadcasted_iota(jnp.int32, (8, 1), 0) < 4

    def in_rows(x, y):
        wide = [jnp.broadcast_to(v, (8, ROWS)) for v in (x, y)]
        return jnp.concatenate(wide + [jnp.where(upper, x, y)], 0)

    phase = freq * in_rows(*base)
    phase = phase - NG * jnp.floor(phase * (1.0 / NG))
    re, im = unit(phase * (1.0 / NG))
    weights = [in_rows(x, y) for x, y in zip(spline(fraction[0]), spline(fraction[1]), strict=True)]
    w_re = sum(steps[:, i : i + 1] * weights[i] for i in range(4))
    w_im = sum(steps[:, 4 + i : 5 + i] * weights[i] for i in range(1, 4))
    return re * w_re - im * w_im, re * w_im + im * w_re


def slot_rows(slots, g):
    return jnp.concatenate([slots[g, 8 + i * 8 : 16 + i * 8, :] for i in range(4)], 1)


def guarded(value, pivot, scale):
    good = pivot > 1e-6 * scale
    return jnp.where(good, value / jnp.where(good, pivot, 1.0), 0.0)


def lookup(tables, atom):
    index = lax.broadcasted_iota(jnp.int32, (128, atom.shape[1]), 0)
    pick = jnp.where(index == (atom & 127), 1.0, 0.0).astype(BF16)
    rows = dot_nn(tables, jnp.concatenate([pick, pick], 0))
    here = index == (atom >> 7)
    count = rows.shape[0] // 128
    return [
        jnp.sum(jnp.where(here, rows[v * 128 : v * 128 + 128], 0.0), 0, keepdims=True) for v in range(count)
    ]


def early_body(slots, first, out, v0):
    for i in range(4):
        v0[pl.ds(i, N_FFT, stride=4), :] = slots[:, 8 + i * 8, :]
    both = jnp.concatenate([v0[...], first[...]], 0)
    high, low = split(both)
    both = jnp.concatenate([high, low], 1)
    for g in range(N_FFT):
        found = lookup(both, slot_rows(slots, g)[1:2].astype(jnp.int32))
        for v in range(2):
            for i in range(4):
                out[v, g * 4 + i : g * 4 + i + 1, :] = found[v][:, i * 128 : i * 128 + 128]


def early(slots, first):
    return pl.pallas_call(
        early_body,
        out_shape=jax.ShapeDtypeStruct((2, 128, 128), F32),
        scratch_shapes=[pltpu.VMEM((128, 128), F32)],
        compiler_params=pltpu.CompilerParams(vmem_limit_bytes=SOME),
        cost_estimate=pl.CostEstimate(flops=2_000_000_000, bytes_accessed=1_000_000, transcendentals=0),
        name="early",
    )(slots, first)


def ml_group(i, slots, charges, grid, perm, steps, store):
    f, s = my_place()
    upper = lax.broadcasted_iota(jnp.int32, (8, 1), 0) < 4
    block = (lax.broadcasted_iota(jnp.int32, (1, ROWS), 1) // OWN * YL).astype(F32)
    local = lax.broadcasted_iota(jnp.int32, (24, 1), 0)
    freq = jnp.where(local < 8, s * KX + local, f * KY + local - 8)
    freq = jnp.where(local < 16, freq, jnp.where(local < 20, s * KX + local - 8, f * KY + local - 12)).astype(F32)
    at = pl.multiple_of(i * 32, 32)
    charge = [charges[v, pl.ds(at, 32), :] for v in range(2)]
    high, low = split(grid[pl.ds(i * 8, 8)].reshape(128, 384))
    base = (dot_nn(high, perm[...]) + dot_nn(low, perm[...])).reshape(8, 16, PAIRS)
    for j in range(8):
        g = i * 8 + j
        rows = slot_rows(slots, g)
        placed_z = placed(16, rows[4:5].astype(jnp.int32), spline(rows[7:8]))
        both = [placed_z * lanes(charge[v][j * 4 : j * 4 + 4]) for v in range(2)]
        z_high, z_low = split(jnp.concatenate(both, 0))
        re, im = site_waves(freq, (rows[2:3], rows[3:4] + block), (rows[5:6], rows[6:7]), steps[...])
        x_re, x_im = re[0:8], im[0:8]
        y_re = [re[8 + k : 9 + k] for k in range(8)] + [re[20 + k : 21 + k] for k in range(4)]
        y_im = [im[8 + k : 9 + k] for k in range(8)] + [im[20 + k : 21 + k] for k in range(4)]
        parts_re, parts_im = [], []
        for k in range(KY):
            a, b = y_re[k], y_im[k]
            parts_re.append(a * x_re - b * x_im)
            parts_im.append(a * x_im + b * x_re)
        parts = parts_re + parts_im
        x_re, x_im = (jnp.where(upper, v[16:24], pltpu.roll(v[16:24], 4, 0)) for v in (re, im))
        parts_re, parts_im = [], []
        for k in range(0, KY, 2):
            a = jnp.where(upper, y_re[k], y_re[k + 1])
            b = jnp.where(upper, y_im[k], y_im[k + 1])
            parts_re.append(a * x_re - b * x_im)
            parts_im.append(a * x_im + b * x_re)
        high, low = split(jnp.concatenate(parts + parts_re + parts_im, 0))
        total = dot_nt(jnp.concatenate([z_high, z_low], 0), high)
        total = total[:32] + total[32:] + dot_nt(z_high, low)
        store(g, total[:16] + base[j], total[16:])


def solve_body(slots, before, first, grid, perm, steps, out, rest, charges, v2, late):
    f, s = my_place()
    for i in range(4):
        pieces = [grid[:, i * 4 + j, 352:384] for j in range(4)]
        v2[pl.ds(i, N_FFT, stride=4), :] = jnp.concatenate(pieces, 1)
    high, low = split(v2[...])
    both = jnp.concatenate([high, low], 1)
    for g in range(N_FFT):
        found = lookup(both, slot_rows(slots, g)[1:2].astype(jnp.int32))[0]
        for i in range(4):
            late[g * 4 + i : g * 4 + i + 1, :] = found[:, i * 128 : i * 128 + 128]

    def dot(a, b):
        return jnp.sum(jnp.sum(a * b, 0, keepdims=True), 1, keepdims=True)

    a, b, c = before[0], before[1], late[...]
    m0, m1, m2, m3, m4 = dot(a, a), dot(a, b), dot(b, b), dot(b, c), dot(c, c)
    l10 = m2 / m1
    l20 = m3 / m1
    d1 = m3 - l10 * m2
    e12 = m4 - l10 * m3
    l21 = guarded(e12, d1, m3)
    g1 = m1 - l10 * m0
    g2 = (m2 - l20 * m0) - l21 * g1
    c1 = guarded(g1, d1, m3)
    c0 = m0 / m1 - l10 * c1
    charges[0] = c0 * a + c1 * b
    charges[1] = c - l21 * b + (l10 * l21 - l20) * a
    at = f * 4 + (s >> 2)
    rest[...] = jnp.zeros_like(rest)
    own = [slots[pl.ds(f, 1), 8 + i * 8, :] for i in range(4)]
    a = sum(jnp.where((s >> 2) == i, own[i], 0.0) for i in range(4))
    b, c = first[pl.ds(at, 1), :], v2[pl.ds(at, 1), :]
    rest[0:1] = c0 * a + c1 * b
    rest[1:2] = c - l21 * b + (l10 * l21 - l20) * a
    rest[...] = pltpu.roll(rest[...], ((4 - (s & 3)) & 3) * OWN, 1)
    rest[2:3] = jnp.broadcast_to(l20 * m3 + l21 * e12, (1, 128))
    rest[3:4] = jnp.broadcast_to(g2, (1, 128))

    def store(g, base, last):
        out[g, 0:16] = base
        out[g, 16:32] = last

    def group(i, carry):
        ml_group(i, slots, charges, grid, perm, steps, store)
        return carry

    lax.fori_loop(0, 2, group, 0)


def solve(*operands):
    return pl.pallas_call(
        solve_body,
        out_shape=(
            jax.ShapeDtypeStruct((N_FFT // 2, 32, PAIRS), F32),
            jax.ShapeDtypeStruct((8, 128), F32),
            jax.ShapeDtypeStruct((2, 128, 128), F32),
        ),
        scratch_shapes=[pltpu.VMEM((128, 128), F32), pltpu.VMEM((128, 128), F32)],
        compiler_params=pltpu.CompilerParams(vmem_limit_bytes=SOME),
        cost_estimate=pl.CostEstimate(flops=5_000_000_000, bytes_accessed=4_000_000, transcendentals=0),
        name="solve",
    )(*operands)


def last_step(quads, rest):
    m5 = jnp.sum(quads[:, 0, :], 0, keepdims=True)
    return guarded(rest[3:4], m5 - rest[2:3], m5)[:, 0:1]


def join_body(slots, charges, grid, perm, steps, early_half, quads, rest, out, out_q):
    step = last_step(quads, rest)
    half = N_FFT // 2
    out[0:half] = early_half[:, 0:16] + step[None] * early_half[:, 16:32]
    out_q[...] = (rest[0:1] + step * rest[1:2])[:, 0:OWN]

    def store(g, base, last):
        out[g] = base + step * last

    def group(i, carry):
        ml_group(i, slots, charges, grid, perm, steps, store)
        return carry

    lax.fori_loop(2, 4, group, 0)


def join(*operands):
    return pl.pallas_call(
        join_body,
        out_shape=(
            jax.ShapeDtypeStruct((N_FFT, 16, PAIRS), F32),
            jax.ShapeDtypeStruct((1, OWN), F32),
        ),
        compiler_params=pltpu.CompilerParams(vmem_limit_bytes=SOME),
        cost_estimate=pl.CostEstimate(flops=4_000_000_000, bytes_accessed=4_000_000, transcendentals=0),
        name="join",
    )(*operands)


def z_body(grid, waves, out_re, out_im):
    both = split(grid[...].reshape(N_FFT * 16, PAIRS))
    cos = three(dot_tn, both, (waves[0], waves[1]))
    sin = three(dot_tn, both, (waves[2], waves[3]))
    for k in range(KY):
        for first, count, re in ((0, 8, k * 8), (8, 4, 192 + k * 4)):
            im = re + KY * count
            out_re[k, first : first + count] = cos[re : re + count] + sin[im : im + count]
            out_im[k, first : first + count] = cos[im : im + count] - sin[re : re + count]


def along_z(*operands):
    shape = jax.ShapeDtypeStruct((KY, KX, NG), F32)
    return pl.pallas_call(
        z_body,
        out_shape=(shape, shape),
        compiler_params=pltpu.CompilerParams(vmem_limit_bytes=SOME),
        cost_estimate=pl.CostEstimate(flops=3_000_000_000, bytes_accessed=5_000_000, transcendentals=0),
        name="along_z",
    )(*operands)


def swap(value, axis):
    return lax.all_to_all(value, axis, 0, 0, tiled=True)


def on_device(
    ml_pos,
    ml_width,
    ml_drive,
    ml_hard,
    mm_charge,
    mm_frac,
    mm_cell,
    slot_atom,
    slot_frac,
    slot_cell,
):
    f = lax.axis_index("fft")
    s = lax.axis_index("slab")

    sent, near = pack(ml_drive, slot_atom, slot_cell, slot_frac, ml_hard, ml_pos, ml_width)
    got = swap(sent, "slab")
    matrix = couple(near)
    got_1 = swap(first_product(got, matrix), "fft")
    mm = spread(mm_charge, mm_frac, mm_cell, jnp.asarray(np.stack(two_parts(x_table()))))
    first_cols = jnp.sum(got_1[:, :8], 0)
    part = jnp.sum(matrix * first_cols.reshape(1, COLS), 1)
    tail = jnp.concatenate([part.reshape(4, 128), first_cols[:4], first_cols[4:]], 1)
    tail = jnp.broadcast_to(tail[None], (N_SLAB, 4, 384))
    got_2 = swap(jnp.concatenate([mm[:, : YE - 4], tail], 1), "slab")
    first_full = jnp.concatenate([got_2[:, YE - 4 :, 128:256], got_2[:, YE - 4 :, 256:]], 1)
    first_full = jnp.transpose(first_full.reshape(N_SLAB, N_FFT, OWN), (1, 0, 2)).reshape(128, 128)

    arh, arl, aih, ail = (jnp.asarray(t) for half in y_tables() for t in two_parts(half))
    got_3 = swap(along_y(got_2, matrix, jnp.asarray(perm_y()), arh, arl, aih, ail), "fft")
    quads = swap(quad_sum(got_3), "slab")

    steps_x = lax.dynamic_index_in_dim(jnp.asarray(step_table(N_SLAB)), s, 0, False)
    steps_y = lax.dynamic_index_in_dim(jnp.asarray(step_table(N_FFT)), f, 0, False)
    steps = jnp.concatenate([steps_x[:8], steps_y[:8], steps_x[8:], steps_y[8:]], 0)
    before = early(got_1, first_full)
    perm = jnp.asarray(perm_z())
    half, rest, charges = solve(got_1, before, first_full, got_3, perm, steps)
    total, charge = join(got_1, charges, got_3, perm, steps, half, quads, rest)
    z_waves = jnp.asarray(np.stack([t for part in z_tables() for t in two_parts(part)]))
    struct_re, struct_im = along_z(total, z_waves)
    return (charge.reshape(OWN), struct_re, struct_im)


def solution(mesh):
    return jax.shard_map(
        on_device,
        mesh=mesh,
        in_specs=(
            P(),
            P(),
            P(("fft", "slab")),
            P(("fft", "slab")),
            P(("fft", "slab")),
            P(None, ("fft", "slab")),
            P(None, ("fft", "slab")),
            P(("fft", "slab")),
            P(None, ("fft", "slab")),
            P(None, ("fft", "slab")),
        ),
        out_specs=(P(("fft", "slab")), P("fft", "slab", None), P("fft", "slab", None)),
        check_vma=False,
    )
```

```python
import math

import jax
import jax.numpy as jnp
import numpy as np
from jax import lax
from jax.experimental import pallas as pl
from jax.experimental.pallas import tpu as pltpu
from jax.sharding import PartitionSpec as P

NG = 384
N_FFT = 32
N_SLAB = 16
YL = 24
ZL = 12
KX = 12
KY = 12
OWN = 32
ROWS = 512
COLS = 1024
ATOMS = 16384
SITES = 6144
CHUNK = 1024
XE = 392
YE = 32
ZE = 15
PAIRS = 288

KE = 14.4
ALPHA = 0.08
SOFT = 0.01
SQPI = math.sqrt(math.pi)
F32 = jnp.float32
BF16 = jnp.bfloat16
MOST = 60 * 1024 * 1024
SOME = 12 * 1024 * 1024


def wave(points, freqs):
    angle = 2.0 * np.pi * ((points[:, None] * freqs[None, :]) % NG) / NG
    return np.cos(angle), np.sin(angle)


def two_parts(table):
    high = np.asarray(table, np.float32).astype(jnp.bfloat16)
    low = (np.asarray(table, np.float64) - high.astype(np.float64)).astype(jnp.bfloat16)
    return high, low


def x_table():
    points = np.arange(XE)
    cos, sin = wave(points, np.arange(NG // 2))
    cos, sin = (t.reshape(XE, N_SLAB, 1, KX) for t in (cos, sin))
    table = np.concatenate([cos, -sin], 2)
    table = table * (points < NG + 3)[:, None, None, None]
    return table.reshape(XE, N_SLAB * 2 * KX)


def y_tables():
    local = np.arange(YE)
    points = (np.arange(N_SLAB)[:, None] * YL + local[None, :]).reshape(-1)
    used = np.tile(local < YL + 3, N_SLAB)[:, None, None, None]
    cos, sin = wave(points, np.arange(NG))
    cos, sin = (t.reshape(-1, N_FFT, 1, KY) for t in (cos, sin))
    from_re = np.concatenate([cos, -sin], 2) * used
    from_im = np.concatenate([sin, cos], 2) * used
    return from_re.reshape(-1, 2 * NG), from_im.reshape(-1, 2 * NG)


def z_tables():
    local = np.arange(16)
    points = (np.arange(N_FFT)[:, None] * ZL + local[None, :]).reshape(-1)
    used = np.tile(local < ZL + 3, N_FFT)[:, None]
    scale = 1.0 / (NG * math.sqrt(NG))
    cos, sin = wave(points, np.arange(NG))
    return cos * used * scale, sin * used * scale


def perm_y():
    table = np.zeros((2, KX, 16, 384), np.float32)
    for c in range(2):
        for k in range(KX):
            for z in range(ZE):
                table[c, k, z, z * 24 + c * KX + k] = 1.0
    return table.reshape(384, 384).astype(jnp.bfloat16)


def perm_z():
    table = np.zeros((384, PAIRS), np.float32)
    for c in range(2):
        for k in range(KY):
            for x in range(KX):
                column = c * 96 + k * 8 + x if x < 8 else 192 + c * 48 + k * 4 + x - 8
                table[x * 24 + c * KY + k, column] = 1.0
    return table.astype(jnp.bfloat16)


def step_table(count):
    freqs = (np.arange(count) * 12)[:, None] + np.arange(12)[None, :]
    angle = 2.0 * np.pi * freqs[:, :, None] * np.arange(4)[None, None, :] / NG
    return np.concatenate([np.cos(angle), -np.sin(angle)], 2).astype(np.float32)


def my_place():
    return lax.axis_index("fft"), lax.axis_index("slab")


def split(value):
    high = value.astype(BF16)
    return high, (value - high.astype(F32)).astype(BF16)


def dot_nn(a, b):
    return lax.dot_general(a, b, (((1,), (0,)), ((), ())), preferred_element_type=F32)


def dot_nt(a, b):
    return lax.dot_general(a, b, (((1,), (1,)), ((), ())), preferred_element_type=F32)


def dot_tn(a, b):
    return lax.dot_general(a, b, (((0,), (0,)), ((), ())), preferred_element_type=F32)


def three(dot, a, b):
    return dot(a[0], b[0]) + dot(a[0], b[1]) + dot(a[1], b[0])


def spline(u):
    squared = u * u
    cubed = squared * u
    rest = 1.0 - u
    return (
        rest * rest * rest / 6.0,
        (3.0 * cubed - 6.0 * squared + 4.0) / 6.0,
        (-3.0 * cubed + 3.0 * squared + 3.0 * u + 1.0) / 6.0,
        cubed / 6.0,
    )


def placed(rows, cell, weights):
    off = lax.broadcasted_iota(jnp.int32, (rows, cell.shape[1]), 0) - cell
    value = jnp.where(off == 3, weights[3], 0.0)
    value = jnp.where(off == 2, weights[2], value)
    value = jnp.where(off == 1, weights[1], value)
    return jnp.where(off == 0, weights[0], value)


def spread_body(charge, frac, cell, waves_from, out, acc, waves, sem):
    step = pl.program_id(0)
    copy = pltpu.make_async_copy(waves_from, waves, sem)

    @pl.when(step == 0)
    def _():
        copy.start()
        acc[...] = jnp.zeros_like(acc)

    along_x = placed(XE, cell[0:1, :], spline(frac[0:1, :]))
    along_y = placed(YE, cell[1:2, :], spline(frac[1:2, :])) * charge[...]
    along_z = placed(16, cell[2:3, :], spline(frac[2:3, :]))
    plane = jnp.concatenate([along_z[z : z + 1, :] * along_y for z in range(ZE)], 0)
    acc[...] += three(dot_nt, split(along_x), split(plane))

    @pl.when(step == pl.num_programs(0) - 1)
    def _():
        copy.wait()
        freq = three(dot_tn, split(acc[...]), (waves[0], waves[1]))
        for s in range(N_SLAB):
            for z in range(ZE):
                out[s, :, z * 24 : z * 24 + 24] = freq[z * YE : z * YE + YE, s * 24 : s * 24 + 24]
            out[s, :, ZE * 24 : 384] = jnp.zeros((YE, 384 - ZE * 24), F32)


def spread(charge, frac, cell, waves):
    return pl.pallas_call(
        spread_body,
        grid=(SITES // CHUNK,),
        in_specs=[
            pl.BlockSpec((1, CHUNK), lambda i: (0, i)),
            pl.BlockSpec((3, CHUNK), lambda i: (0, i)),
            pl.BlockSpec((3, CHUNK), lambda i: (0, i)),
            pl.BlockSpec(memory_space=pltpu.HBM),
        ],
        out_specs=pl.BlockSpec((N_SLAB, YE, 384), lambda i: (0, 0, 0)),
        out_shape=jax.ShapeDtypeStruct((N_SLAB, YE, 384), F32),
        scratch_shapes=[
            pltpu.VMEM((XE, ZE * YE), F32),
            pltpu.VMEM((2, XE, 384), BF16),
            pltpu.SemaphoreType.DMA,
        ],
        compiler_params=pltpu.CompilerParams(vmem_limit_bytes=MOST),
        cost_estimate=pl.CostEstimate(flops=8_000_000_000, bytes_accessed=2_000_000, transcendentals=0),
        name="spread",
    )(charge.reshape(1, SITES), frac, cell, waves)


def lanes(tiles):
    return jnp.concatenate([tiles[i : i + 1] for i in range(tiles.shape[0])], 1)


def pack_body(drive, atom, cell, frac, hard, pos, width, out, near, picked):
    f, s = my_place()
    out[...] = jnp.zeros_like(out)
    for i in range(N_SLAB):
        out[i, 0:1, 0:OWN] = -drive[...]
        out[i, 1:2, 0:OWN] = atom[...].astype(F32)
        out[i, 2:5, 0:OWN] = cell[...].astype(F32)
        out[i, 5:8, 0:OWN] = frac[...]
    for j in range(N_FFT):
        at = pl.multiple_of(j * ROWS + (s >> 2) * 128, 128)
        picked[j, 0:3, :] = pos[:, pl.ds(at, 128)]
        picked[j, 3:4, :] = width[:, pl.ds(at, 128)]
    lane = lax.broadcasted_iota(jnp.int32, (8, 128), 1) >> 5
    for tile in range(COLS // 128):
        value = jnp.zeros((8, 128), F32)
        for j in range(4):
            value = jnp.where(lane == j, pltpu.roll(picked[tile * 4 + j], ((j - (s & 3)) & 3) * OWN, 1), value)
        near[:, tile * 128 : tile * 128 + 128] = value
    at = pl.multiple_of(f * ROWS, 128)
    near[:, COLS:] = jnp.zeros((8, ROWS), F32)
    near[0:3, COLS:] = pos[:, pl.ds(at, ROWS)]
    near[3:4, COLS:] = width[:, pl.ds(at, ROWS)]
    near[4:5, COLS : COLS + OWN] = hard[...]


def pack(drive, atom, cell, frac, hard, pos, width):
    return pl.pallas_call(
        pack_body,
        out_shape=(
            jax.ShapeDtypeStruct((N_SLAB, 8, 128), F32),
            jax.ShapeDtypeStruct((8, COLS + ROWS), F32),
        ),
        scratch_shapes=[pltpu.VMEM((N_FFT, 8, 128), F32)],
        compiler_params=pltpu.CompilerParams(vmem_limit_bytes=MOST),
        name="pack",
    )(
        drive.reshape(1, OWN),
        atom.reshape(1, OWN),
        cell,
        frac,
        hard.reshape(1, OWN),
        pos,
        width.reshape(1, ATOMS),
    )


def erf_ratio(value):
    square = value * value
    p = 0.00022905065861350646
    for c in (0.0034082910107109506, 0.050955695062380861, 0.18520832239976145, 1.128379143519084):
        p = p * square + c
    q = -1.1791602954361697e-7
    for c in (
        0.000023547966471313185,
        0.0010179625278914885,
        0.014070470171167667,
        0.11098505178285362,
        0.49746925110067538,
        1.0,
    ):
        q = q * square + c
    return value * p, q


def couple_body(near, out, own):
    f, s = my_place()
    cols = near[:, :COLS]
    side = jnp.transpose(near[:, COLS:])
    own[...] = jnp.zeros_like(own)
    own[0:1, 0:OWN] = near[4:5, COLS : COLS + OWN]
    own_hard = pltpu.roll(own[...], (f & 3) * OWN, 1)[0:1]
    diag = jnp.concatenate([jnp.where((f >> 2) == t, own_hard, 0.0) for t in range(COLS // 128)], 1)
    diag = diag + KE * (1.0 / (cols[3:4] * SQPI) - 2.0 * ALPHA / SQPI)
    col_id = lax.broadcasted_iota(jnp.int32, (1, COLS), 1) - f * OWN
    col_id = jnp.where((col_id >= 0) & (col_id < OWN), col_id + s * OWN, -1)
    col_sq = 2.0 * cols[3:4] * cols[3:4]
    step = 16
    for first in range(0, ROWS, step):
        here = side[first : first + step]
        square = SOFT
        for i in range(3):
            gap = here[:, i : i + 1] - cols[i : i + 1]
            square = square + gap * gap
        inverse = lax.rsqrt(square)
        distance = square * inverse
        narrow = lax.rsqrt(2.0 * here[:, 3:4] * here[:, 3:4] + col_sq)
        p1, q1 = erf_ratio(jnp.minimum(distance * narrow, 3.832506856900711))
        p2, q2 = erf_ratio(jnp.minimum(distance * ALPHA, 3.832506856900711))
        value = KE * inverse * ((p1 * q2 - p2 * q1) / (q1 * q2))
        row_id = first + lax.broadcasted_iota(jnp.int32, (step, 1), 0)
        out[first : first + step] = jnp.where(row_id == col_id, diag, value)


def couple(near):
    return pl.pallas_call(
        couple_body,
        out_shape=jax.ShapeDtypeStruct((ROWS, COLS), F32),
        scratch_shapes=[pltpu.VMEM((8, 128), F32)],
        compiler_params=pltpu.CompilerParams(vmem_limit_bytes=SOME),
        cost_estimate=pl.CostEstimate(flops=100_000_000, bytes_accessed=2_000_000, transcendentals=1_000_000),
        name="couple",
    )(near)


def first_body(got, matrix, out, slots):
    for s in range(N_SLAB):
        slots[:, s * OWN : s * OWN + OWN] = got[s, :, 0:OWN]
    every = slots[...]
    part = jnp.sum(matrix[...] * jnp.transpose(every)[:, 0:1], 0, keepdims=True)
    for i in range(8):
        out[0, i : i + 1, :] = part[:, i * 128 : i * 128 + 128]
    for i in range(4):
        out[0, 8 + i * 8 : 16 + i * 8, :] = every[:, i * 128 : i * 128 + 128]
    whole = out[0]
    for f in range(1, N_FFT):
        out[f] = whole


def first_product(got, matrix):
    return pl.pallas_call(
        first_body,
        out_shape=jax.ShapeDtypeStruct((N_FFT, 40, 128), F32),
        scratch_shapes=[pltpu.VMEM((8, ROWS), F32)],
        compiler_params=pltpu.CompilerParams(vmem_limit_bytes=SOME),
        name="first_product",
    )(got, matrix)


def y_body(grid, matrix, perm, arh, arl, aih, ail, out, side):
    got = grid[...]
    rows = jnp.sum(got[:, YE - 4 :, 0:128], 0)
    side[0:4, :] = rows
    turned = jnp.transpose(side[...])
    column = jnp.concatenate([turned[:, i : i + 1] for i in range(4)], 0)
    part = jnp.sum(matrix[...] * column, 0, keepdims=True)
    high, low = split(got.reshape(N_SLAB * YE, 384))
    high = dot_nt(perm[...], high).astype(BF16)
    low = dot_nt(perm[...], low).astype(BF16)
    freq = three(dot_nn, (high[:192], low[:192]), (arh[...], arl[...]))
    freq = freq + three(dot_nn, (high[192:], low[192:]), (aih[...], ail[...]))
    for i in range(16):
        out[0, i : i + 1, 288:320] = part[:, i * OWN : i * OWN + OWN]
        out[0, i : i + 1, 320:352] = part[:, ROWS + i * OWN : ROWS + i * OWN + OWN]
        out[0, i : i + 1, 352:384] = rows[i // 4 : i // 4 + 1, i % 4 * OWN : i % 4 * OWN + OWN]
    extra = out[0, :, 256:384]
    for f in range(N_FFT):
        if f > 0:
            out[f, :, 256:384] = extra
        for k in range(KX):
            out[f, :, k * 24 : k * 24 + 24] = freq[k * 16 : k * 16 + 16, f * 24 : f * 24 + 24]


def along_y(*operands):
    return pl.pallas_call(
        y_body,
        out_shape=jax.ShapeDtypeStruct((N_FFT, 16, 384), F32),
        scratch_shapes=[pltpu.VMEM((8, 128), F32)],
        compiler_params=pltpu.CompilerParams(vmem_limit_bytes=2 * SOME),
        cost_estimate=pl.CostEstimate(flops=4_000_000_000, bytes_accessed=5_000_000, transcendentals=0),
        name="along_y",
    )(*operands)


def quad_body(got, out):
    s = my_place()[1]
    third = jnp.sum(got[:, :, 32:96], 0)
    second = got[:, pl.ds(s, 1), 96:128].reshape(N_FFT, OWN)
    total = jnp.sum(third[:, 0:OWN] * second[0:16] + third[:, OWN:] * second[16:], 0, keepdims=True)
    total = jnp.sum(total, 1, keepdims=True)
    out[...] = jnp.broadcast_to(total[None], out.shape)


def quad_sum(got):
    return pl.pallas_call(
        quad_body,
        grid=(1,),
        in_specs=[
            pl.BlockSpec((N_FFT, 16, 128), lambda i: (0, 0, 2)),
        ],
        out_specs=pl.BlockSpec((N_SLAB, 8, 128), lambda i: (0, 0, 0)),
        out_shape=jax.ShapeDtypeStruct((N_SLAB, 8, 128), F32),
        compiler_params=pltpu.CompilerParams(vmem_limit_bytes=SOME),
        name="quad_sum",
    )(got)


def unit(turns):
    half = (turns - 0.5) * math.pi
    square = half * half
    sine = 0.0
    for power in (11, 9, 7, 5, 3):
        sine = (sine + (-1.0) ** (power // 2) / math.factorial(power)) * square
    sine = half * (1.0 + sine)
    cosine = 0.0
    for power in (12, 10, 8, 6, 4, 2):
        cosine = (cosine + (-1.0) ** (power // 2) / math.factorial(power)) * square
    cosine = 1.0 + cosine
    return 2.0 * sine * sine - 1.0, 2.0 * sine * cosine


def site_waves(freq, base, fraction, steps):
    upper = lax.broadcasted_iota(jnp.int32, (8, 1), 0) < 4

    def in_rows(x, y):
        wide = [jnp.broadcast_to(v, (8, ROWS)) for v in (x, y)]
        return jnp.concatenate(wide + [jnp.where(upper, x, y)], 0)

    phase = freq * in_rows(*base)
    phase = phase - NG * jnp.floor(phase * (1.0 / NG))
    re, im = unit(phase * (1.0 / NG))
    weights = [in_rows(x, y) for x, y in zip(spline(fraction[0]), spline(fraction[1]), strict=True)]
    w_re = sum(steps[:, i : i + 1] * weights[i] for i in range(4))
    w_im = sum(steps[:, 4 + i : 5 + i] * weights[i] for i in range(1, 4))
    return re * w_re - im * w_im, re * w_im + im * w_re


def slot_rows(slots, g):
    return jnp.concatenate([slots[g, 8 + i * 8 : 16 + i * 8, :] for i in range(4)], 1)


def guarded(value, pivot, scale):
    good = pivot > 1e-6 * scale
    return jnp.where(good, value / jnp.where(good, pivot, 1.0), 0.0)


def lookup(tables, atom):
    index = lax.broadcasted_iota(jnp.int32, (128, atom.shape[1]), 0)
    pick = jnp.where(index == (atom & 127), 1.0, 0.0).astype(BF16)
    rows = dot_nn(tables, jnp.concatenate([pick, pick], 0))
    here = index == (atom >> 7)
    count = rows.shape[0] // 128
    return [
        jnp.sum(jnp.where(here, rows[v * 128 : v * 128 + 128], 0.0), 0, keepdims=True) for v in range(count)
    ]


def early_body(slots, first, steps, out, ready_0, ready_2, v0):
    waves = phases(steps)
    for ready, start in ((ready_0, 0), (ready_2, 16)):
        for j in range(8):
            ready[j, 0:24], ready[j, 24:48] = waves(j, slot_rows(slots, start + j))
    for i in range(4):
        v0[pl.ds(i, N_FFT, stride=4), :] = slots[:, 8 + i * 8, :]
    both = jnp.concatenate([v0[...], first[...]], 0)
    high, low = split(both)
    both = jnp.concatenate([high, low], 1)
    for g in range(N_FFT):
        found = lookup(both, slot_rows(slots, g)[1:2].astype(jnp.int32))
        for v in range(2):
            for i in range(4):
                out[v, g * 4 + i : g * 4 + i + 1, :] = found[v][:, i * 128 : i * 128 + 128]


def early(slots, first, steps):
    return pl.pallas_call(
        early_body,
        out_shape=(
            jax.ShapeDtypeStruct((2, 128, 128), F32),
            jax.ShapeDtypeStruct((8, 48, ROWS), F32),
            jax.ShapeDtypeStruct((8, 48, ROWS), F32),
        ),
        scratch_shapes=[pltpu.VMEM((128, 128), F32)],
        compiler_params=pltpu.CompilerParams(vmem_limit_bytes=SOME),
        cost_estimate=pl.CostEstimate(flops=2_000_000_000, bytes_accessed=1_000_000, transcendentals=0),
        name="early",
    )(slots, first, steps)


def phases(steps):
    f, s = my_place()
    block = (lax.broadcasted_iota(jnp.int32, (1, ROWS), 1) // OWN * YL).astype(F32)
    local = lax.broadcasted_iota(jnp.int32, (24, 1), 0)
    freq = jnp.where(local < 8, s * KX + local, f * KY + local - 8)
    freq = jnp.where(local < 16, freq, jnp.where(local < 20, s * KX + local - 8, f * KY + local - 12)).astype(F32)

    def waves(_, rows):
        return site_waves(freq, (rows[2:3], rows[3:4] + block), (rows[5:6], rows[6:7]), steps[...])

    return waves


def kept(ref):
    return lambda j, _: (ref[j, 0:24], ref[j, 24:48])


def ml_group(i, slots, charges, grid, perm, waves, store):
    upper = lax.broadcasted_iota(jnp.int32, (8, 1), 0) < 4
    at = pl.multiple_of(i * 32, 32)
    charge = [charges[v, pl.ds(at, 32), :] for v in range(2)]
    high, low = split(grid[pl.ds(i * 8, 8)].reshape(128, 384))
    base = (dot_nn(high, perm[...]) + dot_nn(low, perm[...])).reshape(8, 16, PAIRS)
    for j in range(8):
        g = i * 8 + j
        rows = slot_rows(slots, g)
        placed_z = placed(16, rows[4:5].astype(jnp.int32), spline(rows[7:8]))
        both = [placed_z * lanes(charge[v][j * 4 : j * 4 + 4]) for v in range(2)]
        z_high, z_low = split(jnp.concatenate(both, 0))
        re, im = waves(j, rows)
        x_re, x_im = re[0:8], im[0:8]
        y_re = [re[8 + k : 9 + k] for k in range(8)] + [re[20 + k : 21 + k] for k in range(4)]
        y_im = [im[8 + k : 9 + k] for k in range(8)] + [im[20 + k : 21 + k] for k in range(4)]
        parts_re, parts_im = [], []
        for k in range(KY):
            a, b = y_re[k], y_im[k]
            parts_re.append(a * x_re - b * x_im)
            parts_im.append(a * x_im + b * x_re)
        parts = parts_re + parts_im
        x_re, x_im = (jnp.where(upper, v[16:24], pltpu.roll(v[16:24], 4, 0)) for v in (re, im))
        parts_re, parts_im = [], []
        for k in range(0, KY, 2):
            a = jnp.where(upper, y_re[k], y_re[k + 1])
            b = jnp.where(upper, y_im[k], y_im[k + 1])
            parts_re.append(a * x_re - b * x_im)
            parts_im.append(a * x_im + b * x_re)
        high, low = split(jnp.concatenate(parts + parts_re + parts_im, 0))
        total = dot_nt(jnp.concatenate([z_high, z_low], 0), high)
        total = total[:32] + total[32:] + dot_nt(z_high, low)
        store(g, total[:16] + base[j], total[16:])


def solve_body(slots, before, first, grid, perm, steps, ready, out, rest, charges, v2, late):
    f, s = my_place()
    for i in range(4):
        pieces = [grid[:, i * 4 + j, 352:384] for j in range(4)]
        v2[pl.ds(i, N_FFT, stride=4), :] = jnp.concatenate(pieces, 1)
    high, low = split(v2[...])
    both = jnp.concatenate([high, low], 1)
    for g in range(N_FFT):
        found = lookup(both, slot_rows(slots, g)[1:2].astype(jnp.int32))[0]
        for i in range(4):
            late[g * 4 + i : g * 4 + i + 1, :] = found[:, i * 128 : i * 128 + 128]

    def dot(a, b):
        return jnp.sum(jnp.sum(a * b, 0, keepdims=True), 1, keepdims=True)

    a, b, c = before[0], before[1], late[...]
    m0, m1, m2, m3, m4 = dot(a, a), dot(a, b), dot(b, b), dot(b, c), dot(c, c)
    l10 = m2 / m1
    l20 = m3 / m1
    d1 = m3 - l10 * m2
    e12 = m4 - l10 * m3
    l21 = guarded(e12, d1, m3)
    g1 = m1 - l10 * m0
    g2 = (m2 - l20 * m0) - l21 * g1
    c1 = guarded(g1, d1, m3)
    c0 = m0 / m1 - l10 * c1
    charges[0] = c0 * a + c1 * b
    charges[1] = c - l21 * b + (l10 * l21 - l20) * a
    at = f * 4 + (s >> 2)
    rest[...] = jnp.zeros_like(rest)
    own = [slots[pl.ds(f, 1), 8 + i * 8, :] for i in range(4)]
    a = sum(jnp.where((s >> 2) == i, own[i], 0.0) for i in range(4))
    b, c = first[pl.ds(at, 1), :], v2[pl.ds(at, 1), :]
    rest[0:1] = c0 * a + c1 * b
    rest[1:2] = c - l21 * b + (l10 * l21 - l20) * a
    rest[...] = pltpu.roll(rest[...], ((4 - (s & 3)) & 3) * OWN, 1)
    rest[2:3] = jnp.broadcast_to(l20 * m3 + l21 * e12, (1, 128))
    rest[3:4] = jnp.broadcast_to(g2, (1, 128))

    def store(g, base, last):
        out[g, 0:16] = base
        out[g, 16:32] = last

    ml_group(0, slots, charges, grid, perm, kept(ready), store)
    ml_group(1, slots, charges, grid, perm, phases(steps), store)


def solve(*operands):
    return pl.pallas_call(
        solve_body,
        out_shape=(
            jax.ShapeDtypeStruct((N_FFT // 2, 32, PAIRS), F32),
            jax.ShapeDtypeStruct((8, 128), F32),
            jax.ShapeDtypeStruct((2, 128, 128), F32),
        ),
        scratch_shapes=[pltpu.VMEM((128, 128), F32), pltpu.VMEM((128, 128), F32)],
        compiler_params=pltpu.CompilerParams(vmem_limit_bytes=SOME),
        cost_estimate=pl.CostEstimate(flops=5_000_000_000, bytes_accessed=4_000_000, transcendentals=0),
        name="solve",
    )(*operands)


def last_step(quads, rest):
    m5 = jnp.sum(quads[:, 0, :], 0, keepdims=True)
    return guarded(rest[3:4], m5 - rest[2:3], m5)[:, 0:1]


def join_body(slots, charges, grid, perm, steps, ready, early_half, quads, rest, out, out_q):
    step = last_step(quads, rest)
    half = N_FFT // 2
    out[0:half] = early_half[:, 0:16] + step[None] * early_half[:, 16:32]
    out_q[...] = (rest[0:1] + step * rest[1:2])[:, 0:OWN]

    def store(g, base, last):
        out[g] = base + step * last

    ml_group(2, slots, charges, grid, perm, kept(ready), store)
    ml_group(3, slots, charges, grid, perm, phases(steps), store)


def join(*operands):
    return pl.pallas_call(
        join_body,
        out_shape=(
            jax.ShapeDtypeStruct((N_FFT, 16, PAIRS), F32),
            jax.ShapeDtypeStruct((1, OWN), F32),
        ),
        compiler_params=pltpu.CompilerParams(vmem_limit_bytes=SOME),
        cost_estimate=pl.CostEstimate(flops=4_000_000_000, bytes_accessed=4_000_000, transcendentals=0),
        name="join",
    )(*operands)


def z_body(grid, waves, out_re, out_im):
    both = split(grid[...].reshape(N_FFT * 16, PAIRS))
    cos = three(dot_tn, both, (waves[0], waves[1]))
    sin = three(dot_tn, both, (waves[2], waves[3]))
    for k in range(KY):
        for first, count, re in ((0, 8, k * 8), (8, 4, 192 + k * 4)):
            im = re + KY * count
            out_re[k, first : first + count] = cos[re : re + count] + sin[im : im + count]
            out_im[k, first : first + count] = cos[im : im + count] - sin[re : re + count]


def along_z(*operands):
    shape = jax.ShapeDtypeStruct((KY, KX, NG), F32)
    return pl.pallas_call(
        z_body,
        out_shape=(shape, shape),
        compiler_params=pltpu.CompilerParams(vmem_limit_bytes=SOME),
        cost_estimate=pl.CostEstimate(flops=3_000_000_000, bytes_accessed=5_000_000, transcendentals=0),
        name="along_z",
    )(*operands)


def swap(value, axis):
    return lax.all_to_all(value, axis, 0, 0, tiled=True)


def on_device(
    ml_pos,
    ml_width,
    ml_drive,
    ml_hard,
    mm_charge,
    mm_frac,
    mm_cell,
    slot_atom,
    slot_frac,
    slot_cell,
):
    f = lax.axis_index("fft")
    s = lax.axis_index("slab")

    sent, near = pack(ml_drive, slot_atom, slot_cell, slot_frac, ml_hard, ml_pos, ml_width)
    got = swap(sent, "slab")
    matrix = couple(near)
    got_1 = swap(first_product(got, matrix), "fft")
    mm = spread(mm_charge, mm_frac, mm_cell, jnp.asarray(np.stack(two_parts(x_table()))))
    first_cols = jnp.sum(got_1[:, :8], 0)
    part = jnp.sum(matrix * first_cols.reshape(1, COLS), 1)
    tail = jnp.concatenate([part.reshape(4, 128), first_cols[:4], first_cols[4:]], 1)
    tail = jnp.broadcast_to(tail[None], (N_SLAB, 4, 384))
    got_2 = swap(jnp.concatenate([mm[:, : YE - 4], tail], 1), "slab")
    first_full = jnp.concatenate([got_2[:, YE - 4 :, 128:256], got_2[:, YE - 4 :, 256:]], 1)
    first_full = jnp.transpose(first_full.reshape(N_SLAB, N_FFT, OWN), (1, 0, 2)).reshape(128, 128)

    arh, arl, aih, ail = (jnp.asarray(t) for half in y_tables() for t in two_parts(half))
    got_3 = swap(along_y(got_2, matrix, jnp.asarray(perm_y()), arh, arl, aih, ail), "fft")
    quads = swap(quad_sum(got_3), "slab")

    steps_x = lax.dynamic_index_in_dim(jnp.asarray(step_table(N_SLAB)), s, 0, False)
    steps_y = lax.dynamic_index_in_dim(jnp.asarray(step_table(N_FFT)), f, 0, False)
    steps = jnp.concatenate([steps_x[:8], steps_y[:8], steps_x[8:], steps_y[8:]], 0)
    before, ready_0, ready_2 = early(got_1, first_full, steps)
    perm = jnp.asarray(perm_z())
    half, rest, charges = solve(got_1, before, first_full, got_3, perm, steps, ready_0)
    total, charge = join(got_1, charges, got_3, perm, steps, ready_2, half, quads, rest)
    z_waves = jnp.asarray(np.stack([t for part in z_tables() for t in two_parts(part)]))
    struct_re, struct_im = along_z(total, z_waves)
    return (charge.reshape(OWN), struct_re, struct_im)


def solution(mesh):
    return jax.shard_map(
        on_device,
        mesh=mesh,
        in_specs=(
            P(),
            P(),
            P(("fft", "slab")),
            P(("fft", "slab")),
            P(("fft", "slab")),
            P(None, ("fft", "slab")),
            P(None, ("fft", "slab")),
            P(("fft", "slab")),
            P(None, ("fft", "slab")),
            P(None, ("fft", "slab")),
        ),
        out_specs=(P(("fft", "slab")), P("fft", "slab", None), P("fft", "slab", None)),
        check_vma=False,
    )
```

```python
import math

import jax
import jax.numpy as jnp
import numpy as np
from jax import lax
from jax.experimental import pallas as pl
from jax.experimental.pallas import tpu as pltpu
from jax.sharding import PartitionSpec as P

NG = 384
N_FFT = 32
N_SLAB = 16
YL = 24
ZL = 12
KX = 12
KY = 12
OWN = 32
ROWS = 512
COLS = 1024
ATOMS = 16384
SITES = 6144
CHUNK = 1024
XE = 392
YE = 32
ZE = 15
PAIRS = 288

KE = 14.4
ALPHA = 0.08
SOFT = 0.01
SQPI = math.sqrt(math.pi)
F32 = jnp.float32
BF16 = jnp.bfloat16
MOST = 60 * 1024 * 1024
SOME = 12 * 1024 * 1024


def wave(points, freqs):
    angle = 2.0 * np.pi * ((points[:, None] * freqs[None, :]) % NG) / NG
    return np.cos(angle), np.sin(angle)


def two_parts(table):
    high = np.asarray(table, np.float32).astype(jnp.bfloat16)
    low = (np.asarray(table, np.float64) - high.astype(np.float64)).astype(jnp.bfloat16)
    return high, low


def x_table():
    points = np.arange(XE)
    cos, sin = wave(points, np.arange(NG // 2))
    cos, sin = (t.reshape(XE, N_SLAB, 1, KX) for t in (cos, sin))
    table = np.concatenate([cos, -sin], 2)
    table = table * (points < NG + 3)[:, None, None, None]
    return table.reshape(XE, N_SLAB * 2 * KX)


def y_tables():
    local = np.arange(YE)
    points = (np.arange(N_SLAB)[:, None] * YL + local[None, :]).reshape(-1)
    used = np.tile(local < YL + 3, N_SLAB)[:, None, None, None]
    cos, sin = wave(points, np.arange(NG))
    cos, sin = (t.reshape(-1, N_FFT, 1, KY) for t in (cos, sin))
    from_re = np.concatenate([cos, -sin], 2) * used
    from_im = np.concatenate([sin, cos], 2) * used
    return from_re.reshape(-1, 2 * NG), from_im.reshape(-1, 2 * NG)


def z_tables():
    local = np.arange(16)
    points = (np.arange(N_FFT)[:, None] * ZL + local[None, :]).reshape(-1)
    used = np.tile(local < ZL + 3, N_FFT)[:, None]
    scale = 1.0 / (NG * math.sqrt(NG))
    cos, sin = wave(points, np.arange(NG))
    return cos * used * scale, sin * used * scale


def perm_y():
    table = np.zeros((2, KX, 16, 384), np.float32)
    for c in range(2):
        for k in range(KX):
            for z in range(ZE):
                table[c, k, z, z * 24 + c * KX + k] = 1.0
    return table.reshape(384, 384).astype(jnp.bfloat16)


def perm_z():
    table = np.zeros((384, PAIRS), np.float32)
    for c in range(2):
        for k in range(KY):
            for x in range(KX):
                column = c * 96 + k * 8 + x if x < 8 else 192 + c * 48 + k * 4 + x - 8
                table[x * 24 + c * KY + k, column] = 1.0
    return table.astype(jnp.bfloat16)


def step_table(count):
    freqs = (np.arange(count) * 12)[:, None] + np.arange(12)[None, :]
    angle = 2.0 * np.pi * freqs[:, :, None] * np.arange(4)[None, None, :] / NG
    return np.concatenate([np.cos(angle), -np.sin(angle)], 2).astype(np.float32)


def my_place():
    return lax.axis_index("fft"), lax.axis_index("slab")


def split(value):
    high = value.astype(BF16)
    return high, (value - high.astype(F32)).astype(BF16)


def dot_nn(a, b):
    return lax.dot_general(a, b, (((1,), (0,)), ((), ())), preferred_element_type=F32)


def dot_nt(a, b):
    return lax.dot_general(a, b, (((1,), (1,)), ((), ())), preferred_element_type=F32)


def dot_tn(a, b):
    return lax.dot_general(a, b, (((0,), (0,)), ((), ())), preferred_element_type=F32)


def three(dot, a, b):
    return dot(a[0], b[0]) + dot(a[0], b[1]) + dot(a[1], b[0])


def spline(u):
    squared = u * u
    cubed = squared * u
    rest = 1.0 - u
    return (
        rest * rest * rest / 6.0,
        (3.0 * cubed - 6.0 * squared + 4.0) / 6.0,
        (-3.0 * cubed + 3.0 * squared + 3.0 * u + 1.0) / 6.0,
        cubed / 6.0,
    )


def placed(rows, cell, weights):
    off = lax.broadcasted_iota(jnp.int32, (rows, cell.shape[1]), 0) - cell
    value = jnp.where(off == 3, weights[3], 0.0)
    value = jnp.where(off == 2, weights[2], value)
    value = jnp.where(off == 1, weights[1], value)
    return jnp.where(off == 0, weights[0], value)


def spread_body(charge, frac, cell, waves_from, out, acc, waves, sem):
    step = pl.program_id(0)
    copy = pltpu.make_async_copy(waves_from, waves, sem)

    @pl.when(step == 0)
    def _():
        copy.start()
        acc[...] = jnp.zeros_like(acc)

    along_x = placed(XE, cell[0:1, :], spline(frac[0:1, :]))
    along_y = placed(YE, cell[1:2, :], spline(frac[1:2, :])) * charge[...]
    along_z = placed(16, cell[2:3, :], spline(frac[2:3, :]))
    plane = jnp.concatenate([along_z[z : z + 1, :] * along_y for z in range(ZE)], 0)
    acc[...] += three(dot_nt, split(along_x), split(plane))

    @pl.when(step == pl.num_programs(0) - 1)
    def _():
        copy.wait()
        freq = three(dot_tn, split(acc[...]), (waves[0], waves[1]))
        for s in range(N_SLAB):
            for z in range(ZE):
                out[s, :, z * 24 : z * 24 + 24] = freq[z * YE : z * YE + YE, s * 24 : s * 24 + 24]
            out[s, :, ZE * 24 : 384] = jnp.zeros((YE, 384 - ZE * 24), F32)


def spread(charge, frac, cell, waves):
    return pl.pallas_call(
        spread_body,
        grid=(SITES // CHUNK,),
        in_specs=[
            pl.BlockSpec((1, CHUNK), lambda i: (0, i)),
            pl.BlockSpec((3, CHUNK), lambda i: (0, i)),
            pl.BlockSpec((3, CHUNK), lambda i: (0, i)),
            pl.BlockSpec(memory_space=pltpu.HBM),
        ],
        out_specs=pl.BlockSpec((N_SLAB, YE, 384), lambda i: (0, 0, 0)),
        out_shape=jax.ShapeDtypeStruct((N_SLAB, YE, 384), F32),
        scratch_shapes=[
            pltpu.VMEM((XE, ZE * YE), F32),
            pltpu.VMEM((2, XE, 384), BF16),
            pltpu.SemaphoreType.DMA,
        ],
        compiler_params=pltpu.CompilerParams(vmem_limit_bytes=MOST),
        cost_estimate=pl.CostEstimate(flops=8_000_000_000, bytes_accessed=2_000_000, transcendentals=0),
        name="spread",
    )(charge.reshape(1, SITES), frac, cell, waves)


def lanes(tiles):
    return jnp.concatenate([tiles[i : i + 1] for i in range(tiles.shape[0])], 1)


def pack_body(drive, atom, cell, frac, out):
    out[...] = jnp.zeros_like(out)
    for i in range(N_SLAB):
        out[i, 0:1, 0:OWN] = -drive[...]
        out[i, 1:2, 0:OWN] = atom[...].astype(F32)
        out[i, 2:5, 0:OWN] = cell[...].astype(F32)
        out[i, 5:8, 0:OWN] = frac[...]


def near_body(hard, pos, width, near, picked):
    f, s = my_place()
    for j in range(N_FFT):
        at = pl.multiple_of(j * ROWS + (s >> 2) * 128, 128)
        picked[j, 0:3, :] = pos[:, pl.ds(at, 128)]
        picked[j, 3:4, :] = width[:, pl.ds(at, 128)]
    lane = lax.broadcasted_iota(jnp.int32, (8, 128), 1) >> 5
    for tile in range(COLS // 128):
        value = jnp.zeros((8, 128), F32)
        for j in range(4):
            value = jnp.where(lane == j, pltpu.roll(picked[tile * 4 + j], ((j - (s & 3)) & 3) * OWN, 1), value)
        near[:, tile * 128 : tile * 128 + 128] = value
    at = pl.multiple_of(f * ROWS, 128)
    near[:, COLS:] = jnp.zeros((8, ROWS), F32)
    near[0:3, COLS:] = pos[:, pl.ds(at, ROWS)]
    near[3:4, COLS:] = width[:, pl.ds(at, ROWS)]
    near[4:5, COLS : COLS + OWN] = hard[...]


def pack(drive, atom, cell, frac):
    return pl.pallas_call(
        pack_body,
        out_shape=jax.ShapeDtypeStruct((N_SLAB, 8, 128), F32),
        compiler_params=pltpu.CompilerParams(vmem_limit_bytes=MOST),
        name="pack",
    )(drive.reshape(1, OWN), atom.reshape(1, OWN), cell, frac)


def near_atoms(hard, pos, width):
    return pl.pallas_call(
        near_body,
        out_shape=jax.ShapeDtypeStruct((8, COLS + ROWS), F32),
        scratch_shapes=[pltpu.VMEM((N_FFT, 8, 128), F32)],
        compiler_params=pltpu.CompilerParams(vmem_limit_bytes=MOST),
        name="near_atoms",
    )(hard.reshape(1, OWN), pos, width.reshape(1, ATOMS))


def erf_ratio(value):
    square = value * value
    p = 0.00022905065861350646
    for c in (0.0034082910107109506, 0.050955695062380861, 0.18520832239976145, 1.128379143519084):
        p = p * square + c
    q = -1.1791602954361697e-7
    for c in (
        0.000023547966471313185,
        0.0010179625278914885,
        0.014070470171167667,
        0.11098505178285362,
        0.49746925110067538,
        1.0,
    ):
        q = q * square + c
    return value * p, q


def couple_body(near, out, own):
    f, s = my_place()
    cols = near[:, :COLS]
    side = jnp.transpose(near[:, COLS:])
    own[...] = jnp.zeros_like(own)
    own[0:1, 0:OWN] = near[4:5, COLS : COLS + OWN]
    own_hard = pltpu.roll(own[...], (f & 3) * OWN, 1)[0:1]
    diag = jnp.concatenate([jnp.where((f >> 2) == t, own_hard, 0.0) for t in range(COLS // 128)], 1)
    diag = diag + KE * (1.0 / (cols[3:4] * SQPI) - 2.0 * ALPHA / SQPI)
    col_id = lax.broadcasted_iota(jnp.int32, (1, COLS), 1) - f * OWN
    col_id = jnp.where((col_id >= 0) & (col_id < OWN), col_id + s * OWN, -1)
    col_sq = 2.0 * cols[3:4] * cols[3:4]
    step = 16
    for first in range(0, ROWS, step):
        here = side[first : first + step]
        square = SOFT
        for i in range(3):
            gap = here[:, i : i + 1] - cols[i : i + 1]
            square = square + gap * gap
        inverse = lax.rsqrt(square)
        distance = square * inverse
        narrow = lax.rsqrt(2.0 * here[:, 3:4] * here[:, 3:4] + col_sq)
        p1, q1 = erf_ratio(jnp.minimum(distance * narrow, 3.832506856900711))
        p2, q2 = erf_ratio(jnp.minimum(distance * ALPHA, 3.832506856900711))
        value = KE * inverse * ((p1 * q2 - p2 * q1) / (q1 * q2))
        row_id = first + lax.broadcasted_iota(jnp.int32, (step, 1), 0)
        out[first : first + step] = jnp.where(row_id == col_id, diag, value)


def couple(near):
    return pl.pallas_call(
        couple_body,
        out_shape=jax.ShapeDtypeStruct((ROWS, COLS), F32),
        scratch_shapes=[pltpu.VMEM((8, 128), F32)],
        compiler_params=pltpu.CompilerParams(vmem_limit_bytes=SOME),
        cost_estimate=pl.CostEstimate(flops=100_000_000, bytes_accessed=2_000_000, transcendentals=1_000_000),
        name="couple",
    )(near)


def first_body(got, matrix, out, slots):
    for s in range(N_SLAB):
        slots[:, s * OWN : s * OWN + OWN] = got[s, :, 0:OWN]
    every = slots[...]
    part = jnp.sum(matrix[...] * jnp.transpose(every)[:, 0:1], 0, keepdims=True)
    for i in range(8):
        out[0, i : i + 1, :] = part[:, i * 128 : i * 128 + 128]
    for i in range(4):
        out[0, 8 + i * 8 : 16 + i * 8, :] = every[:, i * 128 : i * 128 + 128]
    whole = out[0]
    for f in range(1, N_FFT):
        out[f] = whole


def first_product(got, matrix):
    return pl.pallas_call(
        first_body,
        out_shape=jax.ShapeDtypeStruct((N_FFT, 40, 128), F32),
        scratch_shapes=[pltpu.VMEM((8, ROWS), F32)],
        compiler_params=pltpu.CompilerParams(vmem_limit_bytes=SOME),
        name="first_product",
    )(got, matrix)


def y_body(grid, matrix, perm, arh, arl, aih, ail, out, side):
    got = grid[...]
    rows = jnp.sum(got[:, YE - 4 :, 0:128], 0)
    side[0:4, :] = rows
    turned = jnp.transpose(side[...])
    column = jnp.concatenate([turned[:, i : i + 1] for i in range(4)], 0)
    part = jnp.sum(matrix[...] * column, 0, keepdims=True)
    high, low = split(got.reshape(N_SLAB * YE, 384))
    high = dot_nt(perm[...], high).astype(BF16)
    low = dot_nt(perm[...], low).astype(BF16)
    freq = three(dot_nn, (high[:192], low[:192]), (arh[...], arl[...]))
    freq = freq + three(dot_nn, (high[192:], low[192:]), (aih[...], ail[...]))
    for i in range(16):
        out[0, i : i + 1, 288:320] = part[:, i * OWN : i * OWN + OWN]
        out[0, i : i + 1, 320:352] = part[:, ROWS + i * OWN : ROWS + i * OWN + OWN]
        out[0, i : i + 1, 352:384] = rows[i // 4 : i // 4 + 1, i % 4 * OWN : i % 4 * OWN + OWN]
    extra = out[0, :, 256:384]
    for f in range(N_FFT):
        if f > 0:
            out[f, :, 256:384] = extra
        for k in range(KX):
            out[f, :, k * 24 : k * 24 + 24] = freq[k * 16 : k * 16 + 16, f * 24 : f * 24 + 24]


def along_y(*operands):
    return pl.pallas_call(
        y_body,
        out_shape=jax.ShapeDtypeStruct((N_FFT, 16, 384), F32),
        scratch_shapes=[pltpu.VMEM((8, 128), F32)],
        compiler_params=pltpu.CompilerParams(vmem_limit_bytes=2 * SOME),
        cost_estimate=pl.CostEstimate(flops=4_000_000_000, bytes_accessed=5_000_000, transcendentals=0),
        name="along_y",
    )(*operands)


def quad_body(got, out):
    s = my_place()[1]
    third = jnp.sum(got[:, :, 32:96], 0)
    second = got[:, pl.ds(s, 1), 96:128].reshape(N_FFT, OWN)
    total = jnp.sum(third[:, 0:OWN] * second[0:16] + third[:, OWN:] * second[16:], 0, keepdims=True)
    total = jnp.sum(total, 1, keepdims=True)
    out[...] = jnp.broadcast_to(total[None], out.shape)


def quad_sum(got):
    return pl.pallas_call(
        quad_body,
        grid=(1,),
        in_specs=[
            pl.BlockSpec((N_FFT, 16, 128), lambda i: (0, 0, 2)),
        ],
        out_specs=pl.BlockSpec((N_SLAB, 8, 128), lambda i: (0, 0, 0)),
        out_shape=jax.ShapeDtypeStruct((N_SLAB, 8, 128), F32),
        compiler_params=pltpu.CompilerParams(vmem_limit_bytes=SOME),
        name="quad_sum",
    )(got)


def unit(turns):
    half = (turns - 0.5) * math.pi
    square = half * half
    sine = 0.0
    for power in (11, 9, 7, 5, 3):
        sine = (sine + (-1.0) ** (power // 2) / math.factorial(power)) * square
    sine = half * (1.0 + sine)
    cosine = 0.0
    for power in (12, 10, 8, 6, 4, 2):
        cosine = (cosine + (-1.0) ** (power // 2) / math.factorial(power)) * square
    cosine = 1.0 + cosine
    return 2.0 * sine * sine - 1.0, 2.0 * sine * cosine


def site_waves(freq, base, fraction, steps):
    upper = lax.broadcasted_iota(jnp.int32, (8, 1), 0) < 4

    def in_rows(x, y):
        wide = [jnp.broadcast_to(v, (8, ROWS)) for v in (x, y)]
        return jnp.concatenate(wide + [jnp.where(upper, x, y)], 0)

    phase = freq * in_rows(*base)
    phase = phase - NG * jnp.floor(phase * (1.0 / NG))
    re, im = unit(phase * (1.0 / NG))
    weights = [in_rows(x, y) for x, y in zip(spline(fraction[0]), spline(fraction[1]), strict=True)]
    w_re = sum(steps[:, i : i + 1] * weights[i] for i in range(4))
    w_im = sum(steps[:, 4 + i : 5 + i] * weights[i] for i in range(1, 4))
    return re * w_re - im * w_im, re * w_im + im * w_re


def slot_rows(slots, g):
    return jnp.concatenate([slots[g, 8 + i * 8 : 16 + i * 8, :] for i in range(4)], 1)


def guarded(value, pivot, scale):
    good = jnp.abs(pivot) > 1e-6 * jnp.abs(scale)
    return jnp.where(good, value / jnp.where(good, pivot, 1.0), 0.0)


def lookup(tables, atom):
    index = lax.broadcasted_iota(jnp.int32, (128, atom.shape[1]), 0)
    pick = jnp.where(index == (atom & 127), 1.0, 0.0).astype(BF16)
    rows = dot_nn(tables, jnp.concatenate([pick, pick], 0))
    here = index == (atom >> 7)
    count = rows.shape[0] // 128
    return [
        jnp.sum(jnp.where(here, rows[v * 128 : v * 128 + 128], 0.0), 0, keepdims=True) for v in range(count)
    ]


def early_body(slots, first, steps, out, ready, v0):
    waves = phases(steps)
    for j in range(8):
        ready[j, 0:24], ready[j, 24:48] = waves(j, slot_rows(slots, j))
    for i in range(4):
        v0[pl.ds(i, N_FFT, stride=4), :] = slots[:, 8 + i * 8, :]
    both = jnp.concatenate([v0[...], first[...]], 0)
    high, low = split(both)
    both = jnp.concatenate([high, low], 1)
    for g in range(N_FFT):
        found = lookup(both, slot_rows(slots, g)[1:2].astype(jnp.int32))
        for v in range(2):
            for i in range(4):
                out[v, g * 4 + i : g * 4 + i + 1, :] = found[v][:, i * 128 : i * 128 + 128]


def early(slots, first, steps):
    return pl.pallas_call(
        early_body,
        out_shape=(
            jax.ShapeDtypeStruct((2, 128, 128), F32),
            jax.ShapeDtypeStruct((8, 48, ROWS), F32),
        ),
        scratch_shapes=[pltpu.VMEM((128, 128), F32)],
        compiler_params=pltpu.CompilerParams(vmem_limit_bytes=SOME),
        cost_estimate=pl.CostEstimate(flops=2_000_000_000, bytes_accessed=1_000_000, transcendentals=0),
        name="early",
    )(slots, first, steps)


def phases(steps):
    f, s = my_place()
    block = (lax.broadcasted_iota(jnp.int32, (1, ROWS), 1) // OWN * YL).astype(F32)
    local = lax.broadcasted_iota(jnp.int32, (24, 1), 0)
    freq = jnp.where(local < 8, s * KX + local, f * KY + local - 8)
    freq = jnp.where(local < 16, freq, jnp.where(local < 20, s * KX + local - 8, f * KY + local - 12)).astype(F32)

    def waves(_, rows):
        return site_waves(freq, (rows[2:3], rows[3:4] + block), (rows[5:6], rows[6:7]), steps[...])

    return waves


def kept(ref):
    return lambda j, _: (ref[j, 0:24], ref[j, 24:48])


def ml_group(i, slots, charges, grid, perm, waves, store):
    upper = lax.broadcasted_iota(jnp.int32, (8, 1), 0) < 4
    at = pl.multiple_of(i * 32, 32)
    charge = [charges[v, pl.ds(at, 32), :] for v in range(2)]
    high, low = split(grid[pl.ds(i * 8, 8)].reshape(128, 384))
    base = (dot_nn(high, perm[...]) + dot_nn(low, perm[...])).reshape(8, 16, PAIRS)
    for j in range(8):
        g = i * 8 + j
        rows = slot_rows(slots, g)
        placed_z = placed(16, rows[4:5].astype(jnp.int32), spline(rows[7:8]))
        both = [placed_z * lanes(charge[v][j * 4 : j * 4 + 4]) for v in range(2)]
        z_high, z_low = split(jnp.concatenate(both, 0))
        re, im = waves(j, rows)
        x_re, x_im = re[0:8], im[0:8]
        y_re = [re[8 + k : 9 + k] for k in range(8)] + [re[20 + k : 21 + k] for k in range(4)]
        y_im = [im[8 + k : 9 + k] for k in range(8)] + [im[20 + k : 21 + k] for k in range(4)]
        parts_re, parts_im = [], []
        for k in range(KY):
            a, b = y_re[k], y_im[k]
            parts_re.append(a * x_re - b * x_im)
            parts_im.append(a * x_im + b * x_re)
        parts = parts_re + parts_im
        x_re, x_im = (jnp.where(upper, v[16:24], pltpu.roll(v[16:24], 4, 0)) for v in (re, im))
        parts_re, parts_im = [], []
        for k in range(0, KY, 2):
            a = jnp.where(upper, y_re[k], y_re[k + 1])
            b = jnp.where(upper, y_im[k], y_im[k + 1])
            parts_re.append(a * x_re - b * x_im)
            parts_im.append(a * x_im + b * x_re)
        high, low = split(jnp.concatenate(parts + parts_re + parts_im, 0))
        total = dot_nt(jnp.concatenate([z_high, z_low], 0), high)
        total = total[:32] + total[32:] + dot_nt(z_high, low)
        store(g, total[:16] + base[j], total[16:])


def solve_body(slots, before, first, grid, perm, steps, ready, out, rest, charges, v2, late):
    f, s = my_place()
    for i in range(4):
        pieces = [grid[:, i * 4 + j, 352:384] for j in range(4)]
        v2[pl.ds(i, N_FFT, stride=4), :] = jnp.concatenate(pieces, 1)
    high, low = split(v2[...])
    both = jnp.concatenate([high, low], 1)
    for g in range(N_FFT):
        found = lookup(both, slot_rows(slots, g)[1:2].astype(jnp.int32))[0]
        for i in range(4):
            late[g * 4 + i : g * 4 + i + 1, :] = found[:, i * 128 : i * 128 + 128]

    def dot(a, b):
        return jnp.sum(jnp.sum(a * b, 0, keepdims=True), 1, keepdims=True)

    a, b, c = before[0], before[1], late[...]
    m0, m1, m2, m3, m4 = dot(a, a), dot(a, b), dot(b, b), dot(b, c), dot(c, c)
    l10 = m2 / m1
    l20 = m3 / m1
    d1 = m3 - l10 * m2
    e12 = m4 - l10 * m3
    l21 = guarded(e12, d1, m3)
    g1 = m1 - l10 * m0
    g2 = (m2 - l20 * m0) - l21 * g1
    c1 = guarded(g1, d1, m3)
    c0 = m0 / m1 - l10 * c1
    charges[0] = c0 * a + c1 * b
    charges[1] = c - l21 * b + (l10 * l21 - l20) * a
    at = f * 4 + (s >> 2)
    rest[...] = jnp.zeros_like(rest)
    own = [slots[pl.ds(f, 1), 8 + i * 8, :] for i in range(4)]
    a = sum(jnp.where((s >> 2) == i, own[i], 0.0) for i in range(4))
    b, c = first[pl.ds(at, 1), :], v2[pl.ds(at, 1), :]
    rest[0:1] = c0 * a + c1 * b
    rest[1:2] = c - l21 * b + (l10 * l21 - l20) * a
    rest[...] = pltpu.roll(rest[...], ((4 - (s & 3)) & 3) * OWN, 1)
    rest[2:3] = jnp.broadcast_to(l20 * m3 + l21 * e12, (1, 128))
    rest[3:4] = jnp.broadcast_to(g2, (1, 128))

    def store(g, base, last):
        out[g, 0:16] = base
        out[g, 16:32] = last

    ml_group(0, slots, charges, grid, perm, kept(ready), store)
    ml_group(1, slots, charges, grid, perm, phases(steps), store)


def solve(*operands):
    return pl.pallas_call(
        solve_body,
        out_shape=(
            jax.ShapeDtypeStruct((N_FFT // 2, 32, PAIRS), F32),
            jax.ShapeDtypeStruct((8, 128), F32),
            jax.ShapeDtypeStruct((2, 128, 128), F32),
        ),
        scratch_shapes=[pltpu.VMEM((128, 128), F32), pltpu.VMEM((128, 128), F32)],
        compiler_params=pltpu.CompilerParams(vmem_limit_bytes=SOME),
        cost_estimate=pl.CostEstimate(flops=5_000_000_000, bytes_accessed=4_000_000, transcendentals=0),
        name="solve",
    )(*operands)


def last_step(quads, rest):
    m5 = jnp.sum(quads[:, 0, :], 0, keepdims=True)
    return guarded(rest[3:4], m5 - rest[2:3], m5)[:, 0:1]


def join_body(slots, charges, grid, perm, steps, early_half, quads, rest, out, out_q):
    step = last_step(quads, rest)
    half = N_FFT // 2
    out[0:half] = early_half[:, 0:16] + step[None] * early_half[:, 16:32]
    out_q[...] = (rest[0:1] + step * rest[1:2])[:, 0:OWN]

    def store(g, base, last):
        out[g] = base + step * last

    def group(i, carry):
        ml_group(i, slots, charges, grid, perm, phases(steps), store)
        return carry

    lax.fori_loop(2, 4, group, 0)


def join(*operands):
    return pl.pallas_call(
        join_body,
        out_shape=(
            jax.ShapeDtypeStruct((N_FFT, 16, PAIRS), F32),
            jax.ShapeDtypeStruct((1, OWN), F32),
        ),
        compiler_params=pltpu.CompilerParams(vmem_limit_bytes=SOME),
        cost_estimate=pl.CostEstimate(flops=4_000_000_000, bytes_accessed=4_000_000, transcendentals=0),
        name="join",
    )(*operands)


def z_body(grid, waves, out_re, out_im):
    both = split(grid[...].reshape(N_FFT * 16, PAIRS))
    cos = three(dot_tn, both, (waves[0], waves[1]))
    sin = three(dot_tn, both, (waves[2], waves[3]))
    for k in range(KY):
        for first, count, re in ((0, 8, k * 8), (8, 4, 192 + k * 4)):
            im = re + KY * count
            out_re[k, first : first + count] = cos[re : re + count] + sin[im : im + count]
            out_im[k, first : first + count] = cos[im : im + count] - sin[re : re + count]


def along_z(*operands):
    shape = jax.ShapeDtypeStruct((KY, KX, NG), F32)
    return pl.pallas_call(
        z_body,
        out_shape=(shape, shape),
        compiler_params=pltpu.CompilerParams(vmem_limit_bytes=SOME),
        cost_estimate=pl.CostEstimate(flops=3_000_000_000, bytes_accessed=5_000_000, transcendentals=0),
        name="along_z",
    )(*operands)


def swap(value, axis):
    return lax.all_to_all(value, axis, 0, 0, tiled=True)


def on_device(
    ml_pos,
    ml_width,
    ml_drive,
    ml_hard,
    mm_charge,
    mm_frac,
    mm_cell,
    slot_atom,
    slot_frac,
    slot_cell,
):
    f = lax.axis_index("fft")
    s = lax.axis_index("slab")

    got = swap(pack(ml_drive, slot_atom, slot_cell, slot_frac), "slab")
    matrix = couple(near_atoms(ml_hard, ml_pos, ml_width))
    got_1 = swap(first_product(got, matrix), "fft")
    mm = spread(mm_charge, mm_frac, mm_cell, jnp.asarray(np.stack(two_parts(x_table()))))
    first_cols = jnp.sum(got_1[:, :8], 0)
    part = jnp.sum(matrix * first_cols.reshape(1, COLS), 1)
    tail = jnp.concatenate([part.reshape(4, 128), first_cols[:4], first_cols[4:]], 1)
    tail = jnp.broadcast_to(tail[None], (N_SLAB, 4, 384))
    got_2 = swap(jnp.concatenate([mm[:, : YE - 4], tail], 1), "slab")
    first_full = jnp.concatenate([got_2[:, YE - 4 :, 128:256], got_2[:, YE - 4 :, 256:]], 1)
    first_full = jnp.transpose(first_full.reshape(N_SLAB, N_FFT, OWN), (1, 0, 2)).reshape(128, 128)

    arh, arl, aih, ail = (jnp.asarray(t) for half in y_tables() for t in two_parts(half))
    got_3 = swap(along_y(got_2, matrix, jnp.asarray(perm_y()), arh, arl, aih, ail), "fft")
    quads = swap(quad_sum(got_3), "slab")

    steps_x = lax.dynamic_index_in_dim(jnp.asarray(step_table(N_SLAB)), s, 0, False)
    steps_y = lax.dynamic_index_in_dim(jnp.asarray(step_table(N_FFT)), f, 0, False)
    steps = jnp.concatenate([steps_x[:8], steps_y[:8], steps_x[8:], steps_y[8:]], 0)
    before, ready = early(got_1, first_full, steps)
    perm = jnp.asarray(perm_z())
    half, rest, charges = solve(got_1, before, first_full, got_3, perm, steps, ready)
    total, charge = join(got_1, charges, got_3, perm, steps, half, quads, rest)
    z_waves = jnp.asarray(np.stack([t for part in z_tables() for t in two_parts(part)]))
    struct_re, struct_im = along_z(total, z_waves)
    return (charge.reshape(OWN), struct_re, struct_im)


def solution(mesh):
    return jax.shard_map(
        on_device,
        mesh=mesh,
        in_specs=(
            P(),
            P(),
            P(("fft", "slab")),
            P(("fft", "slab")),
            P(("fft", "slab")),
            P(None, ("fft", "slab")),
            P(None, ("fft", "slab")),
            P(("fft", "slab")),
            P(None, ("fft", "slab")),
            P(None, ("fft", "slab")),
        ),
        out_specs=(P(("fft", "slab")), P("fft", "slab", None), P("fft", "slab", None)),
        check_vma=False,
    )
```

```python
import math

import jax
import jax.numpy as jnp
import numpy as np
from jax import lax
from jax.experimental import pallas as pl
from jax.experimental.pallas import tpu as pltpu
from jax.sharding import PartitionSpec as P

NG = 384
N_FFT = 32
N_SLAB = 16
YL = 24
ZL = 12
KX = 12
KY = 12
OWN = 32
ROWS = 512
COLS = 1024
ATOMS = 16384
SITES = 6144
CHUNK = 1024
XE = 392
YE = 32
ZE = 15
PAIRS = 288

KE = 14.4
ALPHA = 0.08
SOFT = 0.01
SQPI = math.sqrt(math.pi)
F32 = jnp.float32
BF16 = jnp.bfloat16
MOST = 60 * 1024 * 1024
SOME = 12 * 1024 * 1024


def wave(points, freqs):
    angle = 2.0 * np.pi * ((points[:, None] * freqs[None, :]) % NG) / NG
    return np.cos(angle), np.sin(angle)


def two_parts(table):
    high = np.asarray(table, np.float32).astype(jnp.bfloat16)
    low = (np.asarray(table, np.float64) - high.astype(np.float64)).astype(jnp.bfloat16)
    return high, low


def x_table():
    points = np.arange(XE)
    cos, sin = wave(points, np.arange(NG // 2))
    cos, sin = (t.reshape(XE, N_SLAB, 1, KX) for t in (cos, sin))
    table = np.concatenate([cos, -sin], 2)
    table = table * (points < NG + 3)[:, None, None, None]
    return table.reshape(XE, N_SLAB * 2 * KX)


def y_tables():
    local = np.arange(YE)
    points = (np.arange(N_SLAB)[:, None] * YL + local[None, :]).reshape(-1)
    used = np.tile(local < YL + 3, N_SLAB)[:, None, None, None]
    cos, sin = wave(points, np.arange(NG))
    cos, sin = (t.reshape(-1, N_FFT, 1, KY) for t in (cos, sin))
    from_re = np.concatenate([cos, -sin], 2) * used
    from_im = np.concatenate([sin, cos], 2) * used
    return from_re.reshape(-1, 2 * NG), from_im.reshape(-1, 2 * NG)


def z_tables():
    local = np.arange(16)
    points = (np.arange(N_FFT)[:, None] * ZL + local[None, :]).reshape(-1)
    used = np.tile(local < ZL + 3, N_FFT)[:, None]
    scale = 1.0 / (NG * math.sqrt(NG))
    cos, sin = wave(points, np.arange(NG))
    return cos * used * scale, sin * used * scale


def perm_y():
    table = np.zeros((2, KX, 16, 384), np.float32)
    for c in range(2):
        for k in range(KX):
            for z in range(ZE):
                table[c, k, z, z * 24 + c * KX + k] = 1.0
    return table.reshape(384, 384).astype(jnp.bfloat16)


def perm_z():
    table = np.zeros((384, PAIRS), np.float32)
    for c in range(2):
        for k in range(KY):
            for x in range(KX):
                column = c * 96 + k * 8 + x if x < 8 else 192 + c * 48 + k * 4 + x - 8
                table[x * 24 + c * KY + k, column] = 1.0
    return table.astype(jnp.bfloat16)


def step_table(count):
    freqs = (np.arange(count) * 12)[:, None] + np.arange(12)[None, :]
    angle = 2.0 * np.pi * freqs[:, :, None] * np.arange(4)[None, None, :] / NG
    return np.concatenate([np.cos(angle), -np.sin(angle)], 2).astype(np.float32)


def my_place():
    return lax.axis_index("fft"), lax.axis_index("slab")


def split(value):
    high = value.astype(BF16)
    return high, (value - high.astype(F32)).astype(BF16)


def dot_nn(a, b):
    return lax.dot_general(a, b, (((1,), (0,)), ((), ())), preferred_element_type=F32)


def dot_nt(a, b):
    return lax.dot_general(a, b, (((1,), (1,)), ((), ())), preferred_element_type=F32)


def dot_tn(a, b):
    return lax.dot_general(a, b, (((0,), (0,)), ((), ())), preferred_element_type=F32)


def three(dot, a, b):
    return dot(a[0], b[0]) + dot(a[0], b[1]) + dot(a[1], b[0])


def spline(u):
    squared = u * u
    cubed = squared * u
    rest = 1.0 - u
    return (
        rest * rest * rest / 6.0,
        (3.0 * cubed - 6.0 * squared + 4.0) / 6.0,
        (-3.0 * cubed + 3.0 * squared + 3.0 * u + 1.0) / 6.0,
        cubed / 6.0,
    )


def placed(rows, cell, weights):
    off = lax.broadcasted_iota(jnp.int32, (rows, cell.shape[1]), 0) - cell
    value = jnp.where(off == 3, weights[3], 0.0)
    value = jnp.where(off == 2, weights[2], value)
    value = jnp.where(off == 1, weights[1], value)
    return jnp.where(off == 0, weights[0], value)


def spread_body(charge, frac, cell, waves_from, out, acc, waves, sem):
    step = pl.program_id(0)
    copy = pltpu.make_async_copy(waves_from, waves, sem)

    @pl.when(step == 0)
    def _():
        copy.start()
        acc[...] = jnp.zeros_like(acc)

    along_x = placed(XE, cell[0:1, :], spline(frac[0:1, :]))
    along_y = placed(YE, cell[1:2, :], spline(frac[1:2, :])) * charge[...]
    along_z = placed(16, cell[2:3, :], spline(frac[2:3, :]))
    plane = jnp.concatenate([along_z[z : z + 1, :] * along_y for z in range(ZE)], 0)
    acc[...] += three(dot_nt, split(along_x), split(plane))

    @pl.when(step == pl.num_programs(0) - 1)
    def _():
        copy.wait()
        freq = three(dot_tn, split(acc[...]), (waves[0], waves[1]))
        for s in range(N_SLAB):
            for z in range(ZE):
                out[s, :, z * 24 : z * 24 + 24] = freq[z * YE : z * YE + YE, s * 24 : s * 24 + 24]
            out[s, :, ZE * 24 : 384] = jnp.zeros((YE, 384 - ZE * 24), F32)


def spread(charge, frac, cell, waves):
    return pl.pallas_call(
        spread_body,
        grid=(SITES // CHUNK,),
        in_specs=[
            pl.BlockSpec((1, CHUNK), lambda i: (0, i)),
            pl.BlockSpec((3, CHUNK), lambda i: (0, i)),
            pl.BlockSpec((3, CHUNK), lambda i: (0, i)),
            pl.BlockSpec(memory_space=pltpu.HBM),
        ],
        out_specs=pl.BlockSpec((N_SLAB, YE, 384), lambda i: (0, 0, 0)),
        out_shape=jax.ShapeDtypeStruct((N_SLAB, YE, 384), F32),
        scratch_shapes=[
            pltpu.VMEM((XE, ZE * YE), F32),
            pltpu.VMEM((2, XE, 384), BF16),
            pltpu.SemaphoreType.DMA,
        ],
        compiler_params=pltpu.CompilerParams(vmem_limit_bytes=MOST),
        cost_estimate=pl.CostEstimate(flops=8_000_000_000, bytes_accessed=2_000_000, transcendentals=0),
        name="spread",
    )(charge.reshape(1, SITES), frac, cell, waves)


def lanes(tiles):
    return jnp.concatenate([tiles[i : i + 1] for i in range(tiles.shape[0])], 1)


def pack_body(drive, atom, cell, frac, hard, pos, width, out, near, picked):
    f, s = my_place()
    out[...] = jnp.zeros_like(out)
    for i in range(N_SLAB):
        out[i, 0:1, 0:OWN] = -drive[...]
        out[i, 1:2, 0:OWN] = atom[...].astype(F32)
        out[i, 2:5, 0:OWN] = cell[...].astype(F32)
        out[i, 5:8, 0:OWN] = frac[...]
    for j in range(N_FFT):
        at = pl.multiple_of(j * ROWS + (s >> 2) * 128, 128)
        picked[j, 0:3, :] = pos[:, pl.ds(at, 128)]
        picked[j, 3:4, :] = width[:, pl.ds(at, 128)]
    lane = lax.broadcasted_iota(jnp.int32, (8, 128), 1) >> 5
    for tile in range(COLS // 128):
        value = jnp.zeros((8, 128), F32)
        for j in range(4):
            value = jnp.where(lane == j, pltpu.roll(picked[tile * 4 + j], ((j - (s & 3)) & 3) * OWN, 1), value)
        near[:, tile * 128 : tile * 128 + 128] = value
    at = pl.multiple_of(f * ROWS, 128)
    near[:, COLS:] = jnp.zeros((8, ROWS), F32)
    near[0:3, COLS:] = pos[:, pl.ds(at, ROWS)]
    near[3:4, COLS:] = width[:, pl.ds(at, ROWS)]
    near[4:5, COLS : COLS + OWN] = hard[...]


def pack(drive, atom, cell, frac, hard, pos, width):
    return pl.pallas_call(
        pack_body,
        out_shape=(
            jax.ShapeDtypeStruct((N_SLAB, 8, 128), F32),
            jax.ShapeDtypeStruct((8, COLS + ROWS), F32),
        ),
        scratch_shapes=[pltpu.VMEM((N_FFT, 8, 128), F32)],
        compiler_params=pltpu.CompilerParams(vmem_limit_bytes=MOST),
        name="pack",
    )(
        drive.reshape(1, OWN),
        atom.reshape(1, OWN),
        cell,
        frac,
        hard.reshape(1, OWN),
        pos,
        width.reshape(1, ATOMS),
    )


def erf_ratio(value):
    square = value * value
    p = 0.00022905065861350646
    for c in (0.0034082910107109506, 0.050955695062380861, 0.18520832239976145, 1.128379143519084):
        p = p * square + c
    q = -1.1791602954361697e-7
    for c in (
        0.000023547966471313185,
        0.0010179625278914885,
        0.014070470171167667,
        0.11098505178285362,
        0.49746925110067538,
        1.0,
    ):
        q = q * square + c
    return value * p, q


def couple_body(near, out, own):
    f, s = my_place()
    cols = near[:, :COLS]
    side = jnp.transpose(near[:, COLS:])
    own[...] = jnp.zeros_like(own)
    own[0:1, 0:OWN] = near[4:5, COLS : COLS + OWN]
    own_hard = pltpu.roll(own[...], (f & 3) * OWN, 1)[0:1]
    diag = jnp.concatenate([jnp.where((f >> 2) == t, own_hard, 0.0) for t in range(COLS // 128)], 1)
    diag = diag + KE * (1.0 / (cols[3:4] * SQPI) - 2.0 * ALPHA / SQPI)
    col_id = lax.broadcasted_iota(jnp.int32, (1, COLS), 1) - f * OWN
    col_id = jnp.where((col_id >= 0) & (col_id < OWN), col_id + s * OWN, -1)
    col_sq = 2.0 * cols[3:4] * cols[3:4]
    step = 16
    for first in range(0, ROWS, step):
        here = side[first : first + step]
        square = SOFT
        for i in range(3):
            gap = here[:, i : i + 1] - cols[i : i + 1]
            square = square + gap * gap
        inverse = lax.rsqrt(square)
        distance = square * inverse
        narrow = lax.rsqrt(2.0 * here[:, 3:4] * here[:, 3:4] + col_sq)
        p1, q1 = erf_ratio(jnp.minimum(distance * narrow, 3.832506856900711))
        p2, q2 = erf_ratio(jnp.minimum(distance * ALPHA, 3.832506856900711))
        value = KE * inverse * ((p1 * q2 - p2 * q1) / (q1 * q2))
        row_id = first + lax.broadcasted_iota(jnp.int32, (step, 1), 0)
        out[first : first + step] = jnp.where(row_id == col_id, diag, value)


def couple(near):
    return pl.pallas_call(
        couple_body,
        out_shape=jax.ShapeDtypeStruct((ROWS, COLS), F32),
        scratch_shapes=[pltpu.VMEM((8, 128), F32)],
        compiler_params=pltpu.CompilerParams(vmem_limit_bytes=SOME),
        cost_estimate=pl.CostEstimate(flops=100_000_000, bytes_accessed=2_000_000, transcendentals=1_000_000),
        name="couple",
    )(near)


def first_body(got, matrix, out, slots):
    for s in range(N_SLAB):
        slots[:, s * OWN : s * OWN + OWN] = got[s, :, 0:OWN]
    every = slots[...]
    part = jnp.sum(matrix[...] * jnp.transpose(every)[:, 0:1], 0, keepdims=True)
    for i in range(8):
        out[0, i : i + 1, :] = part[:, i * 128 : i * 128 + 128]
    for i in range(4):
        out[0, 8 + i * 8 : 16 + i * 8, :] = every[:, i * 128 : i * 128 + 128]
    whole = out[0]
    for f in range(1, N_FFT):
        out[f] = whole


def first_product(got, matrix):
    return pl.pallas_call(
        first_body,
        out_shape=jax.ShapeDtypeStruct((N_FFT, 40, 128), F32),
        scratch_shapes=[pltpu.VMEM((8, ROWS), F32)],
        compiler_params=pltpu.CompilerParams(vmem_limit_bytes=SOME),
        name="first_product",
    )(got, matrix)


def y_body(grid, matrix, perm, arh, arl, aih, ail, out, side):
    got = grid[...]
    rows = jnp.sum(got[:, YE - 4 :, 0:128], 0)
    side[0:4, :] = rows
    turned = jnp.transpose(side[...])
    column = jnp.concatenate([turned[:, i : i + 1] for i in range(4)], 0)
    part = jnp.sum(matrix[...] * column, 0, keepdims=True)
    high, low = split(got.reshape(N_SLAB * YE, 384))
    high = dot_nt(perm[...], high).astype(BF16)
    low = dot_nt(perm[...], low).astype(BF16)
    freq = three(dot_nn, (high[:192], low[:192]), (arh[...], arl[...]))
    freq = freq + three(dot_nn, (high[192:], low[192:]), (aih[...], ail[...]))
    for i in range(16):
        out[0, i : i + 1, 288:320] = part[:, i * OWN : i * OWN + OWN]
        out[0, i : i + 1, 320:352] = part[:, ROWS + i * OWN : ROWS + i * OWN + OWN]
        out[0, i : i + 1, 352:384] = rows[i // 4 : i // 4 + 1, i % 4 * OWN : i % 4 * OWN + OWN]
    extra = out[0, :, 256:384]
    for f in range(N_FFT):
        if f > 0:
            out[f, :, 256:384] = extra
        for k in range(KX):
            out[f, :, k * 24 : k * 24 + 24] = freq[k * 16 : k * 16 + 16, f * 24 : f * 24 + 24]


def along_y(*operands):
    return pl.pallas_call(
        y_body,
        out_shape=jax.ShapeDtypeStruct((N_FFT, 16, 384), F32),
        scratch_shapes=[pltpu.VMEM((8, 128), F32)],
        compiler_params=pltpu.CompilerParams(vmem_limit_bytes=2 * SOME),
        cost_estimate=pl.CostEstimate(flops=4_000_000_000, bytes_accessed=5_000_000, transcendentals=0),
        name="along_y",
    )(*operands)


def quad_body(got, out):
    s = my_place()[1]
    third = jnp.sum(got[:, :, 32:96], 0)
    second = got[:, pl.ds(s, 1), 96:128].reshape(N_FFT, OWN)
    total = jnp.sum(third[:, 0:OWN] * second[0:16] + third[:, OWN:] * second[16:], 0, keepdims=True)
    total = jnp.sum(total, 1, keepdims=True)
    out[...] = jnp.broadcast_to(total[None], out.shape)


def quad_sum(got):
    return pl.pallas_call(
        quad_body,
        grid=(1,),
        in_specs=[
            pl.BlockSpec((N_FFT, 16, 128), lambda i: (0, 0, 2)),
        ],
        out_specs=pl.BlockSpec((N_SLAB, 8, 128), lambda i: (0, 0, 0)),
        out_shape=jax.ShapeDtypeStruct((N_SLAB, 8, 128), F32),
        compiler_params=pltpu.CompilerParams(vmem_limit_bytes=SOME),
        name="quad_sum",
    )(got)


def unit(turns):
    half = (turns - 0.5) * math.pi
    square = half * half
    sine = 0.0
    for power in (11, 9, 7, 5, 3):
        sine = (sine + (-1.0) ** (power // 2) / math.factorial(power)) * square
    sine = half * (1.0 + sine)
    cosine = 0.0
    for power in (12, 10, 8, 6, 4, 2):
        cosine = (cosine + (-1.0) ** (power // 2) / math.factorial(power)) * square
    cosine = 1.0 + cosine
    return 2.0 * sine * sine - 1.0, 2.0 * sine * cosine


def site_waves(freq, base, fraction, steps):
    upper = lax.broadcasted_iota(jnp.int32, (8, 1), 0) < 4

    def in_rows(x, y):
        wide = [jnp.broadcast_to(v, (8, ROWS)) for v in (x, y)]
        return jnp.concatenate(wide + [jnp.where(upper, x, y)], 0)

    phase = freq * in_rows(*base)
    phase = phase - NG * jnp.floor(phase * (1.0 / NG))
    re, im = unit(phase * (1.0 / NG))
    weights = [in_rows(x, y) for x, y in zip(spline(fraction[0]), spline(fraction[1]), strict=True)]
    w_re = sum(steps[:, i : i + 1] * weights[i] for i in range(4))
    w_im = sum(steps[:, 4 + i : 5 + i] * weights[i] for i in range(1, 4))
    return re * w_re - im * w_im, re * w_im + im * w_re


def slot_rows(slots, g):
    return jnp.concatenate([slots[g, 8 + i * 8 : 16 + i * 8, :] for i in range(4)], 1)


def guarded(value, pivot, scale):
    good = jnp.abs(pivot) > 1e-6 * jnp.abs(scale)
    return jnp.where(good, value / jnp.where(good, pivot, 1.0), 0.0)


def lookup(tables, atom):
    index = lax.broadcasted_iota(jnp.int32, (128, atom.shape[1]), 0)
    pick = jnp.where(index == (atom & 127), 1.0, 0.0).astype(BF16)
    rows = dot_nn(tables, jnp.concatenate([pick, pick], 0))
    here = index == (atom >> 7)
    count = rows.shape[0] // 128
    return [
        jnp.sum(jnp.where(here, rows[v * 128 : v * 128 + 128], 0.0), 0, keepdims=True) for v in range(count)
    ]


def early_body(slots, first, out, v0):
    for i in range(4):
        v0[pl.ds(i, N_FFT, stride=4), :] = slots[:, 8 + i * 8, :]
    both = jnp.concatenate([v0[...], first[...]], 0)
    high, low = split(both)
    both = jnp.concatenate([high, low], 1)
    for g in range(N_FFT):
        found = lookup(both, slot_rows(slots, g)[1:2].astype(jnp.int32))
        for v in range(2):
            for i in range(4):
                out[v, g * 4 + i : g * 4 + i + 1, :] = found[v][:, i * 128 : i * 128 + 128]


def early(slots, first):
    return pl.pallas_call(
        early_body,
        out_shape=jax.ShapeDtypeStruct((2, 128, 128), F32),
        scratch_shapes=[pltpu.VMEM((128, 128), F32)],
        compiler_params=pltpu.CompilerParams(vmem_limit_bytes=SOME),
        cost_estimate=pl.CostEstimate(flops=2_000_000_000, bytes_accessed=1_000_000, transcendentals=0),
        name="early",
    )(slots, first)


def ml_group(i, slots, charges, grid, perm, steps, store):
    f, s = my_place()
    upper = lax.broadcasted_iota(jnp.int32, (8, 1), 0) < 4
    block = (lax.broadcasted_iota(jnp.int32, (1, ROWS), 1) // OWN * YL).astype(F32)
    local = lax.broadcasted_iota(jnp.int32, (24, 1), 0)
    freq = jnp.where(local < 8, s * KX + local, f * KY + local - 8)
    freq = jnp.where(local < 16, freq, jnp.where(local < 20, s * KX + local - 8, f * KY + local - 12)).astype(F32)
    at = pl.multiple_of(i * 32, 32)
    charge = [charges[v, pl.ds(at, 32), :] for v in range(2)]
    high, low = split(grid[pl.ds(i * 8, 8)].reshape(128, 384))
    base = (dot_nn(high, perm[...]) + dot_nn(low, perm[...])).reshape(8, 16, PAIRS)
    for j in range(8):
        g = i * 8 + j
        rows = slot_rows(slots, g)
        placed_z = placed(16, rows[4:5].astype(jnp.int32), spline(rows[7:8]))
        both = [placed_z * lanes(charge[v][j * 4 : j * 4 + 4]) for v in range(2)]
        z_high, z_low = split(jnp.concatenate(both, 0))
        re, im = site_waves(freq, (rows[2:3], rows[3:4] + block), (rows[5:6], rows[6:7]), steps[...])
        x_re, x_im = re[0:8], im[0:8]
        y_re = [re[8 + k : 9 + k] for k in range(8)] + [re[20 + k : 21 + k] for k in range(4)]
        y_im = [im[8 + k : 9 + k] for k in range(8)] + [im[20 + k : 21 + k] for k in range(4)]
        parts_re, parts_im = [], []
        for k in range(KY):
            a, b = y_re[k], y_im[k]
            parts_re.append(a * x_re - b * x_im)
            parts_im.append(a * x_im + b * x_re)
        parts = parts_re + parts_im
        x_re, x_im = (jnp.where(upper, v[16:24], pltpu.roll(v[16:24], 4, 0)) for v in (re, im))
        parts_re, parts_im = [], []
        for k in range(0, KY, 2):
            a = jnp.where(upper, y_re[k], y_re[k + 1])
            b = jnp.where(upper, y_im[k], y_im[k + 1])
            parts_re.append(a * x_re - b * x_im)
            parts_im.append(a * x_im + b * x_re)
        high, low = split(jnp.concatenate(parts + parts_re + parts_im, 0))
        total = dot_nt(jnp.concatenate([z_high, z_low], 0), high)
        total = total[:32] + total[32:] + dot_nt(z_high, low)
        store(g, total[:16] + base[j], total[16:])


def solve_body(slots, before, first, grid, perm, steps, out, rest, charges, v2, late):
    f, s = my_place()
    for i in range(4):
        pieces = [grid[:, i * 4 + j, 352:384] for j in range(4)]
        v2[pl.ds(i, N_FFT, stride=4), :] = jnp.concatenate(pieces, 1)
    high, low = split(v2[...])
    both = jnp.concatenate([high, low], 1)
    for g in range(N_FFT):
        found = lookup(both, slot_rows(slots, g)[1:2].astype(jnp.int32))[0]
        for i in range(4):
            late[g * 4 + i : g * 4 + i + 1, :] = found[:, i * 128 : i * 128 + 128]

    def dot(a, b):
        return jnp.sum(jnp.sum(a * b, 0, keepdims=True), 1, keepdims=True)

    a, b, c = before[0], before[1], late[...]
    m0, m1, m2, m3, m4 = dot(a, a), dot(a, b), dot(b, b), dot(b, c), dot(c, c)
    l10 = m2 / m1
    l20 = m3 / m1
    d1 = m3 - l10 * m2
    e12 = m4 - l10 * m3
    l21 = guarded(e12, d1, m3)
    g1 = m1 - l10 * m0
    g2 = (m2 - l20 * m0) - l21 * g1
    c1 = guarded(g1, d1, m3)
    c0 = m0 / m1 - l10 * c1
    charges[0] = c0 * a + c1 * b
    charges[1] = c - l21 * b + (l10 * l21 - l20) * a
    at = f * 4 + (s >> 2)
    rest[...] = jnp.zeros_like(rest)
    own = [slots[pl.ds(f, 1), 8 + i * 8, :] for i in range(4)]
    a = sum(jnp.where((s >> 2) == i, own[i], 0.0) for i in range(4))
    b, c = first[pl.ds(at, 1), :], v2[pl.ds(at, 1), :]
    rest[0:1] = c0 * a + c1 * b
    rest[1:2] = c - l21 * b + (l10 * l21 - l20) * a
    rest[...] = pltpu.roll(rest[...], ((4 - (s & 3)) & 3) * OWN, 1)
    rest[2:3] = jnp.broadcast_to(l20 * m3 + l21 * e12, (1, 128))
    rest[3:4] = jnp.broadcast_to(g2, (1, 128))

    def store(g, base, last):
        out[g, 0:16] = base
        out[g, 16:32] = last

    def group(i, carry):
        ml_group(i, slots, charges, grid, perm, steps, store)
        return carry

    lax.fori_loop(0, 2, group, 0)


def solve(*operands):
    return pl.pallas_call(
        solve_body,
        out_shape=(
            jax.ShapeDtypeStruct((N_FFT // 2, 32, PAIRS), F32),
            jax.ShapeDtypeStruct((8, 128), F32),
            jax.ShapeDtypeStruct((2, 128, 128), F32),
        ),
        scratch_shapes=[pltpu.VMEM((128, 128), F32), pltpu.VMEM((128, 128), F32)],
        compiler_params=pltpu.CompilerParams(vmem_limit_bytes=SOME),
        cost_estimate=pl.CostEstimate(flops=5_000_000_000, bytes_accessed=4_000_000, transcendentals=0),
        name="solve",
    )(*operands)


def last_step(quads, rest):
    m5 = jnp.sum(quads[:, 0, :], 0, keepdims=True)
    return guarded(rest[3:4], m5 - rest[2:3], m5)[:, 0:1]


def join_body(slots, charges, grid, perm, steps, early_half, quads, rest, out, out_q):
    step = last_step(quads, rest)
    half = N_FFT // 2
    out[0:half] = early_half[:, 0:16] + step[None] * early_half[:, 16:32]
    out_q[...] = (rest[0:1] + step * rest[1:2])[:, 0:OWN]

    def store(g, base, last):
        out[g] = base + step * last

    def group(i, carry):
        ml_group(i, slots, charges, grid, perm, steps, store)
        return carry

    lax.fori_loop(2, 4, group, 0)


def join(*operands):
    return pl.pallas_call(
        join_body,
        out_shape=(
            jax.ShapeDtypeStruct((N_FFT, 16, PAIRS), F32),
            jax.ShapeDtypeStruct((1, OWN), F32),
        ),
        compiler_params=pltpu.CompilerParams(vmem_limit_bytes=SOME),
        cost_estimate=pl.CostEstimate(flops=4_000_000_000, bytes_accessed=4_000_000, transcendentals=0),
        name="join",
    )(*operands)


def z_body(grid, waves, out_re, out_im):
    both = split(grid[...].reshape(N_FFT * 16, PAIRS))
    cos = three(dot_tn, both, (waves[0], waves[1]))
    sin = three(dot_tn, both, (waves[2], waves[3]))
    for k in range(KY):
        for first, count, re in ((0, 8, k * 8), (8, 4, 192 + k * 4)):
            im = re + KY * count
            out_re[k, first : first + count] = cos[re : re + count] + sin[im : im + count]
            out_im[k, first : first + count] = cos[im : im + count] - sin[re : re + count]


def along_z(*operands):
    shape = jax.ShapeDtypeStruct((KY, KX, NG), F32)
    return pl.pallas_call(
        z_body,
        out_shape=(shape, shape),
        compiler_params=pltpu.CompilerParams(vmem_limit_bytes=SOME),
        cost_estimate=pl.CostEstimate(flops=3_000_000_000, bytes_accessed=5_000_000, transcendentals=0),
        name="along_z",
    )(*operands)


def swap(value, axis):
    return lax.all_to_all(value, axis, 0, 0, tiled=True)


def on_device(
    ml_pos,
    ml_width,
    ml_drive,
    ml_hard,
    mm_charge,
    mm_frac,
    mm_cell,
    slot_atom,
    slot_frac,
    slot_cell,
):
    f = lax.axis_index("fft")
    s = lax.axis_index("slab")

    sent, near = pack(ml_drive, slot_atom, slot_cell, slot_frac, ml_hard, ml_pos, ml_width)
    got = swap(sent, "slab")
    matrix = couple(near)
    got_1 = swap(first_product(got, matrix), "fft")
    mm = spread(mm_charge, mm_frac, mm_cell, jnp.asarray(np.stack(two_parts(x_table()))))
    first_cols = jnp.sum(got_1[:, :8], 0)
    part = jnp.sum(matrix * first_cols.reshape(1, COLS), 1)
    tail = jnp.concatenate([part.reshape(4, 128), first_cols[:4], first_cols[4:]], 1)
    tail = jnp.broadcast_to(tail[None], (N_SLAB, 4, 384))
    got_2 = swap(jnp.concatenate([mm[:, : YE - 4], tail], 1), "slab")
    first_full = jnp.concatenate([got_2[:, YE - 4 :, 128:256], got_2[:, YE - 4 :, 256:]], 1)
    first_full = jnp.transpose(first_full.reshape(N_SLAB, N_FFT, OWN), (1, 0, 2)).reshape(128, 128)

    arh, arl, aih, ail = (jnp.asarray(t) for half in y_tables() for t in two_parts(half))
    got_3 = swap(along_y(got_2, matrix, jnp.asarray(perm_y()), arh, arl, aih, ail), "fft")
    quads = swap(quad_sum(got_3), "slab")

    steps_x = lax.dynamic_index_in_dim(jnp.asarray(step_table(N_SLAB)), s, 0, False)
    steps_y = lax.dynamic_index_in_dim(jnp.asarray(step_table(N_FFT)), f, 0, False)
    steps = jnp.concatenate([steps_x[:8], steps_y[:8], steps_x[8:], steps_y[8:]], 0)
    before = early(got_1, first_full)
    perm = jnp.asarray(perm_z())
    half, rest, charges = solve(got_1, before, first_full, got_3, perm, steps)
    total, charge = join(got_1, charges, got_3, perm, steps, half, quads, rest)
    z_waves = jnp.asarray(np.stack([t for part in z_tables() for t in two_parts(part)]))
    struct_re, struct_im = along_z(total, z_waves)
    return (charge.reshape(OWN), struct_re, struct_im)


def solution(mesh):
    return jax.shard_map(
        on_device,
        mesh=mesh,
        in_specs=(
            P(),
            P(),
            P(("fft", "slab")),
            P(("fft", "slab")),
            P(("fft", "slab")),
            P(None, ("fft", "slab")),
            P(None, ("fft", "slab")),
            P(("fft", "slab")),
            P(None, ("fft", "slab")),
            P(None, ("fft", "slab")),
        ),
        out_specs=(P(("fft", "slab")), P("fft", "slab", None), P("fft", "slab", None)),
        check_vma=False,
    )
```
